32 devices in a mesh: scene: 2 (over x), row: 8 (over z, y), col: 2 (over core).
Axes of the slice: x: 2, y: 2, z: 4, core: 2. Of those that a mesh axis runs over, the one named last changes fastest.
Arguments:
- camera_probe_field: bfloat16 [256, 64, 1024], P(('scene', 'row'), 'col'), parts along dimension 0, may hold values from -135 to 135
- echo_lookup_field: bfloat16 [256, 64, 1024], P(('scene', 'row'), 'col'), parts along dimension 0, may hold values from -135 to 135
- echo_content_field: bfloat16 [256, 64, 1024], P(('scene', 'row'), 'col'), parts along dimension 0, may hold values from -135 to 135
- upstream_sensitivity: bfloat16 [256, 64, 1024], P(('scene', 'row'), 'col'), parts along dimension 0, may hold values from -6 to 6
- sharpness_factor: float32 [16], replicated, may hold values from 1 to 6
- final_projector: bfloat16 [1024, 1024], replicated, may hold values from -0.1875 to 0.1875
- neighborhood_filter: float32 [9, 1024], replicated, may hold values from -2 to 2
Outputs:
- merged_result: bfloat16 [256, 64, 1024], P(('scene', 'row'), 'col'), parts along dimension 0
- probe_sensitivity: bfloat16 [256, 64, 1024], P(('scene', 'row'), 'col'), parts along dimension 0
- lookup_sensitivity: bfloat16 [256, 64, 1024], P(('scene', 'row'), 'col'), parts along dimension 0
- content_sensitivity: bfloat16 [256, 64, 1024], P(('scene', 'row'), 'col'), parts along dimension 0
- sharpness_sensitivity: float32 [32], P('scene'), parts along dimension 0
- neighborhood_sensitivity: float32 [18, 1024], P('scene'), parts along dimension 0
- projector_sensitivity: float32 [2048, 1024], P(('scene', 'row', 'col')), parts along dimension 0
The draws below stay inside these ranges and needn't reach their ends.
There are 2 independent parts, one for each index of `scene`. The reference program is written for one: setup_inputs(seed, part) draws one part's arguments, and reference() takes and returns one part's arrays. A program takes and returns all parts, laid end to end along the dimension named above; an argument that names none is the same for every part. Nothing has to cross between parts.
All inputs are finite; a program needn't handle non-finite values.
Results may differ from the reference program's by a relative error of at most 0.0095.
Values may be sent and summed in bfloat16 or wider, within the bound.
No kernel may reach another device: no remote copies, remote signals or barrier semaphores. Data moves between devices by JAX's collectives and lax.ppermute only.
A program may use at most 128 MiB of HBM per device.

```python
import math
import jax
import jax.numpy as jnp
from jax import lax

NUM_ATTN_GROUPS = 16
C = 1024
NR = 128
NC = 64


def rough_field(key):
    return jax.random.truncated_normal(key, -4.0, 4.0, (NR, NC, C), jnp.float32)


def token_amplitude(key):
    rise = 1.0 + 2.0 * jnp.arange(NR).astype(jnp.float32) / (NR - 1)
    spread = jnp.power(10.0, jax.random.uniform(key, (NR, NC, 1), jnp.float32))
    return rise[:, None, None] * spread * 0.25


def channel_amplitude(key):
    return jnp.power(10.0, jax.random.uniform(key, (C,), jnp.float32, -0.5, 0.5))


def shared_scene(key):
    base = rough_field(jax.random.fold_in(key, 7))
    return (base, token_amplitude(jax.random.fold_in(key, 8)))


def draw_camera_probe_field(key, part):
    base, amplitude = shared_scene(key)
    noise = rough_field(jax.random.fold_in(key, 1))
    channel = channel_amplitude(jax.random.fold_in(key, 3))
    return (amplitude * channel * (0.8 * base + 0.6 * noise)).astype(jnp.bfloat16)


def draw_echo_lookup_field(key, part):
    base, amplitude = shared_scene(key)
    noise = rough_field(jax.random.fold_in(key, 2))
    channel = channel_amplitude(jax.random.fold_in(key, 4))
    return (amplitude * channel * (0.8 * base + 0.6 * noise)).astype(jnp.bfloat16)


def draw_echo_content_field(key, part):
    noise = rough_field(jax.random.fold_in(key, 5))
    amplitude = token_amplitude(jax.random.fold_in(key, 6))
    channel = channel_amplitude(jax.random.fold_in(key, 9))
    return (amplitude * channel * noise).astype(jnp.bfloat16)


def level_of(own_key, shape, cuts, smallest, largest):
    loudness = 1.0
    for position, parts in cuts:
        heights = jax.random.uniform(jax.random.fold_in(jax.random.fold_in(own_key, 6), position), (parts,), jnp.float32, smallest / len(cuts), largest / len(cuts))
        loudness = loudness * jnp.repeat(jnp.exp(heights), shape[position] // parts).reshape((-1,) + (1,) * (len(shape) - 1 - position))
    return loudness


def centred(rng, shape, deviation, most, pieces=(), dtype=jnp.bfloat16):
    result = deviation * jax.random.normal(rng, shape, jnp.float32)
    if pieces:
        result = result * level_of(rng, shape, pieces, -0.22, 0.18)
    return jnp.clip(result, -most, most).astype(dtype)


def setup_inputs(seed: int = 0, part: int = 0) -> dict:
    keys = jax.random.split(jax.random.key(seed), 8)
    part_splits = jax.random.split(jax.random.fold_in(keys[7], part), 8)
    return {
        "camera_probe_field": draw_camera_probe_field(jax.random.fold_in(jax.random.fold_in(keys[7], part), 71), part),
        "echo_lookup_field": draw_echo_lookup_field(jax.random.fold_in(jax.random.fold_in(keys[7], part), 71), part),
        "echo_content_field": draw_echo_content_field(jax.random.fold_in(jax.random.fold_in(keys[7], part), 71), part),
        "upstream_sensitivity": centred(part_splits[3], (NR, NC, C), 1.0, 6.0, ((0, 8), (1, 2))),
        "sharpness_factor": jnp.clip(jnp.exp(jax.random.uniform(keys[4], (NUM_ATTN_GROUPS,), jnp.float32, math.log(1.0), math.log(6.0))), 1.0, 6.0),
        "final_projector": centred(keys[5], (C, C), C ** -0.5, 0.1875),
        "neighborhood_filter": centred(keys[6], (9, C), 9 ** -0.5, 2.0, (), jnp.float32),
    }


epsilon = 1e-06
inverse_root = 0.7071067811865476
density_root = 0.3989422804014327

def gelu_pair(field):
    cumul = 0.5 * (1.0 + lax.erf(field * inverse_root))
    return (field * cumul, cumul + field * jnp.exp(-0.5 * field * field) * density_root)

def stencil_apply(padded, neighborhood_filter):
    tile_rows = padded.shape[0] - 2
    tile_cols = padded.shape[1] - 2
    total = jnp.zeros((tile_rows, tile_cols, padded.shape[2]), jnp.float32)
    for shift_row in range(3):
        for shift_col in range(3):
            total = total + neighborhood_filter[3 * shift_row + shift_col] * padded[shift_row:shift_row + tile_rows, shift_col:shift_col + tile_cols]
    return total

def stencil_back(padded_slope, neighborhood_filter):
    tile_rows = padded_slope.shape[0] - 2
    tile_cols = padded_slope.shape[1] - 2
    total = jnp.zeros((tile_rows, tile_cols, padded_slope.shape[2]), jnp.float32)
    for shift_row in range(3):
        for shift_col in range(3):
            total = total + neighborhood_filter[3 * shift_row + shift_col] * padded_slope[2 - shift_row:2 - shift_row + tile_rows, 2 - shift_col:2 - shift_col + tile_cols]
    return total

def stencil_weights(slope_mid, padded_field):
    tile_rows = slope_mid.shape[0]
    tile_cols = slope_mid.shape[1]
    taps = []
    for shift_row in range(3):
        for shift_col in range(3):
            window = padded_field[shift_row:shift_row + tile_rows, shift_col:shift_col + tile_cols]
            taps.append(lax.optimization_barrier(jnp.sum(slope_mid.astype(jnp.float32) * window.astype(jnp.float32), axis=(0, 1))))
    return jnp.stack(taps, axis=0)

def reference(camera_probe_field, echo_lookup_field, echo_content_field, upstream_sensitivity, sharpness_factor, final_projector, neighborhood_filter):
    scene_rows, scene_cols, width = camera_probe_field.shape
    per_group_layout = sharpness_factor.shape[0]
    head_size = width // per_group_layout
    query_flat = camera_probe_field.reshape(-1, per_group_layout, head_size).astype(jnp.float32)
    key_flat = echo_lookup_field.reshape(-1, per_group_layout, head_size).astype(jnp.float32)
    value_flat = echo_content_field.reshape(-1, per_group_layout, head_size).astype(jnp.float32)
    query_energy = lax.optimization_barrier(jnp.sum(query_flat * query_flat, axis=0))
    key_energy = lax.optimization_barrier(jnp.sum(key_flat * key_flat, axis=0))
    raw_gram = jnp.einsum('nhi,nhj->hij', query_flat, key_flat)
    query_scale = lax.rsqrt(query_energy + epsilon)
    key_scale = lax.rsqrt(key_energy + epsilon)
    channel_similarity = query_scale[:, :, None] * raw_gram * key_scale[:, None, :]
    softmax_numerators = jnp.exp(sharpness_factor[:, None, None] * channel_similarity)
    attention = softmax_numerators / lax.optimization_barrier(jnp.sum(softmax_numerators, axis=2, keepdims=True))
    attention_low = attention.astype(jnp.bfloat16)
    mixed_low = jnp.einsum('nhj,hij->nhi', value_flat, attention_low.astype(jnp.float32)).astype(jnp.bfloat16).reshape(-1, width)
    projected = jnp.dot(mixed_low, final_projector, preferred_element_type=jnp.float32).reshape(scene_rows, scene_cols, width)
    projected_low = projected.astype(jnp.bfloat16)
    padded_field = jnp.pad(projected_low, ((1, 1), (1, 1), (0, 0)))
    stencil_sum = stencil_apply(padded_field, neighborhood_filter)
    activated, slope = gelu_pair(stencil_sum)
    merged_result = (projected + activated).astype(jnp.bfloat16)
    slope_low = (upstream_sensitivity.astype(jnp.float32) * slope).astype(jnp.bfloat16)
    neighborhood_sensitivity = stencil_weights(slope_low, padded_field)
    padded_slope = jnp.pad(slope_low, ((1, 1), (1, 1), (0, 0)))
    target_low = (upstream_sensitivity.astype(jnp.float32) + stencil_back(padded_slope, neighborhood_filter)).astype(jnp.bfloat16).reshape(-1, width)
    projector_sensitivity = jnp.dot(mixed_low.T, target_low, preferred_element_type=jnp.float32)
    mixed_grad_low = jnp.dot(target_low, final_projector.T, preferred_element_type=jnp.float32).astype(jnp.bfloat16)
    grad_heads = mixed_grad_low.reshape(-1, per_group_layout, head_size).astype(jnp.float32)
    attention_grad = jnp.einsum('nhi,nhj->hij', grad_heads, value_flat)
    content_sensitivity = jnp.einsum('nhi,hij->nhj', grad_heads, attention_low.astype(jnp.float32)).astype(jnp.bfloat16)
    logit_sensitivity = attention * (attention_grad - lax.optimization_barrier(jnp.sum(attention * attention_grad, axis=2, keepdims=True)))
    sharpness_sensitivity = lax.optimization_barrier(jnp.sum(logit_sensitivity * channel_similarity, axis=(1, 2)))
    similarity_sensitivity = sharpness_factor[:, None, None] * logit_sensitivity
    query_corr = lax.optimization_barrier(jnp.sum(similarity_sensitivity * channel_similarity, axis=2))
    key_corr = lax.optimization_barrier(jnp.sum(similarity_sensitivity * channel_similarity, axis=1))
    mixer_low = (query_scale[:, :, None] * similarity_sensitivity * key_scale[:, None, :]).astype(jnp.bfloat16).astype(jnp.float32)
    probe_sensitivity = jnp.einsum('nhj,hij->nhi', key_flat, mixer_low) - query_flat * (query_scale * query_scale * query_corr)[None]
    lookup_sensitivity = jnp.einsum('nhi,hij->nhj', query_flat, mixer_low) - key_flat * (key_scale * key_scale * key_corr)[None]
    full_dimensions = (scene_rows, scene_cols, width)
    return (merged_result, probe_sensitivity.astype(jnp.bfloat16).reshape(full_dimensions), lookup_sensitivity.astype(jnp.bfloat16).reshape(full_dimensions), content_sensitivity.reshape(full_dimensions), sharpness_sensitivity, neighborhood_sensitivity, projector_sensitivity)
```

```python
import functools

import jax
import jax.numpy as jnp
from jax import lax
from jax.experimental import pallas as pl
from jax.experimental.pallas import tpu as pltpu
from jax.sharding import PartitionSpec as P

epsilon = 1e-06
inverse_root = 0.7071067811865476
density_root = 0.3989422804014327
LANES = 128
GROUP = 256
RIM = 8
f32 = jnp.float32
bf16 = jnp.bfloat16
VMEM_LIMIT = 56 * 1024 * 1024


def whole(shape):
    return pl.BlockSpec(shape, lambda *_: (0,) * len(shape))


SCALAR = pl.BlockSpec(memory_space=pltpu.SMEM)


def params():
    return pltpu.CompilerParams(vmem_limit_bytes=VMEM_LIMIT)


def dot_tn(a, b):
    return lax.dot_general(a, b, (((0,), (0,)), ((), ())), preferred_element_type=f32)


def dot_nt(a, b):
    return lax.dot_general(a, b, (((1,), (1,)), ((), ())), preferred_element_type=f32)


def dot_nn(a, b):
    return jnp.dot(a, b, preferred_element_type=f32)


def lane_head(head_size):
    return lax.broadcasted_iota(jnp.int32, (head_size, LANES), 1) // head_size


def by_head(parts, owner):
    out = parts[0]
    for k in range(1, len(parts)):
        out = jnp.where(owner == k, parts[k], out)
    return out


def pack_diagonal(square, head_size):
    owner = lane_head(head_size)
    return by_head(
        [square[k * head_size : (k + 1) * head_size] for k in range(LANES // head_size)], owner
    )


def sum_in_head(values, owner, packed):
    sums = [jnp.sum(jnp.where(owner == k, values, 0.0), axis=1, keepdims=True) for k in range(packed)]
    return by_head([jnp.broadcast_to(s, values.shape) for s in sums], owner)


def gram_kernel(head_size, col_ref, q_ref, k_ref, mine_ref, other_ref):
    half = pl.program_id(0)
    span = q_ref.shape[1]
    rows = []
    for g in range(span // GROUP):
        at = pl.ds(g * GROUP, GROUP)
        square = dot_tn(q_ref[:, at], k_ref[:, at])
        for p in range(GROUP // LANES):
            cut = slice(p * LANES, (p + 1) * LANES)
            rows.append(pack_diagonal(square[cut, cut], head_size))
    for ref in (q_ref, k_ref):
        for p in range(span // LANES):
            x = ref[:, pl.ds(p * LANES, LANES)].astype(f32)
            rows.append(jnp.sum(x * x, axis=0, keepdims=True))

    def put(ref):
        at = 0
        for row in rows:
            ref[pl.ds(at, row.shape[0]), :] = row
            at += row.shape[0]

    @pl.when(half == col_ref[0])
    def _():
        put(mine_ref)

    @pl.when(half != col_ref[0])
    def _():
        put(other_ref)


def gram_call(col, q, k, head_size):
    tokens, width = q.shape
    span = width // 2
    lines = span // LANES * (head_size + 2)
    out = jax.ShapeDtypeStruct((lines, LANES), f32)
    return pl.pallas_call(
        functools.partial(gram_kernel, head_size),
        grid=(2,),
        in_specs=[
            SCALAR,
            pl.BlockSpec((tokens, span), lambda i: (0, i)),
            pl.BlockSpec((tokens, span), lambda i: (0, i)),
        ],
        out_specs=[whole((lines, LANES))] * 2,
        out_shape=[out, out],
        compiler_params=params(),
        name="gram",
    )(col, q, k)


def gelu_terms(u):
    cumul = 0.5 * (1.0 + lax.erf(u * inverse_root))
    return u * cumul, cumul + u * jnp.exp(-0.5 * u * u) * density_root


def attention_block(head_size, raw, q_line, k_line, sharp):
    packed = LANES // head_size
    owner = lane_head(head_size)
    row = lax.broadcasted_iota(jnp.int32, (head_size, LANES), 0)
    lane = lax.broadcasted_iota(jnp.int32, (head_size, LANES), 1)
    q_energy = by_head(
        [
            jnp.broadcast_to(
                jnp.sum(jnp.where(lane == row + k * head_size, q_line, 0.0), axis=1, keepdims=True),
                raw.shape,
            )
            for k in range(packed)
        ],
        owner,
    )
    q_scale = lax.rsqrt(q_energy + epsilon)
    k_scale = lax.rsqrt(k_line + epsilon)
    gram = q_scale * raw * k_scale
    heat = by_head([jnp.full(raw.shape, s, f32) for s in sharp], owner)
    numer = jnp.exp(heat * gram)
    attention = numer / sum_in_head(numer, owner, packed)
    return attention, gram, q_scale * k_scale


def middle_kernel(
    head_size,
    tile,
    col_ref,
    sharp_ref,
    own_ref,
    far_ref,
    v_ref,
    u_ref,
    side_ref,
    rim_ref,
    proj_ref,
    taps_ref,
    merged_ref,
    attn_ref,
    gram_ref,
    scale_ref,
    block_ref,
    mixed_ref,
    target_ref,
    grad_ref,
    mine_ref,
    other_ref,
    mixed_all,
    field_ref,
    slope_ref,
    projected_ref,
    upside_ref,
    tapsum_ref,
):
    step = pl.program_id(0)
    last = pl.num_programs(0) - 1
    tile_rows, tile_cols = tile
    tokens, width = v_ref.shape
    ring = tile_cols + RIM
    side = tile_rows * RIM
    packed = LANES // head_size
    blocks = width // LANES
    half_blocks = blocks // 2
    is_first = col_ref[0] == 0

    @pl.when(step == 0)
    def _():
        block_ref[...] = jnp.zeros(block_ref.shape, bf16)
        tapsum_ref[...] = jnp.zeros(tapsum_ref.shape, f32)
        owner = lane_head(head_size)
        for p in range(blocks):
            h, inner = divmod(p, half_blocks)

            def take(at, size):
                a = own_ref[pl.ds(at, size), :]
                b = far_ref[pl.ds(at, size), :]
                return jnp.where(is_first, a, b) if h == 0 else jnp.where(is_first, b, a)

            raw = take(inner * head_size, head_size)
            q_line = take(half_blocks * head_size + inner, 1)
            k_line = take(half_blocks * (head_size + 1) + inner, 1)
            attention, gram, scale = attention_block(
                head_size, raw, q_line, k_line, [sharp_ref[p * packed + k] for k in range(packed)]
            )
            at = pl.ds(p * head_size, head_size)
            attn_ref[at, :] = attention
            gram_ref[at, :] = gram
            scale_ref[at, :] = scale
            low = attention.astype(bf16)
            inside = (p * LANES) % GROUP
            for k in range(packed):
                block_ref[pl.ds(p * LANES + k * head_size, head_size), pl.ds(inside, LANES)] = jnp.where(
                    owner == k, low, jnp.zeros_like(low)
                )
        for g in range(width // GROUP):
            at = pl.ds(g * GROUP, GROUP)
            weights = block_ref[at, :]
            centre = dot_nt(v_ref[:, at], weights).astype(bf16)
            mixed_all[pl.ds(0, tokens), at] = centre
            mixed_ref[:, at] = centre
            mixed_all[pl.ds(tokens, side), at] = dot_nt(side_ref[pl.ds(0, side), at], weights).astype(bf16)
            mixed_all[pl.ds(tokens + side, 4 * ring), at] = dot_nt(
                rim_ref[pl.ds(0, 4 * ring), at], weights
            ).astype(bf16)

    chunk = pl.ds(pl.multiple_of(step * GROUP, GROUP), GROUP)
    projected_ref[...] = dot_nn(mixed_all[...], proj_ref[:, chunk])
    upside_ref[pl.ds(0, side), :] = side_ref[pl.ds(side, side), chunk].astype(f32)
    upside_ref[pl.ds(side, 2 * ring), :] = rim_ref[pl.ds(4 * ring, 2 * ring), chunk].astype(f32)

    def lanes_body(part, carry):
        lanes = pl.ds(pl.multiple_of(part * LANES, LANES), LANES)
        glob = pl.ds(pl.multiple_of(step * GROUP + part * LANES, LANES), LANES)
        taps = [taps_ref[pl.ds(t, 1), glob] for t in range(9)]

        def ring_row(r):
            if 0 <= r < tile_rows:
                return jnp.concatenate(
                    [
                        projected_ref[pl.ds(r * tile_cols, tile_cols), lanes],
                        projected_ref[pl.ds(tokens + r * RIM, RIM), lanes],
                    ],
                    axis=0,
                )
            k = r + 2 if r < 0 else r - tile_rows + 2
            return projected_ref[pl.ds(tokens + side + k * ring, ring), lanes]

        def up_row(r):
            if 0 <= r < tile_rows:
                return jnp.concatenate(
                    [
                        u_ref[pl.ds(r * tile_cols, tile_cols), glob].astype(f32),
                        upside_ref[pl.ds(r * RIM, RIM), lanes],
                    ],
                    axis=0,
                )
            k = 0 if r < 0 else 1
            return upside_ref[pl.ds(side + k * ring, ring), lanes]

        for r in range(-2, tile_rows + 2):
            field_ref[r + 2] = ring_row(r).astype(bf16).astype(f32)
        for r in range(-1, tile_rows + 1):
            near = [field_ref[r + 1 + a] for a in range(3)]
            sums = [sum(taps[3 * a + b] * near[a] for a in range(3)) for b in range(3)]
            total = pltpu.roll(sums[0], 1, 0) + sums[1] + pltpu.roll(sums[2], ring - 1, 0)
            active, slope = gelu_terms(total)
            slope_ref[r + 1] = (up_row(r) * slope).astype(bf16).astype(f32)
            if 0 <= r < tile_rows:
                at = pl.ds(r * tile_cols, tile_cols)
                merged_ref[at, glob] = (projected_ref[at, lanes] + active[:tile_cols]).astype(bf16)
        weights = [jnp.zeros((8, LANES), f32) for _ in range(9)]
        blank = jnp.zeros((RIM, LANES), f32)
        for r in range(tile_rows):
            near = [slope_ref[r + 2 - a] for a in range(3)]
            sums = [sum(taps[3 * a + b] * near[a] for a in range(3)) for b in range(3)]
            back = pltpu.roll(sums[0], ring - 1, 0) + sums[1] + pltpu.roll(sums[2], 1, 0)
            at = pl.ds(r * tile_cols, tile_cols)
            target_ref[at, glob] = (u_ref[at, glob].astype(f32) + back[:tile_cols]).astype(bf16)
            centre = jnp.concatenate([near[1][:tile_cols], blank], axis=0)
            shifted = [pltpu.roll(centre, ring - 1, 0), centre, pltpu.roll(centre, 1, 0)]
            for a in range(3):
                line = field_ref[r + 1 + a]
                for b in range(3):
                    product = shifted[b] * line
                    weights[3 * a + b] = weights[3 * a + b] + jnp.sum(
                        product.reshape(ring // 8, 8, LANES), axis=0
                    )
        for t in range(9):
            tapsum_ref[pl.ds(t, 1), glob] = jnp.sum(weights[t], axis=0, keepdims=True)
        return carry

    lax.fori_loop(0, GROUP // LANES, lanes_body, 0)

    @pl.when(step == last)
    def _():
        for g in range(width // GROUP):
            at = pl.ds(g * GROUP, GROUP)
            grad_ref[:, at] = dot_nt(target_ref[...], proj_ref[at, :]).astype(bf16)
        for g in range(width // GROUP):
            at = pl.ds(g * GROUP, GROUP)
            square = dot_tn(grad_ref[:, at], v_ref[:, at])
            for p in range(GROUP // LANES):
                cut = slice(p * LANES, (p + 1) * LANES)
                block = g * (GROUP // LANES) + p
                h, inner = divmod(block, half_blocks)
                packed_rows = pack_diagonal(square[cut, cut], head_size)
                tap_rows = tapsum_ref[:, pl.ds(block * LANES, LANES)]

                def put(ref, inner=inner, packed_rows=packed_rows, tap_rows=tap_rows):
                    ref[pl.ds(inner * head_size, head_size), :] = packed_rows
                    ref[pl.ds(half_blocks * head_size + inner * 16, 16), :] = tap_rows

                @pl.when(col_ref[0] == h)
                def _():
                    put(mine_ref)

                @pl.when(col_ref[0] != h)
                def _():
                    put(other_ref)


def middle_call(col, sharp, own, far, v, u, side, rim, proj, taps, tile, head_size):
    tokens, width = v.shape
    ring = tile[1] + RIM
    blocks = width // LANES
    grams = blocks * head_size
    lines = blocks // 2 * (head_size + 16)
    sds = jax.ShapeDtypeStruct
    outs = [
        sds((tokens, width), bf16),
        sds((grams, LANES), f32),
        sds((grams, LANES), f32),
        sds((grams, LANES), f32),
        sds((width, GROUP), bf16),
        sds((tokens, width), bf16),
        sds((tokens, width), bf16),
        sds((tokens, width), bf16),
        sds((lines, LANES), f32),
        sds((lines, LANES), f32),
    ]
    args = (col, sharp, own, far, v, u, side, rim, proj, taps)
    return pl.pallas_call(
        functools.partial(middle_kernel, head_size, tile),
        grid=(width // GROUP,),
        in_specs=[SCALAR, SCALAR] + [whole(x.shape) for x in args[2:]],
        out_specs=[whole(o.shape) for o in outs],
        out_shape=outs,
        scratch_shapes=[
            pltpu.VMEM((tokens + tile[0] * RIM + 4 * ring, width), bf16),
            pltpu.VMEM((tile[0] + 4, ring, LANES), f32),
            pltpu.VMEM((tile[0] + 2, ring, LANES), f32),
            pltpu.VMEM((tokens + tile[0] * RIM + 4 * ring, GROUP), f32),
            pltpu.VMEM((tile[0] * RIM + 2 * ring, GROUP), f32),
            pltpu.VMEM((16, width), f32),
        ],
        compiler_params=params(),
        name="middle",
    )(*args)


def projector_kernel(chunk, slots_ref, mixed_ref, target_ref, mine_ref, other_ref):
    step = pl.program_id(0)
    product = dot_tn(mixed_ref[...], target_ref[...])
    per = GROUP // chunk
    for k in range(per):
        piece = product[k * chunk : (k + 1) * chunk]
        far = slots_ref[0, step * per + k]
        at = pl.ds(pl.multiple_of(slots_ref[1, step * per + k] * chunk, chunk), chunk)

        @pl.when(far == 0)
        def _():
            mine_ref[at, :] = piece

        @pl.when(far != 0)
        def _():
            other_ref[at, :] = piece.astype(bf16)


def projector_call(slots, mixed, target, chunk):
    tokens, width = mixed.shape
    sds = jax.ShapeDtypeStruct
    outs = [sds((width // 2, width), f32), sds((width // 2, width), bf16)]
    return pl.pallas_call(
        functools.partial(projector_kernel, chunk),
        grid=(width // GROUP,),
        in_specs=[SCALAR, pl.BlockSpec((tokens, GROUP), lambda i: (0, i)), whole(target.shape)],
        out_specs=[whole(o.shape) for o in outs],
        out_shape=outs,
        compiler_params=params(),
        name="projector",
    )(slots, mixed, target)


def content_kernel(grad_ref, block_ref, out_ref):
    out_ref[...] = dot_nn(grad_ref[...], block_ref[...]).astype(bf16)


def content_call(grad, block):
    tokens, width = grad.shape
    return pl.pallas_call(
        content_kernel,
        grid=(width // GROUP,),
        in_specs=[
            pl.BlockSpec((tokens, GROUP), lambda i: (0, i)),
            pl.BlockSpec((GROUP, GROUP), lambda i: (i, 0)),
        ],
        out_specs=pl.BlockSpec((tokens, GROUP), lambda i: (0, i)),
        out_shape=jax.ShapeDtypeStruct((tokens, width), bf16),
        compiler_params=params(),
        name="content",
    )(grad, block)


def final_kernel(
    head_size,
    col_ref,
    sharp_ref,
    own_ref,
    far_ref,
    energy_own_ref,
    energy_far_ref,
    attn_ref,
    gram_ref,
    scale_ref,
    q_ref,
    k_ref,
    dq_ref,
    dk_ref,
    heat_ref,
    taps_ref,
    mixer_ref,
):
    step = pl.program_id(0)
    steps = pl.num_programs(0)
    packed = LANES // head_size
    per = GROUP // LANES
    half_blocks = steps * per // 2
    mine = (step // (steps // 2)) == col_ref[0]
    owner = lane_head(head_size)
    row = lax.broadcasted_iota(jnp.int32, (head_size, LANES), 0)
    lane = lax.broadcasted_iota(jnp.int32, (head_size, LANES), 1)
    mixer_ref[...] = jnp.zeros(mixer_ref.shape, bf16)
    q_terms, k_terms = [], []
    for p in range(per):
        block = step * per + p
        inner = lax.rem(block, half_blocks)

        def take(own, far, at, size):
            return jnp.where(mine, own[pl.ds(at, size), :], far[pl.ds(at, size), :])

        grad = take(own_ref, far_ref, pl.multiple_of(inner * head_size, head_size), head_size)
        taps_ref[:, pl.ds(p * LANES, LANES)] = take(
            own_ref, far_ref, pl.multiple_of(half_blocks * head_size + inner * 16, 16), 16
        )[:9]
        q_line = take(energy_own_ref, energy_far_ref, half_blocks * head_size + inner, 1)
        k_line = take(energy_own_ref, energy_far_ref, half_blocks * (head_size + 1) + inner, 1)
        at = pl.ds(pl.multiple_of(block * head_size, head_size), head_size)
        attention, gram, scale = attn_ref[at, :], gram_ref[at, :], scale_ref[at, :]
        scores = attention * (grad - sum_in_head(attention * grad, owner, packed))
        heated = scores * gram
        heat = by_head(
            [jnp.full(scores.shape, sharp_ref[block * packed + k], f32) for k in range(packed)], owner
        )
        for k in range(packed):
            heat_ref[block * packed + k] = jnp.sum(jnp.where(owner == k, heated, 0.0))
        gram_grad = heat * scores
        corr = gram_grad * gram
        k_corr = jnp.sum(corr, axis=0, keepdims=True)
        columns = sum_in_head(corr, owner, packed)
        q_corr = jnp.sum(jnp.where(lane == row + owner * head_size, columns, 0.0), axis=0, keepdims=True)
        q_scale = lax.rsqrt(q_line + epsilon)
        k_scale = lax.rsqrt(k_line + epsilon)
        q_terms.append(q_scale * q_scale * q_corr)
        k_terms.append(k_scale * k_scale * k_corr)
        low = (scale * gram_grad).astype(bf16)
        for k in range(packed):
            mixer_ref[pl.ds(p * LANES + k * head_size, head_size), pl.ds(p * LANES, LANES)] = jnp.where(
                owner == k, low, jnp.zeros_like(low)
            )
    q, k = q_ref[...], k_ref[...]
    mixer = mixer_ref[...]
    dq_ref[...] = (dot_nt(k, mixer) - q.astype(f32) * jnp.concatenate(q_terms, axis=1)).astype(bf16)
    dk_ref[...] = (dot_nn(q, mixer) - k.astype(f32) * jnp.concatenate(k_terms, axis=1)).astype(bf16)


def final_call(col, sharp, own, far, energy_own, energy_far, attn, gram, scale, q, k, head_size):
    tokens, width = q.shape
    sds = jax.ShapeDtypeStruct
    token_block = pl.BlockSpec((tokens, GROUP), lambda i: (0, i))
    args = (col, sharp, own, far, energy_own, energy_far, attn, gram, scale, q, k)
    return pl.pallas_call(
        functools.partial(final_kernel, head_size),
        grid=(width // GROUP,),
        in_specs=[SCALAR, SCALAR] + [whole(x.shape) for x in args[2:9]] + [token_block] * 2,
        out_specs=[
            token_block,
            token_block,
            SCALAR,
            pl.BlockSpec((9, GROUP), lambda i: (0, i)),
        ],
        out_shape=[
            sds((tokens, width), bf16),
            sds((tokens, width), bf16),
            sds(sharp.shape, f32),
            sds((9, width), f32),
        ],
        scratch_shapes=[pltpu.VMEM((GROUP, GROUP), bf16)],
        compiler_params=params(),
        name="final",
    )(*args)


def swap(x, axis, bit):
    return lax.ppermute(x, axis, [(i, i ^ bit) for i in range(lax.axis_size(axis))])


def row_bits():
    bits, bit = [], 1
    while bit < lax.axis_size("row"):
        bits.append(bit)
        bit *= 2
    return bits


def sum_halves(mine, other):
    total = mine + swap(other, "col", 1)
    for bit in row_bits():
        total = total + swap(total, "row", bit)
    return total, swap(total, "col", 1)


def halo(v, u):
    tile_rows, tile_cols, width = v.shape
    rows, cols = lax.axis_size("row"), lax.axis_size("col")
    down = [(i, i + 1) for i in range(rows - 1)]
    up = [(i + 1, i) for i in range(rows - 1)]
    above = lax.ppermute(jnp.concatenate([v[-2:], u[-1:]]), "row", down)
    below = lax.ppermute(jnp.concatenate([v[:2], u[:1]]), "row", up)
    rim = jnp.concatenate([above[:2], below[:2], above[2:], below[2:]])
    first = lax.axis_index("col") == 0
    edge = jnp.concatenate(
        [jnp.where(first, x[:, -2:], x[:, :2]) for x in (v, u, rim)]
    )
    got = swap(edge, "col", 1)
    none = jnp.zeros((got.shape[0], RIM - 2, width), got.dtype)
    side = jnp.where(
        first,
        jnp.concatenate([got, none], axis=1),
        jnp.concatenate([none, got], axis=1),
    )
    rim = jnp.concatenate([rim, side[2 * tile_rows :]], axis=1)
    return (
        side[: 2 * tile_rows].reshape(2 * tile_rows * RIM, width),
        rim.reshape(6 * (tile_cols + RIM), width),
    )


def projector_sum(mine, other):
    total = mine + swap(other, "col", 1).astype(f32)
    for bit in row_bits():
        half = total.shape[0] // 2
        total = total[:half] + swap(total[half:].astype(bf16), "row", bit).astype(f32)
    return total


def projector_slots():
    rows, cols = lax.axis_size("row"), lax.axis_size("col")
    piece = jnp.arange(rows * cols, dtype=jnp.int32)
    away = (piece // cols) ^ lax.axis_index("row")
    place = jnp.zeros_like(piece)
    for bit in row_bits():
        place = 2 * place + (away // bit) % 2
    return jnp.stack([(piece % cols) ^ lax.axis_index("col"), place])


def shards(q, k, v, u, sharp, proj, taps):
    tile = v.shape[:2]
    width = v.shape[2]
    tokens = tile[0] * tile[1]
    head_size = width // sharp.shape[0]
    flat = lambda x: x.reshape(tokens, width)
    col = lax.axis_index("col").astype(jnp.int32).reshape(1)
    q2, k2, v2, u2 = flat(q), flat(k), flat(v), flat(u)
    energy_own, energy_far = sum_halves(*gram_call(col, q2, k2, head_size))
    side, rim = halo(v, u)
    (merged, attn, gram, scale, block, mixed, target, grad, mine, other) = middle_call(
        col, sharp, energy_own, energy_far, v2, u2, side, rim, proj, taps, tile, head_size
    )
    own, far = sum_halves(mine, other)
    chunk = width // (lax.axis_size("row") * lax.axis_size("col"))
    projector = projector_sum(*projector_call(projector_slots(), mixed, target, chunk))
    content = content_call(grad, block)
    dq, dk, heat, tap_sums = final_call(
        col, sharp, own, far, energy_own, energy_far, attn, gram, scale, q2, k2, head_size
    )
    full = lambda x: x.reshape(tile + (width,))
    return full(merged), full(dq), full(dk), full(content), heat, tap_sums, projector


def solution(mesh):
    field = P(("scene", "row"), "col", None)
    return jax.shard_map(
        shards,
        mesh=mesh,
        in_specs=(field, field, field, field, P(), P(), P()),
        out_specs=(
            field,
            field,
            field,
            field,
            P("scene"),
            P("scene", None),
            P(("scene", "row", "col"), None),
        ),
        check_vma=False,
    )
```

```python
import functools

import jax
import jax.numpy as jnp
from jax import lax
from jax.experimental import pallas as pl
from jax.experimental.pallas import tpu as pltpu
from jax.sharding import PartitionSpec as P

epsilon = 1e-06
inverse_root = 0.7071067811865476
density_root = 0.3989422804014327
LANES = 128
GROUP = 256
RIM = 8
f32 = jnp.float32
bf16 = jnp.bfloat16
VMEM_LIMIT = 24 * 1024 * 1024


def whole(shape):
    return pl.BlockSpec(shape, lambda *_: (0,) * len(shape))


SCALAR = pl.BlockSpec(memory_space=pltpu.SMEM)
LOCAL = pl.BlockSpec(memory_space=pltpu.VMEM)


def params(limit=VMEM_LIMIT):
    return pltpu.CompilerParams(vmem_limit_bytes=limit)


def cost(microseconds):
    return pl.CostEstimate(flops=0, bytes_accessed=int(microseconds * 3.6e6), transcendentals=0)


def pad_lines(lines, count):
    blank = jnp.zeros((count - len(lines), LANES), f32)
    return jnp.concatenate(lines + [blank], axis=0) if count > len(lines) else jnp.concatenate(lines, axis=0)


def dot_tn(a, b):
    return lax.dot_general(a, b, (((0,), (0,)), ((), ())), preferred_element_type=f32)


def dot_nt(a, b):
    return lax.dot_general(a, b, (((1,), (1,)), ((), ())), preferred_element_type=f32)


def dot_nn(a, b):
    return jnp.dot(a, b, preferred_element_type=f32)


def lane_head(head_size):
    return lax.broadcasted_iota(jnp.int32, (head_size, LANES), 1) // head_size


def by_head(parts, owner):
    out = parts[0]
    for k in range(1, len(parts)):
        out = jnp.where(owner == k, parts[k], out)
    return out


def pack_diagonal(square, head_size):
    owner = lane_head(head_size)
    return by_head(
        [square[k * head_size : (k + 1) * head_size] for k in range(LANES // head_size)], owner
    )


def sum_in_head(values, owner, packed):
    sums = [jnp.sum(jnp.where(owner == k, values, 0.0), axis=1, keepdims=True) for k in range(packed)]
    return by_head([jnp.broadcast_to(s, values.shape) for s in sums], owner)


def edges_kernel(here_ref, v_head, v_tail, u_head, u_tail, twin_ref, next_ref):
    even = lax.rem(here_ref[1], 2) == 0

    def put(tail_ref, head_ref):
        tail_ref[:2] = v_tail[...]
        tail_ref[2:] = u_tail[...]
        head_ref[:2] = v_head[...]
        head_ref[2:] = u_head[...]

    @pl.when(even)
    def _():
        put(twin_ref, next_ref)

    @pl.when(jnp.logical_not(even))
    def _():
        put(next_ref, twin_ref)


def edges_call(here, v, u):
    rows, cols, width = v.shape
    out = jax.ShapeDtypeStruct((3, cols, width), bf16)
    return pl.pallas_call(
        edges_kernel,
        grid=(1,),
        in_specs=[
            SCALAR,
            pl.BlockSpec((2, cols, width), lambda i: (0, 0, 0)),
            pl.BlockSpec((2, cols, width), lambda i: (rows // 2 - 1, 0, 0)),
            pl.BlockSpec((1, cols, width), lambda i: (0, 0, 0)),
            pl.BlockSpec((1, cols, width), lambda i: (rows - 1, 0, 0)),
        ],
        out_specs=[LOCAL, LOCAL],
        out_shape=[out, out],
        compiler_params=params(),
        cost_estimate=cost(1),
        name="edges",
    )(here, v, v, u, u)


def gram_kernel(head_size, col_ref, q_ref, k_ref, mine_ref, other_ref):
    half = pl.program_id(0)
    per = GROUP // LANES
    energy = mine_ref.shape[0] - 16
    values = []
    for g in range(q_ref.shape[1] // GROUP):
        at = pl.ds(g * GROUP, GROUP)
        square = dot_tn(q_ref[:, at], k_ref[:, at])
        for p in range(per):
            cut = slice(p * LANES, (p + 1) * LANES)
            block = g * per + p
            values.append((block * head_size, pack_diagonal(square[cut, cut], head_size)))
            for line, ref in ((energy, q_ref), (energy + 8, k_ref)):
                x = ref[:, pl.ds(block * LANES, LANES)].astype(f32)
                values.append((line + block, jnp.sum(x * x, axis=0, keepdims=True)))

    def put(ref):
        for at, value in values:
            ref[pl.ds(at, value.shape[0]), :] = value

    @pl.when(half == 0)
    def _():
        mine_ref[pl.ds(energy, 16), :] = jnp.zeros((16, LANES), f32)
        other_ref[pl.ds(energy, 16), :] = jnp.zeros((16, LANES), f32)

    @pl.when(half == col_ref[0])
    def _():
        put(mine_ref)

    @pl.when(half != col_ref[0])
    def _():
        put(other_ref)


def gram_call(col, q, k, head_size):
    tokens, width = q.shape
    lines = width // 2 // LANES * head_size + 16
    out = jax.ShapeDtypeStruct((lines, LANES), f32)
    return pl.pallas_call(
        functools.partial(gram_kernel, head_size),
        grid=(2,),
        in_specs=[
            SCALAR,
            pl.BlockSpec((tokens, width // 2), lambda i: (0, i)),
            pl.BlockSpec((tokens, width // 2), lambda i: (0, i)),
        ],
        out_specs=[LOCAL, LOCAL],
        out_shape=[out, out],
        compiler_params=params(60 * 1024 * 1024),
        cost_estimate=cost(2.5),
        name="gram",
    )(col, q, k)


def gelu_terms(u):
    cumul = 0.5 * (1.0 + lax.erf(u * inverse_root))
    return u * cumul, cumul + u * jnp.exp(-0.5 * u * u) * density_root


def attention_block(head_size, raw, q_line, k_line, sharp):
    packed = LANES // head_size
    owner = lane_head(head_size)
    row = lax.broadcasted_iota(jnp.int32, (head_size, LANES), 0)
    lane = lax.broadcasted_iota(jnp.int32, (head_size, LANES), 1)
    q_energy = by_head(
        [
            jnp.broadcast_to(
                jnp.sum(jnp.where(lane == row + k * head_size, q_line, 0.0), axis=1, keepdims=True),
                raw.shape,
            )
            for k in range(packed)
        ],
        owner,
    )
    q_scale = lax.rsqrt(q_energy + epsilon)
    k_scale = lax.rsqrt(k_line + epsilon)
    gram = q_scale * raw * k_scale
    heat = by_head([jnp.full(raw.shape, s, f32) for s in sharp], owner)
    numer = jnp.exp(heat * gram)
    attention = numer / sum_in_head(numer, owner, packed)
    return attention, gram, q_scale * k_scale


def attention_phase(
    head_size, col_ref, sharp_ref, own_ref, far_ref, attn_ref, gram_ref, scale_ref, block_ref
):
    packed = LANES // head_size
    blocks = attn_ref.shape[0] // head_size
    half_blocks = blocks // 2
    is_first = col_ref[0] == 0
    block_ref[...] = jnp.zeros(block_ref.shape, bf16)
    owner = lane_head(head_size)
    for p in range(blocks):
        h, inner = divmod(p, half_blocks)

        def take(at, size):
            a = own_ref[pl.ds(at, size), :]
            b = far_ref[pl.ds(at, size), :]
            return jnp.where(is_first, a, b) if h == 0 else jnp.where(is_first, b, a)

        raw = take(inner * head_size, head_size)
        q_line = take(half_blocks * head_size + inner, 1)
        k_line = take(half_blocks * head_size + 8 + inner, 1)
        attention, gram, scale = attention_block(
            head_size, raw, q_line, k_line, [sharp_ref[p * packed + k] for k in range(packed)]
        )
        at = pl.ds(p * head_size, head_size)
        attn_ref[at, :] = attention
        gram_ref[at, :] = gram
        scale_ref[at, :] = scale
        low = attention.astype(bf16)
        inside = (p * LANES) % GROUP
        for k in range(packed):
            block_ref[pl.ds(p * LANES + k * head_size, head_size), pl.ds(inside, LANES)] = jnp.where(
                owner == k, low, jnp.zeros_like(low)
            )


def keep_side(col_ref, shape):
    place = lax.rem(lax.broadcasted_iota(jnp.int32, shape, 0), RIM)
    second = col_ref[0].astype(f32)
    right = jnp.where(place < 2, 1.0, 0.0)
    left = jnp.where(place >= RIM - 2, 1.0, 0.0)
    return right + second * (left - right)


def stencil_chunk(
    step, tile, col_ref, u_ref, side_ref, twin_ref, next_ref, corner_ref, mixed_all, proj, taps_ref,
    merged_ref, target_ref, tapsum_ref, field_ref, slope_ref, projected_ref, upside_ref,
    first_channel,
):
    tile_rows, tile_cols = tile
    tokens = tile_rows * tile_cols
    ring = tile_cols + RIM
    side = tile_rows * RIM
    chunk = pl.ds(pl.multiple_of(first_channel + step * GROUP, GROUP), GROUP)
    here = pl.ds(pl.multiple_of(step * GROUP, GROUP), GROUP)
    projected_ref[...] = dot_nn(mixed_all[...], proj[:, chunk])
    for at, size, ref, start in (
        (0, side, side_ref, side),
        (side, tile_cols, twin_ref, 2 * tile_cols),
        (side + tile_cols, tile_cols, next_ref, 2 * tile_cols),
        (side + 2 * tile_cols, 2 * RIM, corner_ref, 4 * RIM),
    ):
        piece = ref[pl.ds(start, size), chunk].astype(f32)
        if ref is side_ref or ref is corner_ref:
            piece = piece * keep_side(col_ref, piece.shape)
        upside_ref[pl.ds(at, size), :] = piece

    def lanes_body(part, carry):
        lanes = pl.ds(pl.multiple_of(part * LANES, LANES), LANES)
        glob = pl.ds(pl.multiple_of(first_channel + step * GROUP + part * LANES, LANES), LANES)
        away = pl.ds(pl.multiple_of(step * GROUP + part * LANES, LANES), LANES)
        taps = [taps_ref[pl.ds(t, 1), glob] for t in range(9)]
        rim = tokens + side
        from_next = 1 - lax.rem(col_ref[1], 2)

        def ring_row(r):
            if 0 <= r < tile_rows:
                pieces = (r * tile_cols, tokens + r * RIM)
            else:
                k = r + 2 if r < 0 else r - tile_rows
                k = k + 2 * (from_next if r < 0 else 1 - from_next)
                pieces = (
                    pl.multiple_of(rim + k * tile_cols, RIM),
                    pl.multiple_of(rim + 4 * tile_cols + k * RIM, RIM),
                )
            return jnp.concatenate(
                [
                    projected_ref[pl.ds(pieces[0], tile_cols), lanes],
                    projected_ref[pl.ds(pieces[1], RIM), lanes],
                ],
                axis=0,
            )

        def up_row(r):
            if 0 <= r < tile_rows:
                return jnp.concatenate(
                    [
                        u_ref[pl.ds(r * tile_cols, tile_cols), glob].astype(f32),
                        upside_ref[pl.ds(r * RIM, RIM), lanes],
                    ],
                    axis=0,
                )
            k = from_next if r < 0 else 1 - from_next
            pieces = (
                pl.multiple_of(side + k * tile_cols, RIM),
                pl.multiple_of(side + 2 * tile_cols + k * RIM, RIM),
            )
            return jnp.concatenate(
                [
                    upside_ref[pl.ds(pieces[0], tile_cols), lanes],
                    upside_ref[pl.ds(pieces[1], RIM), lanes],
                ],
                axis=0,
            )

        for r in range(-2, tile_rows + 2):
            field_ref[r + 2] = ring_row(r).astype(bf16).astype(f32)
        for r in range(-1, tile_rows + 1):
            near = [field_ref[r + 1 + a] for a in range(3)]
            sums = [sum(taps[3 * a + b] * near[a] for a in range(3)) for b in range(3)]
            total = pltpu.roll(sums[0], 1, 0) + sums[1] + pltpu.roll(sums[2], ring - 1, 0)
            active, slope = gelu_terms(total)
            slope_ref[r + 1] = (up_row(r) * slope).astype(bf16).astype(f32)
            if 0 <= r < tile_rows:
                at = pl.ds(r * tile_cols, tile_cols)
                merged_ref[at, lanes] = (projected_ref[at, lanes] + active[:tile_cols]).astype(bf16)
        weights = [jnp.zeros((8, LANES), f32) for _ in range(9)]
        blank = jnp.zeros((RIM, LANES), f32)
        for r in range(tile_rows):
            near = [slope_ref[r + 2 - a] for a in range(3)]
            sums = [sum(taps[3 * a + b] * near[a] for a in range(3)) for b in range(3)]
            back = pltpu.roll(sums[0], ring - 1, 0) + sums[1] + pltpu.roll(sums[2], 1, 0)
            at = pl.ds(r * tile_cols, tile_cols)
            target_ref[at, away] = (u_ref[at, glob].astype(f32) + back[:tile_cols]).astype(bf16)
            centre = jnp.concatenate([near[1][:tile_cols], blank], axis=0)
            shifted = [pltpu.roll(centre, ring - 1, 0), centre, pltpu.roll(centre, 1, 0)]
            for a in range(3):
                line = field_ref[r + 1 + a]
                for b in range(3):
                    product = shifted[b] * line
                    weights[3 * a + b] = weights[3 * a + b] + jnp.sum(
                        product.reshape(ring // 8, 8, LANES), axis=0
                    )
        for t in range(9):
            tapsum_ref[pl.ds(t, 1), away] = jnp.sum(weights[t], axis=0, keepdims=True)
        return carry

    lax.fori_loop(0, GROUP // LANES, lanes_body, 0)


def spread_product(piece_rows, cols, order, here_ref, mixed_all, target_ref, mine_ref, other_ref):
    tokens = target_ref.shape[0]
    axis, bit = order[0]
    apart = bit if axis == "col" else bit * cols
    index = {"col": here_ref[0], "row": here_ref[1]}
    flipped = (index[axis] // bit) % 2 == 1
    per = GROUP // piece_rows
    for g in range(mixed_all.shape[1] // GROUP):
        product = dot_tn(mixed_all[pl.ds(0, tokens), pl.ds(g * GROUP, GROUP)], target_ref[...])
        for k in range(per):
            if k & apart:
                continue
            owner = g * per + k
            a, b = (product[x * piece_rows : (x + 1) * piece_rows] for x in (k, k | apart))
            away = {"col": (owner % cols) ^ index["col"], "row": (owner // cols) ^ index["row"]}
            place = 0
            for name, digit in order[1:]:
                place = 2 * place + (away[name] // digit) % 2
            at = pl.ds(pl.multiple_of(place * piece_rows, piece_rows), piece_rows)
            mine_ref[at, :] = jnp.where(flipped, b, a)
            other_ref[at, :] = jnp.where(flipped, a, b).astype(bf16)


def front_kernel(
    head_size, tile, piece_rows, cols, order,
    col_ref, sharp_ref, own_ref, far_ref, v_ref, u_ref, side_ref, twin_ref, next_ref,
    corner_ref, proj_ref, taps_ref,
    merged_ref, attn_ref, gram_ref, scale_ref, block_ref, mixed_all, target_ref, tapsum_ref,
    mine_ref, other_ref,
    field_ref, slope_ref, projected_ref, upside_ref,
):
    step = pl.program_id(0)
    tile_rows, tile_cols = tile
    tokens, width = v_ref.shape
    side = tile_rows * RIM
    two = 2 * tile_cols

    @pl.when(step == 0)
    def _():
        tapsum_ref[...] = jnp.zeros(tapsum_ref.shape, f32)
        attention_phase(
            head_size, col_ref, sharp_ref, own_ref, far_ref, attn_ref, gram_ref, scale_ref, block_ref
        )
        for g in range(width // GROUP):
            at = pl.ds(g * GROUP, GROUP)
            weights = block_ref[at, :]
            mixed_all[pl.ds(0, tokens), at] = dot_nt(v_ref[:, at], weights).astype(bf16)
            around = [(side_ref, side), (twin_ref, two), (next_ref, two), (corner_ref, 4 * RIM)]
            value = dot_nt(
                jnp.concatenate([ref[pl.ds(0, size), at] for ref, size in around], axis=0), weights
            )
            start = 0
            for ref, size in around:
                piece = value[start : start + size]
                if ref is side_ref or ref is corner_ref:
                    piece = piece * keep_side(col_ref, piece.shape)
                mixed_all[pl.ds(tokens + start, size), at] = piece.astype(bf16)
                start += size

    stencil_chunk(
        step, tile, col_ref, u_ref, side_ref, twin_ref, next_ref, corner_ref, mixed_all, proj_ref,
        taps_ref, merged_ref, target_ref, tapsum_ref, field_ref, slope_ref, projected_ref, upside_ref, 0,
    )

    @pl.when(step == pl.num_programs(0) - 1)
    def _():
        spread_product(piece_rows, cols, order, col_ref, mixed_all, target_ref, mine_ref, other_ref)


def back_kernel(
    head_size, tile, first_channel,
    col_ref, u_ref, v_ref, side_ref, twin_ref, next_ref, corner_ref, mixed_all, proj_ref, taps_ref,
    front_target, front_taps, merged_before,
    merged_ref, target_ref, grad_ref, mine_ref, other_ref,
    field_ref, slope_ref, projected_ref, upside_ref, tapsum_ref, whole_ref,
):
    step = pl.program_id(0)
    last = pl.num_programs(0) - 1
    tokens, width = v_ref.shape
    blocks = width // LANES
    half_blocks = blocks // 2

    @pl.when(step == 0)
    def _():
        tapsum_ref[...] = jnp.zeros(tapsum_ref.shape, f32)

    stencil_chunk(
        step, tile, col_ref, u_ref, side_ref, twin_ref, next_ref, corner_ref, mixed_all, proj_ref,
        taps_ref, merged_ref, target_ref, tapsum_ref, field_ref, slope_ref, projected_ref, upside_ref,
        first_channel,
    )

    @pl.when(step == last)
    def _():
        whole_ref[:, pl.ds(0, first_channel)] = front_target[...]
        whole_ref[:, pl.ds(first_channel, width - first_channel)] = target_ref[...]
        grad_ref[...] = dot_nt(whole_ref[...], proj_ref[...]).astype(bf16)
        for g in range(width // GROUP):
            at = pl.ds(g * GROUP, GROUP)
            square = dot_tn(grad_ref[:, at], v_ref[:, at])
            for p in range(GROUP // LANES):
                cut = slice(p * LANES, (p + 1) * LANES)
                block = g * (GROUP // LANES) + p
                h, inner = divmod(block, half_blocks)
                packed_rows = pack_diagonal(square[cut, cut], head_size)
                if block * LANES < first_channel:
                    tap_rows = front_taps[:, pl.ds(block * LANES, LANES)]
                else:
                    tap_rows = tapsum_ref[:, pl.ds(block * LANES - first_channel, LANES)]

                def put(ref, inner=inner, packed_rows=packed_rows, tap_rows=tap_rows):
                    ref[pl.ds(inner * head_size, head_size), :] = packed_rows.astype(ref.dtype)
                    ref[pl.ds(half_blocks * head_size + inner * 16, 16), :] = tap_rows.astype(ref.dtype)

                @pl.when(col_ref[0] == h)
                def _():
                    put(mine_ref)

                @pl.when(col_ref[0] != h)
                def _():
                    put(other_ref)


def stencil_scratch(tile):
    ring = tile[1] + RIM
    return [
        pltpu.VMEM((tile[0] + 4, ring, LANES), f32),
        pltpu.VMEM((tile[0] + 2, ring, LANES), f32),
        pltpu.VMEM(((tile[0] + 4) * ring, GROUP), f32),
        pltpu.VMEM(((tile[0] + 2) * ring, GROUP), f32),
    ]


def front_call(col, sharp, own, far, v, u, halo, proj, taps, tile, head_size, piece_rows, cols, order):
    tokens, width = v.shape
    ring = tile[1] + RIM
    span = width // 2
    grams = width // LANES * head_size
    sds = jax.ShapeDtypeStruct
    outs = [
        sds((tokens, width), bf16),
        sds((grams, LANES), f32),
        sds((grams, LANES), f32),
        sds((grams, LANES), f32),
        sds((width, GROUP), bf16),
        sds(((tile[0] + 4) * ring, width), bf16),
        sds((tokens, span), bf16),
        sds((16, span), f32),
        sds((width // 2, span), f32),
        sds((width // 2, span), bf16),
    ]
    args = (col, sharp, own, far, v, u, *halo, proj, taps)
    return pl.pallas_call(
        functools.partial(front_kernel, head_size, tile, piece_rows, cols, order),
        grid=(span // GROUP,),
        in_specs=[SCALAR] * 2 + [LOCAL] * (len(args) - 2),
        out_specs=[pl.BlockSpec((tokens, GROUP), lambda i: (0, i))] + [LOCAL] * (len(outs) - 1),
        out_shape=outs,
        scratch_shapes=stencil_scratch(tile),
        compiler_params=params(),
        cost_estimate=cost(10),
        name="front",
    )(*args)


def back_call(col, u, v, halo, mixed_all, proj, taps, target, tapsum, merged, tile, head_size):
    tokens, width = v.shape
    span = width // 2
    lines = width // LANES // 2 * (head_size + 16)
    sds = jax.ShapeDtypeStruct
    outs = [
        sds((tokens, width), bf16),
        sds((tokens, span), bf16),
        sds((tokens, width), bf16),
        sds((lines, LANES), f32),
        sds((lines, LANES), bf16),
    ]
    args = (col, u, v, *halo, mixed_all, proj, taps, target, tapsum, merged)
    first = span // GROUP
    return pl.pallas_call(
        functools.partial(back_kernel, head_size, tile, span),
        grid=(span // GROUP,),
        in_specs=[SCALAR] + [LOCAL] * (len(args) - 2) + [pl.BlockSpec(memory_space=pl.ANY)],
        out_specs=[pl.BlockSpec((tokens, GROUP), lambda i: (0, i + first))] + [LOCAL] * (len(outs) - 1),
        out_shape=outs,
        input_output_aliases={len(args) - 1: 0},
        scratch_shapes=stencil_scratch(tile)
        + [pltpu.VMEM((16, span), f32), pltpu.VMEM((tokens, width), bf16)],
        compiler_params=params(),
        cost_estimate=cost(10),
        name="back",
    )(*args)


def projector_kernel(
    piece_rows, cols, order, here_ref, mixed_all, target_ref, after_ref, mine_ref, other_ref
):
    spread_product(piece_rows, cols, order, here_ref, mixed_all, target_ref, mine_ref, other_ref)


def projector_call(here, mixed_all, target, after, piece_rows, cols, order):
    width, span = mixed_all.shape[1], target.shape[1]
    sds = jax.ShapeDtypeStruct
    return pl.pallas_call(
        functools.partial(projector_kernel, piece_rows, cols, order),
        in_specs=[SCALAR, LOCAL, LOCAL, pl.BlockSpec(memory_space=pl.ANY)],
        out_specs=[LOCAL, LOCAL],
        out_shape=[sds((width // 2, span), f32), sds((width // 2, span), bf16)],
        compiler_params=params(),
        cost_estimate=cost(2),
        name="projector",
    )(here, mixed_all, target, after)


def content_kernel(grad_ref, block_ref, after_ref, out_ref):
    span = out_ref.shape[1]
    for g in range(span // GROUP):
        at = pl.ds(pl.multiple_of(pl.program_id(0) * span + g * GROUP, GROUP), GROUP)
        out_ref[:, pl.ds(g * GROUP, GROUP)] = dot_nn(grad_ref[:, at], block_ref[at, :]).astype(bf16)


def content_call(grad, block, after):
    tokens, width = grad.shape
    return pl.pallas_call(
        content_kernel,
        grid=(2,),
        in_specs=[LOCAL] * 2 + [pl.BlockSpec(memory_space=pl.ANY)],
        out_specs=pl.BlockSpec((tokens, width // 2), lambda i: (0, i)),
        out_shape=jax.ShapeDtypeStruct((tokens, width), bf16),
        compiler_params=params(),
        cost_estimate=cost(2),
        name="content",
    )(grad, block, after)


def final_kernel(
    head_size,
    col_ref,
    sharp_ref,
    own_ref,
    far_ref,
    energy_own_ref,
    energy_far_ref,
    attn_ref,
    gram_ref,
    scale_ref,
    q_ref,
    k_ref,
    dq_ref,
    dk_ref,
    heat_ref,
    taps_ref,
    mixer_ref,
):
    step = pl.program_id(0)
    steps = pl.num_programs(0)
    packed = LANES // head_size
    per = GROUP // LANES
    half_blocks = steps * per // 2
    mine = (step // (steps // 2)) == col_ref[0]
    owner = lane_head(head_size)
    row = lax.broadcasted_iota(jnp.int32, (head_size, LANES), 0)
    lane = lax.broadcasted_iota(jnp.int32, (head_size, LANES), 1)
    mixer_ref[...] = jnp.zeros(mixer_ref.shape, bf16)
    q_terms, k_terms = [], []
    for p in range(per):
        block = step * per + p
        inner = lax.rem(block, half_blocks)

        def take(own, far, at, size):
            return jnp.where(mine, own[pl.ds(at, size), :], far[pl.ds(at, size), :])

        grad = take(own_ref, far_ref, pl.multiple_of(inner * head_size, head_size), head_size)
        taps_ref[:, pl.ds(p * LANES, LANES)] = take(
            own_ref, far_ref, pl.multiple_of(half_blocks * head_size + inner * 16, 16), 16
        )[:9]
        q_line = take(energy_own_ref, energy_far_ref, half_blocks * head_size + inner, 1)
        k_line = take(energy_own_ref, energy_far_ref, half_blocks * head_size + 8 + inner, 1)
        at = pl.ds(pl.multiple_of(block * head_size, head_size), head_size)
        attention, gram, scale = attn_ref[at, :], gram_ref[at, :], scale_ref[at, :]
        scores = attention * (grad - sum_in_head(attention * grad, owner, packed))
        heated = scores * gram
        heat = by_head(
            [jnp.full(scores.shape, sharp_ref[block * packed + k], f32) for k in range(packed)], owner
        )
        for k in range(packed):
            heat_ref[block * packed + k] = jnp.sum(jnp.where(owner == k, heated, 0.0))
        gram_grad = heat * scores
        corr = gram_grad * gram
        k_corr = jnp.sum(corr, axis=0, keepdims=True)
        columns = sum_in_head(corr, owner, packed)
        q_corr = jnp.sum(jnp.where(lane == row + owner * head_size, columns, 0.0), axis=0, keepdims=True)
        q_scale = lax.rsqrt(q_line + epsilon)
        k_scale = lax.rsqrt(k_line + epsilon)
        q_terms.append(q_scale * q_scale * q_corr)
        k_terms.append(k_scale * k_scale * k_corr)
        low = (scale * gram_grad).astype(bf16)
        for k in range(packed):
            mixer_ref[pl.ds(p * LANES + k * head_size, head_size), pl.ds(p * LANES, LANES)] = jnp.where(
                owner == k, low, jnp.zeros_like(low)
            )
    here = pl.ds(pl.multiple_of(step * GROUP, GROUP), GROUP)
    q, k = q_ref[:, here], k_ref[:, here]
    mixer = mixer_ref[...]
    dq_ref[...] = (dot_nt(k, mixer) - q.astype(f32) * jnp.concatenate(q_terms, axis=1)).astype(bf16)
    dk_ref[...] = (dot_nn(q, mixer) - k.astype(f32) * jnp.concatenate(k_terms, axis=1)).astype(bf16)


def final_call(col, sharp, own, far, energy_own, energy_far, attn, gram, scale, q, k, head_size):
    tokens, width = q.shape
    sds = jax.ShapeDtypeStruct
    token_block = pl.BlockSpec((tokens, GROUP), lambda i: (0, i))
    args = (col, sharp, own, far, energy_own, energy_far, attn, gram, scale, q, k)
    return pl.pallas_call(
        functools.partial(final_kernel, head_size),
        grid=(width // GROUP,),
        in_specs=[SCALAR, SCALAR] + [LOCAL] * 9,
        out_specs=[
            token_block,
            token_block,
            SCALAR,
            pl.BlockSpec((9, GROUP), lambda i: (0, i)),
        ],
        out_shape=[
            sds((tokens, width), bf16),
            sds((tokens, width), bf16),
            sds(sharp.shape, f32),
            sds((9, width), f32),
        ],
        scratch_shapes=[pltpu.VMEM((GROUP, GROUP), bf16)],
        compiler_params=params(),
        cost_estimate=cost(5),
        name="final",
    )(*args)


def swap(x, axis, bit):
    return lax.ppermute(x, axis, [(i, i ^ bit) for i in range(lax.axis_size(axis))])


def row_bits():
    bits, bit = [], 1
    while bit < lax.axis_size("row"):
        bits.append(bit)
        bit *= 2
    return bits


def halve(total):
    half = total.shape[0] // 2
    return total[:half], total[half:].astype(bf16)


def add_low(total, got):
    return total + got.astype(f32)


def add_step(total, axis, bit):
    low = total.astype(bf16)
    return low.astype(f32) + swap(low, axis, bit).astype(f32)


def scatter_step(total, group):
    count = 2 ** len(group)
    rows = total.shape[0] // count
    out = total[:rows]
    for k in range(1, count):
        mask = sum(bit for i, bit in enumerate(group) if (k >> (len(group) - 1 - i)) & 1)
        out = add_low(out, swap(total[k * rows : (k + 1) * rows].astype(bf16), "row", mask))
    return out


def scatter_both(first, second, group):
    early, late = group
    quarter, half = first.shape[0] // 4, second.shape[0] // 2
    pieces = [first[k * quarter : (k + 1) * quarter] for k in range(4)]
    joint = swap(jnp.concatenate([pieces[1], second[half:]]).astype(bf16), "row", late)
    first = add_low(pieces[0], swap(pieces[2].astype(bf16), "row", early))
    first = add_low(first, swap(pieces[3].astype(bf16), "row", early | late))
    return add_low(first, joint[:quarter]), add_low(second[:half], joint[quarter:])


def tie(*values):
    return lax.optimization_barrier(values)


def shards(q, k, v, u, sharp, proj, taps):
    tile = v.shape[:2]
    width = v.shape[2]
    tokens = tile[0] * tile[1]
    head_size = width // sharp.shape[0]
    rows, cols = lax.axis_size("row"), lax.axis_size("col")
    flat = lambda x: x.reshape(tokens, width)
    here = jnp.stack([lax.axis_index("col"), lax.axis_index("row")]).astype(jnp.int32)
    q2, k2, v2, u2 = flat(q), flat(k), flat(v), flat(u)
    bits = row_bits()
    early = [("row", bits[0]), ("col", 1)] + [("row", bit) for bit in bits[1:]]
    late = [("col", 1)] + [("row", bit) for bit in bits]
    piece_rows = width // (rows * cols)

    mine, other = gram_call(here, q2, k2, head_size)
    to_twin, to_next = edges_call(here, v, u)
    total = add_low(mine, swap(other, "col", 1))
    start = jnp.where(lax.axis_index("col") == 0, v.shape[1] - RIM, 0)
    edge = lambda x: lax.dynamic_slice_in_dim(x, start, RIM, axis=1)
    pairs_next = [(j, j + 1) for j in range(1, rows - 1, 2)]
    pairs_next = pairs_next + [(b, a) for a, b in pairs_next]
    side = swap(jnp.concatenate([edge(v), edge(u)]), "col", 1)
    for i, bit in enumerate(bits):
        total = total + swap(total, "row", bit)
        if i == 1:
            from_twin = swap(to_twin, "row", 1)
            total, from_twin = tie(total, from_twin)
        if i == 2:
            from_next = lax.ppermute(to_next, "row", pairs_next)
            total, from_next = tie(total, from_next)
    corner = swap(
        edge(jnp.concatenate([from_twin[:2], from_next[:2], from_twin[2:], from_next[2:]])), "col", 1
    )
    around = tuple(x.reshape(-1, width) for x in (side, from_twin, from_next, corner))
    energy_own, energy_far = total, swap(total, "col", 1)

    (merged, attn, gram, scale, block, mixed_all, front_target, front_taps, mine, other) = front_call(
        here, sharp, energy_own, energy_far, v2, u2, around, proj, taps, tile, head_size, piece_rows, cols, early
    )
    halves = [swap(x, "row", bits[0]) for x in jnp.split(other, 2)]
    first = halves[:1]
    front_mine = mine
    merged, target, grad, mine, other = back_call(
        here, u2, v2, around, mixed_all, proj, taps, front_target, front_taps, merged, tile, head_size
    )

    mine, other, *first = tie(mine, other, *first)
    after = swap(other, "col", 1)
    total = add_low(mine, after)
    turns = bits[1:2] + bits[:1] + bits[2:]
    back_mine, back_other = projector_call(here, mixed_all, target, after, piece_rows, cols, late)
    front_sum = add_low(front_mine, jnp.concatenate([*first, *halves[1:]]))
    back_sum = add_low(back_mine, swap(back_other, "col", 1))
    total = add_step(total, "row", turns[0])
    total, back_sum = tie(total, back_sum)
    total = add_step(total, "row", turns[1])
    total, front_sum = tie(total, front_sum)
    for bit in turns[2:]:
        total = add_step(total, "row", bit)
    front_sum, leaves = halve(front_sum)
    front_sum = add_low(front_sum, swap(leaves, "col", 1))
    back_sum = scatter_step(back_sum, bits[:2])
    front_sum = scatter_step(front_sum, bits[1:2])
    total, back_sum = tie(total, back_sum)
    for bit in bits[2:-1]:
        front_sum, back_sum = scatter_step(front_sum, [bit]), scatter_step(back_sum, [bit])
    far = swap(total, "col", 1)
    kept, leaves = zip(halve(front_sum), halve(back_sum))
    got = swap(jnp.concatenate(leaves), "row", bits[-1])
    dq, dk, heat, tap_sums = final_call(
        here, sharp, total, far, energy_own, energy_far, attn, gram, scale, q2, k2, head_size
    )
    content = content_call(grad, block, tap_sums)
    content, *kept = tie(content, *kept)
    front_sum, back_sum = (add_low(x, y) for x, y in zip(kept, jnp.split(got, 2)))
    projector = jnp.concatenate([front_sum, back_sum], axis=1)
    full = lambda x: x.reshape(tile + (width,))
    return full(merged), full(dq), full(dk), full(content), heat, tap_sums, projector


def solution(mesh):
    field = P(("scene", "row"), "col", None)
    return jax.shard_map(
        shards,
        mesh=mesh,
        in_specs=(field, field, field, field, P(), P(), P()),
        out_specs=(
            field,
            field,
            field,
            field,
            P("scene"),
            P("scene", None),
            P(("scene", "row", "col"), None),
        ),
        check_vma=False,
    )
```

```python
import functools

import jax
import jax.numpy as jnp
from jax import lax
from jax.experimental import pallas as pl
from jax.experimental.pallas import tpu as pltpu
from jax.sharding import PartitionSpec as P

epsilon = 1e-06
inverse_root = 0.7071067811865476
density_root = 0.3989422804014327
LANES = 128
GROUP = 256
RIM = 8
f32 = jnp.float32
bf16 = jnp.bfloat16
VMEM_LIMIT = 24 * 1024 * 1024


def whole(shape):
    return pl.BlockSpec(shape, lambda *_: (0,) * len(shape))


SCALAR = pl.BlockSpec(memory_space=pltpu.SMEM)
LOCAL = pl.BlockSpec(memory_space=pltpu.VMEM)


def params(limit=VMEM_LIMIT):
    return pltpu.CompilerParams(vmem_limit_bytes=limit)


def cost(microseconds):
    return pl.CostEstimate(flops=0, bytes_accessed=int(microseconds * 3.6e6), transcendentals=0)


def pad_lines(lines, count):
    blank = jnp.zeros((count - len(lines), LANES), f32)
    return jnp.concatenate(lines + [blank], axis=0) if count > len(lines) else jnp.concatenate(lines, axis=0)


def dot_tn(a, b):
    return lax.dot_general(a, b, (((0,), (0,)), ((), ())), preferred_element_type=f32)


def dot_nt(a, b):
    return lax.dot_general(a, b, (((1,), (1,)), ((), ())), preferred_element_type=f32)


def dot_nn(a, b):
    return jnp.dot(a, b, preferred_element_type=f32)


def lane_head(head_size):
    return lax.broadcasted_iota(jnp.int32, (head_size, LANES), 1) // head_size


def by_head(parts, owner):
    out = parts[0]
    for k in range(1, len(parts)):
        out = jnp.where(owner == k, parts[k], out)
    return out


def pack_diagonal(square, head_size):
    owner = lane_head(head_size)
    return by_head(
        [square[k * head_size : (k + 1) * head_size] for k in range(LANES // head_size)], owner
    )


def sum_in_head(values, owner, packed):
    sums = [jnp.sum(jnp.where(owner == k, values, 0.0), axis=1, keepdims=True) for k in range(packed)]
    return by_head([jnp.broadcast_to(s, values.shape) for s in sums], owner)


def edges_kernel(here_ref, v_head, v_tail, u_head, u_tail, twin_ref, next_ref):
    even = lax.rem(here_ref[1], 2) == 0

    def put(tail_ref, head_ref):
        tail_ref[:2] = v_tail[...]
        tail_ref[2:] = u_tail[...]
        head_ref[:2] = v_head[...]
        head_ref[2:] = u_head[...]

    @pl.when(even)
    def _():
        put(twin_ref, next_ref)

    @pl.when(jnp.logical_not(even))
    def _():
        put(next_ref, twin_ref)


def edges_call(here, v, u):
    rows, cols, width = v.shape
    out = jax.ShapeDtypeStruct((3, cols, width), bf16)
    return pl.pallas_call(
        edges_kernel,
        grid=(1,),
        in_specs=[
            SCALAR,
            pl.BlockSpec((2, cols, width), lambda i: (0, 0, 0)),
            pl.BlockSpec((2, cols, width), lambda i: (rows // 2 - 1, 0, 0)),
            pl.BlockSpec((1, cols, width), lambda i: (0, 0, 0)),
            pl.BlockSpec((1, cols, width), lambda i: (rows - 1, 0, 0)),
        ],
        out_specs=[LOCAL, LOCAL],
        out_shape=[out, out],
        compiler_params=params(),
        cost_estimate=cost(1),
        name="edges",
    )(here, v, v, u, u)


def gram_kernel(head_size, col_ref, q_ref, k_ref, mine_ref, other_ref):
    half = pl.program_id(0)
    per = GROUP // LANES
    energy = mine_ref.shape[0] - 16
    values = []
    for g in range(q_ref.shape[1] // GROUP):
        at = pl.ds(g * GROUP, GROUP)
        square = dot_tn(q_ref[:, at], k_ref[:, at])
        for p in range(per):
            cut = slice(p * LANES, (p + 1) * LANES)
            block = g * per + p
            values.append((block * head_size, pack_diagonal(square[cut, cut], head_size)))
            for line, ref in ((energy, q_ref), (energy + 8, k_ref)):
                x = ref[:, pl.ds(block * LANES, LANES)].astype(f32)
                values.append((line + block, jnp.sum(x * x, axis=0, keepdims=True)))

    def put(ref):
        for at, value in values:
            ref[pl.ds(at, value.shape[0]), :] = value

    @pl.when(half == 0)
    def _():
        mine_ref[pl.ds(energy, 16), :] = jnp.zeros((16, LANES), f32)
        other_ref[pl.ds(energy, 16), :] = jnp.zeros((16, LANES), f32)

    @pl.when(half == col_ref[0])
    def _():
        put(mine_ref)

    @pl.when(half != col_ref[0])
    def _():
        put(other_ref)


def gram_call(col, q, k, head_size):
    tokens, width = q.shape
    lines = width // 2 // LANES * head_size + 16
    out = jax.ShapeDtypeStruct((lines, LANES), f32)
    return pl.pallas_call(
        functools.partial(gram_kernel, head_size),
        grid=(2,),
        in_specs=[
            SCALAR,
            pl.BlockSpec((tokens, width // 2), lambda i: (0, i)),
            pl.BlockSpec((tokens, width // 2), lambda i: (0, i)),
        ],
        out_specs=[LOCAL, LOCAL],
        out_shape=[out, out],
        compiler_params=params(60 * 1024 * 1024),
        cost_estimate=cost(2.5),
        name="gram",
    )(col, q, k)


def gelu_terms(u):
    cumul = 0.5 * (1.0 + lax.erf(u * inverse_root))
    return u * cumul, cumul + u * jnp.exp(-0.5 * u * u) * density_root


def attention_block(head_size, raw, q_line, k_line, sharp):
    packed = LANES // head_size
    owner = lane_head(head_size)
    row = lax.broadcasted_iota(jnp.int32, (head_size, LANES), 0)
    lane = lax.broadcasted_iota(jnp.int32, (head_size, LANES), 1)
    q_energy = by_head(
        [
            jnp.broadcast_to(
                jnp.sum(jnp.where(lane == row + k * head_size, q_line, 0.0), axis=1, keepdims=True),
                raw.shape,
            )
            for k in range(packed)
        ],
        owner,
    )
    q_scale = lax.rsqrt(q_energy + epsilon)
    k_scale = lax.rsqrt(k_line + epsilon)
    gram = q_scale * raw * k_scale
    heat = by_head([jnp.full(raw.shape, s, f32) for s in sharp], owner)
    numer = jnp.exp(heat * gram)
    attention = numer / sum_in_head(numer, owner, packed)
    return attention, gram, q_scale * k_scale


def attention_phase(
    head_size, col_ref, sharp_ref, own_ref, far_ref, attn_ref, gram_ref, scale_ref, block_ref
):
    packed = LANES // head_size
    blocks = attn_ref.shape[0] // head_size
    half_blocks = blocks // 2
    is_first = col_ref[0] == 0
    block_ref[...] = jnp.zeros(block_ref.shape, bf16)
    owner = lane_head(head_size)
    for p in range(blocks):
        h, inner = divmod(p, half_blocks)

        def take(at, size):
            a = own_ref[pl.ds(at, size), :]
            b = far_ref[pl.ds(at, size), :]
            return jnp.where(is_first, a, b) if h == 0 else jnp.where(is_first, b, a)

        raw = take(inner * head_size, head_size)
        q_line = take(half_blocks * head_size + inner, 1)
        k_line = take(half_blocks * head_size + 8 + inner, 1)
        attention, gram, scale = attention_block(
            head_size, raw, q_line, k_line, [sharp_ref[p * packed + k] for k in range(packed)]
        )
        at = pl.ds(p * head_size, head_size)
        attn_ref[at, :] = attention
        gram_ref[at, :] = gram
        scale_ref[at, :] = scale
        low = attention.astype(bf16)
        inside = (p * LANES) % GROUP
        for k in range(packed):
            block_ref[pl.ds(p * LANES + k * head_size, head_size), pl.ds(inside, LANES)] = jnp.where(
                owner == k, low, jnp.zeros_like(low)
            )


def keep_side(col_ref, shape):
    place = lax.rem(lax.broadcasted_iota(jnp.int32, shape, 0), RIM)
    second = col_ref[0].astype(f32)
    right = jnp.where(place < 2, 1.0, 0.0)
    left = jnp.where(place >= RIM - 2, 1.0, 0.0)
    return right + second * (left - right)


def stencil_chunk(
    step, tile, col_ref, u_ref, side_ref, twin_ref, next_ref, corner_ref, taps_ref,
    merged_ref, target_ref, tapsum_ref, field_ref, slope_ref, projected_ref, upside_ref,
    first_channel, beside,
):
    tile_rows, tile_cols = tile
    tokens = tile_rows * tile_cols
    ring = tile_cols + RIM
    side = tile_rows * RIM
    chunk = pl.ds(first_channel + step * GROUP, GROUP)
    for at, size, ref, start in (
        (0, side, side_ref, side),
        (side, tile_cols, twin_ref, 2 * tile_cols),
        (side + tile_cols, tile_cols, next_ref, 2 * tile_cols),
        (side + 2 * tile_cols, 2 * RIM, corner_ref, 4 * RIM),
    ):
        piece = ref[pl.ds(start, size), chunk].astype(f32)
        if ref is side_ref or ref is corner_ref:
            piece = piece * keep_side(col_ref, piece.shape)
        upside_ref[pl.ds(at, size), :] = piece

    def lanes_body(part, carry):
        lanes = pl.ds(pl.multiple_of(part * LANES, LANES), LANES)
        glob = pl.ds(pl.multiple_of(first_channel + step * GROUP + part * LANES, LANES), LANES)
        away = pl.ds(pl.multiple_of(step * GROUP + part * LANES, LANES), LANES)
        taps = [taps_ref[pl.ds(t, 1), glob] for t in range(9)]
        rim = tokens + side
        from_next = 1 - lax.rem(col_ref[1], 2)
        beside(part)

        def ring_row(r):
            if 0 <= r < tile_rows:
                pieces = (r * tile_cols, tokens + r * RIM)
            else:
                k = r + 2 if r < 0 else r - tile_rows
                k = k + 2 * (from_next if r < 0 else 1 - from_next)
                pieces = (
                    pl.multiple_of(rim + k * tile_cols, RIM),
                    pl.multiple_of(rim + 4 * tile_cols + k * RIM, RIM),
                )
            return jnp.concatenate(
                [
                    projected_ref[pl.ds(pieces[0], tile_cols), lanes],
                    projected_ref[pl.ds(pieces[1], RIM), lanes],
                ],
                axis=0,
            )

        def up_row(r):
            if 0 <= r < tile_rows:
                return jnp.concatenate(
                    [
                        u_ref[pl.ds(r * tile_cols, tile_cols), glob].astype(f32),
                        upside_ref[pl.ds(r * RIM, RIM), lanes],
                    ],
                    axis=0,
                )
            k = from_next if r < 0 else 1 - from_next
            pieces = (
                pl.multiple_of(side + k * tile_cols, RIM),
                pl.multiple_of(side + 2 * tile_cols + k * RIM, RIM),
            )
            return jnp.concatenate(
                [
                    upside_ref[pl.ds(pieces[0], tile_cols), lanes],
                    upside_ref[pl.ds(pieces[1], RIM), lanes],
                ],
                axis=0,
            )

        for r in range(-2, tile_rows + 2):
            field_ref[r + 2] = ring_row(r).astype(bf16).astype(f32)
        for r in range(-1, tile_rows + 1):
            near = [field_ref[r + 1 + a] for a in range(3)]
            sums = [sum(taps[3 * a + b] * near[a] for a in range(3)) for b in range(3)]
            total = pltpu.roll(sums[0], 1, 0) + sums[1] + pltpu.roll(sums[2], ring - 1, 0)
            active, slope = gelu_terms(total)
            slope_ref[r + 1] = (up_row(r) * slope).astype(bf16).astype(f32)
            if 0 <= r < tile_rows:
                at = pl.ds(r * tile_cols, tile_cols)
                merged_ref[at, away] = (projected_ref[at, lanes] + active[:tile_cols]).astype(bf16)
        weights = [jnp.zeros((8, LANES), f32) for _ in range(9)]
        blank = jnp.zeros((RIM, LANES), f32)
        for r in range(tile_rows):
            near = [slope_ref[r + 2 - a] for a in range(3)]
            sums = [sum(taps[3 * a + b] * near[a] for a in range(3)) for b in range(3)]
            back = pltpu.roll(sums[0], ring - 1, 0) + sums[1] + pltpu.roll(sums[2], 1, 0)
            at = pl.ds(r * tile_cols, tile_cols)
            target_ref[at, away] = (u_ref[at, glob].astype(f32) + back[:tile_cols]).astype(bf16)
            centre = jnp.concatenate([near[1][:tile_cols], blank], axis=0)
            shifted = [pltpu.roll(centre, ring - 1, 0), centre, pltpu.roll(centre, 1, 0)]
            for a in range(3):
                line = field_ref[r + 1 + a]
                for b in range(3):
                    product = shifted[b] * line
                    weights[3 * a + b] = weights[3 * a + b] + jnp.sum(
                        product.reshape(ring // 8, 8, LANES), axis=0
                    )
        for t in range(9):
            tapsum_ref[pl.ds(t, 1), away] = jnp.sum(weights[t], axis=0, keepdims=True)
        return carry

    lax.fori_loop(0, GROUP // LANES, lanes_body, 0)


def spread_product(piece_rows, cols, order, here_ref, mixed_all, target_ref, mine_ref, other_ref):
    tokens = target_ref.shape[0]
    axis, bit = order[0]
    apart = bit if axis == "col" else bit * cols
    index = {"col": here_ref[0], "row": here_ref[1]}
    flipped = (index[axis] // bit) % 2 == 1
    per = GROUP // piece_rows
    for g in range(mixed_all.shape[1] // GROUP):
        product = dot_tn(mixed_all[pl.ds(0, tokens), pl.ds(g * GROUP, GROUP)], target_ref[...])
        for k in range(per):
            if k & apart:
                continue
            owner = g * per + k
            a, b = (product[x * piece_rows : (x + 1) * piece_rows] for x in (k, k | apart))
            away = {"col": (owner % cols) ^ index["col"], "row": (owner // cols) ^ index["row"]}
            place = 0
            for name, digit in order[1:]:
                place = 2 * place + (away[name] // digit) % 2
            at = pl.ds(pl.multiple_of(place * piece_rows, piece_rows), piece_rows)
            mine_ref[at, :] = jnp.where(flipped, b, a)
            other_ref[at, :] = jnp.where(flipped, a, b).astype(bf16)


def front_kernel(
    head_size, tile, piece_rows, cols, order,
    col_ref, sharp_ref, own_ref, far_ref, v_ref, u_ref, side_ref, twin_ref, next_ref,
    corner_ref, proj_ref, taps_ref,
    merged_ref, attn_ref, gram_ref, scale_ref, block_ref, mixed_all, target_ref, tapsum_ref,
    mine_ref, other_ref, carry_ref,
    field_ref, slope_ref, upside_ref, *projected,
):
    tile_rows, tile_cols = tile
    tokens, width = v_ref.shape
    side = tile_rows * RIM
    two = 2 * tile_cols

    tapsum_ref[...] = jnp.zeros(tapsum_ref.shape, f32)
    attention_phase(
        head_size, col_ref, sharp_ref, own_ref, far_ref, attn_ref, gram_ref, scale_ref, block_ref
    )
    for g in range(width // GROUP):
        at = pl.ds(g * GROUP, GROUP)
        weights = block_ref[at, :]
        mixed_all[pl.ds(0, tokens), at] = dot_nt(v_ref[:, at], weights).astype(bf16)
        around = [(side_ref, side), (twin_ref, two), (next_ref, two), (corner_ref, 4 * RIM)]
        value = dot_nt(
            jnp.concatenate([ref[pl.ds(0, size), at] for ref, size in around], axis=0), weights
        )
        start = 0
        for ref, size in around:
            piece = value[start : start + size]
            if ref is side_ref or ref is corner_ref:
                piece = piece * keep_side(col_ref, piece.shape)
            mixed_all[pl.ds(tokens + start, size), at] = piece.astype(bf16)
            start += size

    steps = target_ref.shape[1] // GROUP
    projected[0][...] = dot_nn(mixed_all[...], proj_ref[:, pl.ds(0, GROUP)])
    for step in range(steps):
        into = carry_ref if step == steps - 1 else projected[(step + 1) % 2]
        stencil_chunk(
            step, tile, col_ref, u_ref, side_ref, twin_ref, next_ref, corner_ref, taps_ref,
            merged_ref, target_ref, tapsum_ref, field_ref, slope_ref, projected[step % 2], upside_ref, 0,
            functools.partial(project_part, mixed_all, proj_ref, into, (step + 1) * GROUP),
        )
    spread_product(piece_rows, cols, order, col_ref, mixed_all, target_ref, mine_ref, other_ref)


def project_part(mixed_all, proj_ref, into_ref, channel, part):
    rows = mixed_all.shape[0] // (GROUP // LANES)
    at = pl.ds(pl.multiple_of(part * rows, 16), rows)
    into_ref[at, :] = dot_nn(mixed_all[at, :], proj_ref[:, pl.ds(channel, GROUP)])


def back_kernel(
    head_size, tile, first_channel,
    col_ref, u_ref, v_ref, side_ref, twin_ref, next_ref, corner_ref, mixed_all, proj_ref, taps_ref,
    front_target, front_taps, carry_ref,
    merged_ref, target_ref, grad_ref, mine_ref, other_ref,
    field_ref, slope_ref, upside_ref, projected_a, projected_b, tapsum_ref, partial_ref,
):
    tokens, width = v_ref.shape
    blocks = width // LANES
    half_blocks = blocks // 2
    span = width - first_channel
    tapsum_ref[...] = jnp.zeros(tapsum_ref.shape, f32)

    def grad_part(part):
        rows = width // (GROUP // LANES)
        at = pl.ds(pl.multiple_of(part * rows, LANES), rows)
        partial_ref[:, at] = dot_nt(front_target[...], proj_ref[at, pl.ds(0, first_channel)])

    steps = span // GROUP
    source = carry_ref
    for step in range(steps):
        into = (projected_a, projected_b)[step % 2]
        if step == steps - 1:
            beside = grad_part
        else:
            beside = functools.partial(
                project_part, mixed_all, proj_ref, into, first_channel + (step + 1) * GROUP
            )
        stencil_chunk(
            step, tile, col_ref, u_ref, side_ref, twin_ref, next_ref, corner_ref, taps_ref,
            merged_ref, target_ref, tapsum_ref, field_ref, slope_ref, source, upside_ref, first_channel, beside,
        )
        source = into
    grad_ref[...] = (
        partial_ref[...] + dot_nt(target_ref[...], proj_ref[:, pl.ds(first_channel, span)])
    ).astype(bf16)
    for g in range(width // GROUP):
        at = pl.ds(g * GROUP, GROUP)
        square = dot_tn(grad_ref[:, at], v_ref[:, at])
        for p in range(GROUP // LANES):
            cut = slice(p * LANES, (p + 1) * LANES)
            block = g * (GROUP // LANES) + p
            h, inner = divmod(block, half_blocks)
            packed_rows = pack_diagonal(square[cut, cut], head_size)
            if block * LANES < first_channel:
                tap_rows = front_taps[:, pl.ds(block * LANES, LANES)]
            else:
                tap_rows = tapsum_ref[:, pl.ds(block * LANES - first_channel, LANES)]

            def put(ref, inner=inner, packed_rows=packed_rows, tap_rows=tap_rows):
                ref[pl.ds(inner * head_size, head_size), :] = packed_rows.astype(ref.dtype)
                ref[pl.ds(half_blocks * head_size + inner * 16, 16), :] = tap_rows.astype(ref.dtype)

            @pl.when(col_ref[0] == h)
            def _():
                put(mine_ref)

            @pl.when(col_ref[0] != h)
            def _():
                put(other_ref)


def stencil_scratch(tile):
    ring = tile[1] + RIM
    return [
        pltpu.VMEM((tile[0] + 4, ring, LANES), f32),
        pltpu.VMEM((tile[0] + 2, ring, LANES), f32),
        pltpu.VMEM(((tile[0] + 2) * ring, GROUP), f32),
        pltpu.VMEM(((tile[0] + 4) * ring, GROUP), f32),
        pltpu.VMEM(((tile[0] + 4) * ring, GROUP), f32),
    ]


def front_call(col, sharp, own, far, v, u, halo, proj, taps, tile, head_size, piece_rows, cols, order):
    tokens, width = v.shape
    ring = tile[1] + RIM
    span = width // 2
    grams = width // LANES * head_size
    sds = jax.ShapeDtypeStruct
    outs = [
        sds((tokens, span), bf16),
        sds((grams, LANES), f32),
        sds((grams, LANES), f32),
        sds((grams, LANES), f32),
        sds((width, GROUP), bf16),
        sds(((tile[0] + 4) * ring, width), bf16),
        sds((tokens, span), bf16),
        sds((16, span), f32),
        sds((width // 2, span), f32),
        sds((width // 2, span), bf16),
        sds(((tile[0] + 4) * ring, GROUP), f32),
    ]
    args = (col, sharp, own, far, v, u, *halo, proj, taps)
    return pl.pallas_call(
        functools.partial(front_kernel, head_size, tile, piece_rows, cols, order),
        in_specs=[SCALAR] * 2 + [LOCAL] * (len(args) - 2),
        out_specs=[LOCAL] * len(outs),
        out_shape=outs,
        scratch_shapes=stencil_scratch(tile),
        compiler_params=params(),
        cost_estimate=cost(10),
        name="front",
    )(*args)


def back_call(col, u, v, halo, mixed_all, proj, taps, target, tapsum, carry, tile, head_size):
    tokens, width = v.shape
    span = width // 2
    lines = width // LANES // 2 * (head_size + 16)
    sds = jax.ShapeDtypeStruct
    outs = [
        sds((tokens, span), bf16),
        sds((tokens, span), bf16),
        sds((tokens, width), bf16),
        sds((lines, LANES), f32),
        sds((lines, LANES), bf16),
    ]
    args = (col, u, v, *halo, mixed_all, proj, taps, target, tapsum, carry)
    return pl.pallas_call(
        functools.partial(back_kernel, head_size, tile, span),
        in_specs=[SCALAR] + [LOCAL] * (len(args) - 1),
        out_specs=[LOCAL] * len(outs),
        out_shape=outs,
        scratch_shapes=stencil_scratch(tile)
        + [pltpu.VMEM((16, span), f32), pltpu.VMEM((tokens, width), f32)],
        compiler_params=params(),
        cost_estimate=cost(10),
        name="back",
    )(*args)


def projector_kernel(
    piece_rows, cols, order, here_ref, mixed_all, target_ref, after_ref, mine_ref, other_ref
):
    spread_product(piece_rows, cols, order, here_ref, mixed_all, target_ref, mine_ref, other_ref)


def projector_call(here, mixed_all, target, after, piece_rows, cols, order):
    width, span = mixed_all.shape[1], target.shape[1]
    sds = jax.ShapeDtypeStruct
    return pl.pallas_call(
        functools.partial(projector_kernel, piece_rows, cols, order),
        in_specs=[SCALAR, LOCAL, LOCAL, pl.BlockSpec(memory_space=pl.ANY)],
        out_specs=[LOCAL, LOCAL],
        out_shape=[sds((width // 2, span), f32), sds((width // 2, span), bf16)],
        compiler_params=params(),
        cost_estimate=cost(2),
        name="projector",
    )(here, mixed_all, target, after)


def content_kernel(grad_ref, block_ref, merged_front, merged_back, after_ref, out_ref, merged_ref):
    span = out_ref.shape[1]
    for g in range(span // GROUP):
        at = pl.ds(pl.multiple_of(pl.program_id(0) * span + g * GROUP, GROUP), GROUP)
        out_ref[:, pl.ds(g * GROUP, GROUP)] = dot_nn(grad_ref[:, at], block_ref[at, :]).astype(bf16)

    @pl.when(pl.program_id(0) == 0)
    def _():
        merged_ref[...] = merged_front[...]

    @pl.when(pl.program_id(0) != 0)
    def _():
        merged_ref[...] = merged_back[...]


def content_call(grad, block, merged_front, merged_back, after):
    tokens, width = grad.shape
    half = pl.BlockSpec((tokens, width // 2), lambda i: (0, i))
    out = jax.ShapeDtypeStruct((tokens, width), bf16)
    return pl.pallas_call(
        content_kernel,
        grid=(2,),
        in_specs=[LOCAL] * 4 + [pl.BlockSpec(memory_space=pl.ANY)],
        out_specs=[half, half],
        out_shape=[out, out],
        compiler_params=params(),
        cost_estimate=cost(2),
        name="content",
    )(grad, block, merged_front, merged_back, after)


def final_kernel(
    head_size,
    col_ref,
    sharp_ref,
    own_ref,
    far_ref,
    energy_own_ref,
    energy_far_ref,
    attn_ref,
    gram_ref,
    scale_ref,
    q_ref,
    k_ref,
    dq_ref,
    dk_ref,
    heat_ref,
    taps_ref,
    mixer_ref,
):
    half = pl.program_id(0)
    groups = dq_ref.shape[1] // GROUP
    packed = LANES // head_size
    per = GROUP // LANES
    half_blocks = groups * per
    mine = half == col_ref[0]
    owner = lane_head(head_size)
    row = lax.broadcasted_iota(jnp.int32, (head_size, LANES), 0)
    lane = lax.broadcasted_iota(jnp.int32, (head_size, LANES), 1)
    mixer_ref[...] = jnp.zeros(mixer_ref.shape, bf16)
    q_terms, k_terms = [], []

    def take(own, far, at, size):
        return jnp.where(mine, own[pl.ds(at, size), :], far[pl.ds(at, size), :])

    for inner in range(half_blocks):
        block = half * half_blocks + inner
        p = inner % per
        grad = take(own_ref, far_ref, inner * head_size, head_size)
        taps_ref[:, pl.ds(inner * LANES, LANES)] = take(
            own_ref, far_ref, half_blocks * head_size + inner * 16, 16
        )[:9]
        q_line = take(energy_own_ref, energy_far_ref, half_blocks * head_size + inner, 1)
        k_line = take(energy_own_ref, energy_far_ref, half_blocks * head_size + 8 + inner, 1)
        at = pl.ds(pl.multiple_of(block * head_size, head_size), head_size)
        attention, gram, scale = attn_ref[at, :], gram_ref[at, :], scale_ref[at, :]
        scores = attention * (grad - sum_in_head(attention * grad, owner, packed))
        heated = scores * gram
        heat = by_head(
            [jnp.full(scores.shape, sharp_ref[block * packed + k], f32) for k in range(packed)], owner
        )
        for k in range(packed):
            heat_ref[block * packed + k] = jnp.sum(jnp.where(owner == k, heated, 0.0))
        gram_grad = heat * scores
        corr = gram_grad * gram
        k_corr = jnp.sum(corr, axis=0, keepdims=True)
        columns = sum_in_head(corr, owner, packed)
        q_corr = jnp.sum(jnp.where(lane == row + owner * head_size, columns, 0.0), axis=0, keepdims=True)
        q_scale = lax.rsqrt(q_line + epsilon)
        k_scale = lax.rsqrt(k_line + epsilon)
        q_terms.append(q_scale * q_scale * q_corr)
        k_terms.append(k_scale * k_scale * k_corr)
        low = (scale * gram_grad).astype(bf16)
        for k in range(packed):
            mixer_ref[pl.ds(inner * LANES + k * head_size, head_size), pl.ds(p * LANES, LANES)] = jnp.where(
                owner == k, low, jnp.zeros_like(low)
            )
    for g in range(groups):
        here = pl.ds(pl.multiple_of((half * groups + g) * GROUP, GROUP), GROUP)
        at = pl.ds(g * GROUP, GROUP)
        q, k = q_ref[:, here], k_ref[:, here]
        mixer = mixer_ref[at, :]
        q_term = jnp.concatenate(q_terms[g * per : (g + 1) * per], axis=1)
        k_term = jnp.concatenate(k_terms[g * per : (g + 1) * per], axis=1)
        dq_ref[:, at] = (dot_nt(k, mixer) - q.astype(f32) * q_term).astype(bf16)
        dk_ref[:, at] = (dot_nn(q, mixer) - k.astype(f32) * k_term).astype(bf16)


def final_call(col, sharp, own, far, energy_own, energy_far, attn, gram, scale, q, k, head_size):
    tokens, width = q.shape
    sds = jax.ShapeDtypeStruct
    token_block = pl.BlockSpec((tokens, width // 2), lambda i: (0, i))
    args = (col, sharp, own, far, energy_own, energy_far, attn, gram, scale, q, k)
    return pl.pallas_call(
        functools.partial(final_kernel, head_size),
        grid=(2,),
        in_specs=[SCALAR, SCALAR] + [LOCAL] * 9,
        out_specs=[
            token_block,
            token_block,
            SCALAR,
            pl.BlockSpec((9, width // 2), lambda i: (0, i)),
        ],
        out_shape=[
            sds((tokens, width), bf16),
            sds((tokens, width), bf16),
            sds(sharp.shape, f32),
            sds((9, width), f32),
        ],
        scratch_shapes=[pltpu.VMEM((width // 2, GROUP), bf16)],
        compiler_params=params(),
        cost_estimate=cost(5),
        name="final",
    )(*args)


def swap(x, axis, bit):
    return lax.ppermute(x, axis, [(i, i ^ bit) for i in range(lax.axis_size(axis))])


def row_bits():
    bits, bit = [], 1
    while bit < lax.axis_size("row"):
        bits.append(bit)
        bit *= 2
    return bits


def halve(total):
    half = total.shape[0] // 2
    return total[:half], total[half:].astype(bf16)


def add_low(total, got):
    return total + got.astype(f32)


def add_step(total, axis, bit):
    low = total.astype(bf16)
    return low.astype(f32) + swap(low, axis, bit).astype(f32)


def scatter_step(total, group):
    count = 2 ** len(group)
    rows = total.shape[0] // count
    out = total[:rows]
    for k in range(1, count):
        mask = sum(bit for i, bit in enumerate(group) if (k >> (len(group) - 1 - i)) & 1)
        out = add_low(out, swap(total[k * rows : (k + 1) * rows].astype(bf16), "row", mask))
    return out


def scatter_both(first, second, group):
    early, late = group
    quarter, half = first.shape[0] // 4, second.shape[0] // 2
    pieces = [first[k * quarter : (k + 1) * quarter] for k in range(4)]
    joint = swap(jnp.concatenate([pieces[1], second[half:]]).astype(bf16), "row", late)
    first = add_low(pieces[0], swap(pieces[2].astype(bf16), "row", early))
    first = add_low(first, swap(pieces[3].astype(bf16), "row", early | late))
    return add_low(first, joint[:quarter]), add_low(second[:half], joint[quarter:])


def tie(*values):
    return lax.optimization_barrier(values)


def shards(q, k, v, u, sharp, proj, taps):
    tile = v.shape[:2]
    width = v.shape[2]
    tokens = tile[0] * tile[1]
    head_size = width // sharp.shape[0]
    rows, cols = lax.axis_size("row"), lax.axis_size("col")
    flat = lambda x: x.reshape(tokens, width)
    here = jnp.stack([lax.axis_index("col"), lax.axis_index("row")]).astype(jnp.int32)
    q2, k2, v2, u2 = flat(q), flat(k), flat(v), flat(u)
    bits = row_bits()
    early = [("row", bits[0]), ("col", 1)] + [("row", bit) for bit in bits[1:]]
    late = [("col", 1)] + [("row", bit) for bit in bits]
    piece_rows = width // (rows * cols)

    mine, other = gram_call(here, q2, k2, head_size)
    to_twin, to_next = edges_call(here, v, u)
    total = add_low(mine, swap(other, "col", 1))
    start = jnp.where(lax.axis_index("col") == 0, v.shape[1] - RIM, 0)
    edge = lambda x: lax.dynamic_slice_in_dim(x, start, RIM, axis=1)
    pairs_next = [(j, j + 1) for j in range(1, rows - 1, 2)]
    pairs_next = pairs_next + [(b, a) for a, b in pairs_next]
    side = swap(jnp.concatenate([edge(v), edge(u)]), "col", 1)
    for i, bit in enumerate(bits):
        total = total + swap(total, "row", bit)
        if i == 2:
            from_twin = swap(to_twin, "row", 1)
            total, from_twin = tie(total, from_twin)
        if i == 2:
            from_next = lax.ppermute(to_next, "row", pairs_next)
            total, from_next = tie(total, from_next)
    corner = swap(
        edge(jnp.concatenate([from_twin[:2], from_next[:2], from_twin[2:], from_next[2:]])), "col", 1
    )
    around = tuple(x.reshape(-1, width) for x in (side, from_twin, from_next, corner))
    energy_own, energy_far = total, swap(total, "col", 1)

    (merged_front, attn, gram, scale, block, mixed_all, front_target, front_taps, mine, other, carry) = front_call(
        here, sharp, energy_own, energy_far, v2, u2, around, proj, taps, tile, head_size, piece_rows, cols, early
    )
    halves = [swap(x, "row", bits[0]) for x in jnp.split(other, 2)]
    first = halves[:1]
    front_mine = mine
    merged_back, target, grad, mine, other = back_call(
        here, u2, v2, around, mixed_all, proj, taps, front_target, front_taps, carry, tile, head_size
    )

    mine, other, *first = tie(mine, other, *first)
    after = swap(other, "col", 1)
    total = add_low(mine, after)
    turns = bits[1:2] + bits[:1] + bits[2:]
    back_mine, back_other = projector_call(here, mixed_all, target, after, piece_rows, cols, late)
    front_sum = add_low(front_mine, jnp.concatenate([*first, *halves[1:]]))
    back_sum = add_low(back_mine, swap(back_other, "col", 1))
    total = add_step(total, "row", turns[0])
    total, back_sum = tie(total, back_sum)
    total = add_step(total, "row", turns[1])
    total, front_sum = tie(total, front_sum)
    for bit in turns[2:]:
        total = add_step(total, "row", bit)
    front_sum, leaves = halve(front_sum)
    front_sum = add_low(front_sum, swap(leaves, "col", 1))
    back_sum = scatter_step(back_sum, bits[:2])
    front_sum = scatter_step(front_sum, bits[1:2])
    total, back_sum = tie(total, back_sum)
    for bit in bits[2:-1]:
        front_sum, back_sum = scatter_step(front_sum, [bit]), scatter_step(back_sum, [bit])
    far = swap(total, "col", 1)
    kept, leaves = zip(halve(front_sum), halve(back_sum))
    got = swap(jnp.concatenate(leaves), "row", bits[-1])
    dq, dk, heat, tap_sums = final_call(
        here, sharp, total, far, energy_own, energy_far, attn, gram, scale, q2, k2, head_size
    )
    content, merged = content_call(grad, block, merged_front, merged_back, tap_sums)
    content, *kept = tie(content, *kept)
    front_sum, back_sum = (add_low(x, y) for x, y in zip(kept, jnp.split(got, 2)))
    projector = jnp.concatenate([front_sum, back_sum], axis=1)
    full = lambda x: x.reshape(tile + (width,))
    return full(merged), full(dq), full(dk), full(content), heat, tap_sums, projector


def solution(mesh):
    field = P(("scene", "row"), "col", None)
    return jax.shard_map(
        shards,
        mesh=mesh,
        in_specs=(field, field, field, field, P(), P(), P()),
        out_specs=(
            field,
            field,
            field,
            field,
            P("scene"),
            P("scene", None),
            P(("scene", "row", "col"), None),
        ),
        check_vma=False,
    )
```

```python
import functools

import jax
import jax.numpy as jnp
from jax import lax
from jax.experimental import pallas as pl
from jax.experimental.pallas import tpu as pltpu
from jax.sharding import PartitionSpec as P

epsilon = 1e-06
inverse_root = 0.7071067811865476
density_root = 0.3989422804014327
LANES = 128
GROUP = 256
RIM = 8
f32 = jnp.float32
bf16 = jnp.bfloat16
VMEM_LIMIT = 24 * 1024 * 1024


def whole(shape):
    return pl.BlockSpec(shape, lambda *_: (0,) * len(shape))


SCALAR = pl.BlockSpec(memory_space=pltpu.SMEM)
LOCAL = pl.BlockSpec(memory_space=pltpu.VMEM)


def params(limit=VMEM_LIMIT):
    return pltpu.CompilerParams(vmem_limit_bytes=limit)


def cost(microseconds):
    return pl.CostEstimate(flops=0, bytes_accessed=int(microseconds * 3.6e6), transcendentals=0)


def pad_lines(lines, count):
    blank = jnp.zeros((count - len(lines), LANES), f32)
    return jnp.concatenate(lines + [blank], axis=0) if count > len(lines) else jnp.concatenate(lines, axis=0)


def dot_tn(a, b):
    return lax.dot_general(a, b, (((0,), (0,)), ((), ())), preferred_element_type=f32)


def dot_nt(a, b):
    return lax.dot_general(a, b, (((1,), (1,)), ((), ())), preferred_element_type=f32)


def dot_nn(a, b):
    return jnp.dot(a, b, preferred_element_type=f32)


def lane_head(head_size):
    return lax.broadcasted_iota(jnp.int32, (head_size, LANES), 1) // head_size


def by_head(parts, owner):
    out = parts[0]
    for k in range(1, len(parts)):
        out = jnp.where(owner == k, parts[k], out)
    return out


def pack_diagonal(square, head_size):
    owner = lane_head(head_size)
    return by_head(
        [square[k * head_size : (k + 1) * head_size] for k in range(LANES // head_size)], owner
    )


def sum_in_head(values, owner, packed):
    sums = [jnp.sum(jnp.where(owner == k, values, 0.0), axis=1, keepdims=True) for k in range(packed)]
    return by_head([jnp.broadcast_to(s, values.shape) for s in sums], owner)


def edges_kernel(here_ref, v_head, v_tail, u_head, u_tail, twin_ref, next_ref):
    even = lax.rem(here_ref[1], 2) == 0

    def put(tail_ref, head_ref):
        tail_ref[:2] = v_tail[...]
        tail_ref[2:] = u_tail[...]
        head_ref[:2] = v_head[...]
        head_ref[2:] = u_head[...]

    @pl.when(even)
    def _():
        put(twin_ref, next_ref)

    @pl.when(jnp.logical_not(even))
    def _():
        put(next_ref, twin_ref)


def edges_call(here, v, u):
    rows, cols, width = v.shape
    out = jax.ShapeDtypeStruct((3, cols, width), bf16)
    return pl.pallas_call(
        edges_kernel,
        grid=(1,),
        in_specs=[
            SCALAR,
            pl.BlockSpec((2, cols, width), lambda i: (0, 0, 0)),
            pl.BlockSpec((2, cols, width), lambda i: (rows // 2 - 1, 0, 0)),
            pl.BlockSpec((1, cols, width), lambda i: (0, 0, 0)),
            pl.BlockSpec((1, cols, width), lambda i: (rows - 1, 0, 0)),
        ],
        out_specs=[LOCAL, LOCAL],
        out_shape=[out, out],
        compiler_params=params(),
        cost_estimate=cost(1),
        name="edges",
    )(here, v, v, u, u)


def gram_kernel(head_size, q_ref, k_ref, mine_ref, other_ref):
    half = pl.program_id(0)
    per = GROUP // LANES
    energy = mine_ref.shape[0] - 16
    values = []
    for g in range(q_ref.shape[1] // GROUP):
        at = pl.ds(g * GROUP, GROUP)
        square = dot_tn(q_ref[:, at], k_ref[:, at])
        for p in range(per):
            cut = slice(p * LANES, (p + 1) * LANES)
            block = g * per + p
            values.append((block * head_size, pack_diagonal(square[cut, cut], head_size)))
            for line, ref in ((energy, q_ref), (energy + 8, k_ref)):
                x = ref[:, pl.ds(block * LANES, LANES)].astype(f32)
                values.append((line + block, jnp.sum(x * x, axis=0, keepdims=True)))

    def put(ref):
        for at, value in values:
            ref[pl.ds(at, value.shape[0]), :] = value

    @pl.when(half == 0)
    def _():
        mine_ref[pl.ds(energy, 16), :] = jnp.zeros((16, LANES), f32)
        other_ref[pl.ds(energy, 16), :] = jnp.zeros((16, LANES), f32)

    col = lax.axis_index("col")

    @pl.when(half == col)
    def _():
        put(mine_ref)

    @pl.when(half != col)
    def _():
        put(other_ref)


def gram_call(q, k, head_size):
    tokens, width = q.shape
    lines = width // 2 // LANES * head_size + 16
    out = jax.ShapeDtypeStruct((lines, LANES), f32)
    return pl.pallas_call(
        functools.partial(gram_kernel, head_size),
        grid=(2,),
        in_specs=[
            pl.BlockSpec((tokens, width // 2), lambda i: (0, i)),
            pl.BlockSpec((tokens, width // 2), lambda i: (0, i)),
        ],
        out_specs=[LOCAL, LOCAL],
        out_shape=[out, out],
        compiler_params=params(48 * 1024 * 1024),
        cost_estimate=cost(2.5),
        name="gram",
    )(q, k)


def gelu_terms(u):
    cumul = 0.5 * (1.0 + lax.erf(u * inverse_root))
    return u * cumul, cumul + u * jnp.exp(-0.5 * u * u) * density_root


def attention_block(head_size, raw, q_line, k_line, sharp):
    packed = LANES // head_size
    owner = lane_head(head_size)
    row = lax.broadcasted_iota(jnp.int32, (head_size, LANES), 0)
    lane = lax.broadcasted_iota(jnp.int32, (head_size, LANES), 1)
    q_energy = by_head(
        [
            jnp.broadcast_to(
                jnp.sum(jnp.where(lane == row + k * head_size, q_line, 0.0), axis=1, keepdims=True),
                raw.shape,
            )
            for k in range(packed)
        ],
        owner,
    )
    q_scale = lax.rsqrt(q_energy + epsilon)
    k_scale = lax.rsqrt(k_line + epsilon)
    gram = q_scale * raw * k_scale
    heat = by_head([jnp.full(raw.shape, s, f32) for s in sharp], owner)
    numer = jnp.exp(heat * gram)
    attention = numer / sum_in_head(numer, owner, packed)
    return attention, gram, q_scale * k_scale


def attention_phase(
    head_size, col_ref, sharp_ref, own_ref, far_ref, attn_ref, gram_ref, scale_ref, block_ref
):
    packed = LANES // head_size
    blocks = attn_ref.shape[0] // head_size
    half_blocks = blocks // 2
    is_first = col_ref[0] == 0
    block_ref[...] = jnp.zeros(block_ref.shape, bf16)
    owner = lane_head(head_size)
    for p in range(blocks):
        h, inner = divmod(p, half_blocks)

        def take(at, size):
            a = own_ref[pl.ds(at, size), :]
            b = far_ref[pl.ds(at, size), :]
            return jnp.where(is_first, a, b) if h == 0 else jnp.where(is_first, b, a)

        raw = take(inner * head_size, head_size)
        q_line = take(half_blocks * head_size + inner, 1)
        k_line = take(half_blocks * head_size + 8 + inner, 1)
        attention, gram, scale = attention_block(
            head_size, raw, q_line, k_line, [sharp_ref[p * packed + k] for k in range(packed)]
        )
        at = pl.ds(p * head_size, head_size)
        attn_ref[at, :] = attention
        gram_ref[at, :] = gram
        scale_ref[at, :] = scale
        low = attention.astype(bf16)
        inside = (p * LANES) % GROUP
        for k in range(packed):
            block_ref[pl.ds(p * LANES + k * head_size, head_size), pl.ds(inside, LANES)] = jnp.where(
                owner == k, low, jnp.zeros_like(low)
            )


def keep_side(col_ref, shape):
    place = lax.rem(lax.broadcasted_iota(jnp.int32, shape, 0), RIM)
    second = col_ref[0].astype(f32)
    right = jnp.where(place < 2, 1.0, 0.0)
    left = jnp.where(place >= RIM - 2, 1.0, 0.0)
    return right + second * (left - right)


def stencil_chunk(
    step, tile, col_ref, u_ref, side_ref, twin_ref, next_ref, corner_ref, taps_ref,
    merged_ref, target_ref, tapsum_ref, field_ref, slope_ref, projected_ref, upside_ref,
    first_channel, beside,
):
    tile_rows, tile_cols = tile
    tokens = tile_rows * tile_cols
    ring = tile_cols + RIM
    side = tile_rows * RIM
    chunk = pl.ds(first_channel + step * GROUP, GROUP)
    for at, size, ref, start in (
        (0, side, side_ref, side),
        (side, tile_cols, twin_ref, 2 * tile_cols),
        (side + tile_cols, tile_cols, next_ref, 2 * tile_cols),
        (side + 2 * tile_cols, 2 * RIM, corner_ref, 4 * RIM),
    ):
        piece = ref[pl.ds(start, size), chunk].astype(f32)
        if ref is side_ref or ref is corner_ref:
            piece = piece * keep_side(col_ref, piece.shape)
        upside_ref[pl.ds(at, size), :] = piece

    def lanes_body(part, carry):
        lanes = pl.ds(pl.multiple_of(part * LANES, LANES), LANES)
        glob = pl.ds(pl.multiple_of(first_channel + step * GROUP + part * LANES, LANES), LANES)
        away = pl.ds(pl.multiple_of(step * GROUP + part * LANES, LANES), LANES)
        taps = [taps_ref[pl.ds(t, 1), glob] for t in range(9)]
        rim = tokens + side
        from_next = 1 - lax.rem(col_ref[1], 2)
        beside(part)

        def ring_row(r):
            if 0 <= r < tile_rows:
                pieces = (r * tile_cols, tokens + r * RIM)
            else:
                k = r + 2 if r < 0 else r - tile_rows
                k = k + 2 * (from_next if r < 0 else 1 - from_next)
                pieces = (
                    pl.multiple_of(rim + k * tile_cols, RIM),
                    pl.multiple_of(rim + 4 * tile_cols + k * RIM, RIM),
                )
            return jnp.concatenate(
                [
                    projected_ref[pl.ds(pieces[0], tile_cols), lanes],
                    projected_ref[pl.ds(pieces[1], RIM), lanes],
                ],
                axis=0,
            )

        def up_row(r):
            if 0 <= r < tile_rows:
                return jnp.concatenate(
                    [
                        u_ref[pl.ds(r * tile_cols, tile_cols), glob].astype(f32),
                        upside_ref[pl.ds(r * RIM, RIM), lanes],
                    ],
                    axis=0,
                )
            k = from_next if r < 0 else 1 - from_next
            pieces = (
                pl.multiple_of(side + k * tile_cols, RIM),
                pl.multiple_of(side + 2 * tile_cols + k * RIM, RIM),
            )
            return jnp.concatenate(
                [
                    upside_ref[pl.ds(pieces[0], tile_cols), lanes],
                    upside_ref[pl.ds(pieces[1], RIM), lanes],
                ],
                axis=0,
            )

        for r in range(-2, tile_rows + 2):
            field_ref[r + 2] = ring_row(r).astype(bf16).astype(f32)
        for r in range(-1, tile_rows + 1):
            near = [field_ref[r + 1 + a] for a in range(3)]
            sums = [sum(taps[3 * a + b] * near[a] for a in range(3)) for b in range(3)]
            total = pltpu.roll(sums[0], 1, 0) + sums[1] + pltpu.roll(sums[2], ring - 1, 0)
            active, slope = gelu_terms(total)
            slope_ref[r + 1] = (up_row(r) * slope).astype(bf16).astype(f32)
            if 0 <= r < tile_rows:
                at = pl.ds(r * tile_cols, tile_cols)
                merged_ref[at, away] = (projected_ref[at, lanes] + active[:tile_cols]).astype(bf16)
        weights = [jnp.zeros((8, LANES), f32) for _ in range(9)]
        blank = jnp.zeros((RIM, LANES), f32)
        for r in range(tile_rows):
            near = [slope_ref[r + 2 - a] for a in range(3)]
            sums = [sum(taps[3 * a + b] * near[a] for a in range(3)) for b in range(3)]
            back = pltpu.roll(sums[0], ring - 1, 0) + sums[1] + pltpu.roll(sums[2], 1, 0)
            at = pl.ds(r * tile_cols, tile_cols)
            target_ref[at, away] = (u_ref[at, glob].astype(f32) + back[:tile_cols]).astype(bf16)
            centre = jnp.concatenate([near[1][:tile_cols], blank], axis=0)
            shifted = [pltpu.roll(centre, ring - 1, 0), centre, pltpu.roll(centre, 1, 0)]
            for a in range(3):
                line = field_ref[r + 1 + a]
                for b in range(3):
                    product = shifted[b] * line
                    weights[3 * a + b] = weights[3 * a + b] + jnp.sum(
                        product.reshape(ring // 8, 8, LANES), axis=0
                    )
        for t in range(9):
            tapsum_ref[pl.ds(t, 1), away] = jnp.sum(weights[t], axis=0, keepdims=True)
        return carry

    lax.fori_loop(0, GROUP // LANES, lanes_body, 0)


def spread_product(piece_rows, cols, order, here_ref, mixed_all, target_ref, mine_ref, other_ref):
    tokens = target_ref.shape[0]
    axis, bit = order[0]
    apart = bit if axis == "col" else bit * cols
    index = {"col": here_ref[0], "row": here_ref[1]}
    flipped = (index[axis] // bit) % 2 == 1
    per = GROUP // piece_rows
    for g in range(mixed_all.shape[1] // GROUP):
        product = dot_tn(mixed_all[pl.ds(0, tokens), pl.ds(g * GROUP, GROUP)], target_ref[...])
        for k in range(per):
            if k & apart:
                continue
            owner = g * per + k
            a, b = (product[x * piece_rows : (x + 1) * piece_rows] for x in (k, k | apart))
            away = {"col": (owner % cols) ^ index["col"], "row": (owner // cols) ^ index["row"]}
            place = 0
            for name, digit in order[1:]:
                place = 2 * place + (away[name] // digit) % 2
            at = pl.ds(pl.multiple_of(place * piece_rows, piece_rows), piece_rows)
            mine_ref[at, :] = jnp.where(flipped, b, a)
            other_ref[at, :] = jnp.where(flipped, a, b).astype(bf16)


def front_kernel(
    head_size, tile, piece_rows, cols, order,
    col_ref, sharp_ref, own_ref, far_ref, v_ref, u_ref, side_ref, twin_ref, next_ref,
    corner_ref, proj_ref, taps_ref,
    merged_ref, attn_ref, gram_ref, scale_ref, block_ref, mixed_all, target_ref, tapsum_ref,
    mine_ref, other_ref, carry_ref,
    field_ref, slope_ref, upside_ref, *projected,
):
    tile_rows, tile_cols = tile
    tokens, width = v_ref.shape
    side = tile_rows * RIM
    two = 2 * tile_cols

    tapsum_ref[...] = jnp.zeros(tapsum_ref.shape, f32)
    attention_phase(
        head_size, col_ref, sharp_ref, own_ref, far_ref, attn_ref, gram_ref, scale_ref, block_ref
    )
    for g in range(width // GROUP):
        at = pl.ds(g * GROUP, GROUP)
        weights = block_ref[at, :]
        mixed_all[pl.ds(0, tokens), at] = dot_nt(v_ref[:, at], weights).astype(bf16)
        around = [(side_ref, side), (twin_ref, two), (next_ref, two), (corner_ref, 4 * RIM)]
        value = dot_nt(
            jnp.concatenate([ref[pl.ds(0, size), at] for ref, size in around], axis=0), weights
        )
        start = 0
        for ref, size in around:
            piece = value[start : start + size]
            if ref is side_ref or ref is corner_ref:
                piece = piece * keep_side(col_ref, piece.shape)
            mixed_all[pl.ds(tokens + start, size), at] = piece.astype(bf16)
            start += size

    steps = target_ref.shape[1] // GROUP
    projected[0][...] = dot_nn(mixed_all[...], proj_ref[:, pl.ds(0, GROUP)])
    for step in range(steps):
        into = carry_ref if step == steps - 1 else projected[(step + 1) % 2]
        stencil_chunk(
            step, tile, col_ref, u_ref, side_ref, twin_ref, next_ref, corner_ref, taps_ref,
            merged_ref, target_ref, tapsum_ref, field_ref, slope_ref, projected[step % 2], upside_ref, 0,
            functools.partial(project_part, mixed_all, proj_ref, into, (step + 1) * GROUP),
        )
    spread_product(piece_rows, cols, order, col_ref, mixed_all, target_ref, mine_ref, other_ref)


def project_part(mixed_all, proj_ref, into_ref, channel, part):
    rows = mixed_all.shape[0] // (GROUP // LANES)
    at = pl.ds(pl.multiple_of(part * rows, 16), rows)
    into_ref[at, :] = dot_nn(mixed_all[at, :], proj_ref[:, pl.ds(channel, GROUP)])


def back_kernel(
    head_size, tile, first_channel,
    col_ref, u_ref, v_ref, side_ref, twin_ref, next_ref, corner_ref, mixed_all, proj_ref, taps_ref,
    front_target, front_taps, carry_ref,
    merged_ref, target_ref, grad_ref, mine_ref, other_ref,
    field_ref, slope_ref, upside_ref, projected_a, projected_b, tapsum_ref, partial_ref,
):
    tokens, width = v_ref.shape
    blocks = width // LANES
    half_blocks = blocks // 2
    span = width - first_channel
    tapsum_ref[...] = jnp.zeros(tapsum_ref.shape, f32)

    def grad_part(part):
        rows = width // (GROUP // LANES)
        at = pl.ds(pl.multiple_of(part * rows, LANES), rows)
        partial_ref[:, at] = dot_nt(front_target[...], proj_ref[at, pl.ds(0, first_channel)])

    steps = span // GROUP
    source = carry_ref
    for step in range(steps):
        into = (projected_a, projected_b)[step % 2]
        if step == steps - 1:
            beside = grad_part
        else:
            beside = functools.partial(
                project_part, mixed_all, proj_ref, into, first_channel + (step + 1) * GROUP
            )
        stencil_chunk(
            step, tile, col_ref, u_ref, side_ref, twin_ref, next_ref, corner_ref, taps_ref,
            merged_ref, target_ref, tapsum_ref, field_ref, slope_ref, source, upside_ref, first_channel, beside,
        )
        source = into
    grad_ref[...] = (
        partial_ref[...] + dot_nt(target_ref[...], proj_ref[:, pl.ds(first_channel, span)])
    ).astype(bf16)
    for g in range(width // GROUP):
        at = pl.ds(g * GROUP, GROUP)
        square = dot_tn(grad_ref[:, at], v_ref[:, at])
        for p in range(GROUP // LANES):
            cut = slice(p * LANES, (p + 1) * LANES)
            block = g * (GROUP // LANES) + p
            h, inner = divmod(block, half_blocks)
            packed_rows = pack_diagonal(square[cut, cut], head_size)
            if block * LANES < first_channel:
                tap_rows = front_taps[:, pl.ds(block * LANES, LANES)]
            else:
                tap_rows = tapsum_ref[:, pl.ds(block * LANES - first_channel, LANES)]

            def put(ref, inner=inner, packed_rows=packed_rows, tap_rows=tap_rows):
                ref[pl.ds(inner * head_size, head_size), :] = packed_rows.astype(ref.dtype)
                ref[pl.ds(half_blocks * head_size + inner * 16, 16), :] = tap_rows.astype(ref.dtype)

            @pl.when(col_ref[0] == h)
            def _():
                put(mine_ref)

            @pl.when(col_ref[0] != h)
            def _():
                put(other_ref)


def stencil_scratch(tile):
    ring = tile[1] + RIM
    return [
        pltpu.VMEM((tile[0] + 4, ring, LANES), f32),
        pltpu.VMEM((tile[0] + 2, ring, LANES), f32),
        pltpu.VMEM(((tile[0] + 2) * ring, GROUP), f32),
        pltpu.VMEM(((tile[0] + 4) * ring, GROUP), f32),
        pltpu.VMEM(((tile[0] + 4) * ring, GROUP), f32),
    ]


def front_call(col, sharp, own, far, v, u, halo, proj, taps, tile, head_size, piece_rows, cols, order):
    tokens, width = v.shape
    ring = tile[1] + RIM
    span = width // 2
    grams = width // LANES * head_size
    sds = jax.ShapeDtypeStruct
    outs = [
        sds((tokens, span), bf16),
        sds((grams, LANES), f32),
        sds((grams, LANES), f32),
        sds((grams, LANES), f32),
        sds((width, GROUP), bf16),
        sds(((tile[0] + 4) * ring, width), bf16),
        sds((tokens, span), bf16),
        sds((16, span), f32),
        sds((width // 2, span), f32),
        sds((width // 2, span), bf16),
        sds(((tile[0] + 4) * ring, GROUP), f32),
    ]
    args = (col, sharp, own, far, v, u, *halo, proj, taps)
    return pl.pallas_call(
        functools.partial(front_kernel, head_size, tile, piece_rows, cols, order),
        in_specs=[SCALAR] * 2 + [LOCAL] * (len(args) - 2),
        out_specs=[LOCAL] * len(outs),
        out_shape=outs,
        scratch_shapes=stencil_scratch(tile),
        compiler_params=params(),
        cost_estimate=cost(10),
        name="front",
    )(*args)


def back_call(col, u, v, halo, mixed_all, proj, taps, target, tapsum, carry, tile, head_size):
    tokens, width = v.shape
    span = width // 2
    lines = width // LANES // 2 * (head_size + 16)
    sds = jax.ShapeDtypeStruct
    outs = [
        sds((tokens, span), bf16),
        sds((tokens, span), bf16),
        sds((tokens, width), bf16),
        sds((lines, LANES), f32),
        sds((lines, LANES), bf16),
    ]
    args = (col, u, v, *halo, mixed_all, proj, taps, target, tapsum, carry)
    return pl.pallas_call(
        functools.partial(back_kernel, head_size, tile, span),
        in_specs=[SCALAR] + [LOCAL] * (len(args) - 1),
        out_specs=[LOCAL] * len(outs),
        out_shape=outs,
        scratch_shapes=stencil_scratch(tile)
        + [pltpu.VMEM((16, span), f32), pltpu.VMEM((tokens, width), f32)],
        compiler_params=params(),
        cost_estimate=cost(10),
        name="back",
    )(*args)


def projector_kernel(
    piece_rows, cols, order, here_ref, mixed_all, target_ref, after_ref, mine_ref, other_ref
):
    spread_product(piece_rows, cols, order, here_ref, mixed_all, target_ref, mine_ref, other_ref)


def projector_call(here, mixed_all, target, after, piece_rows, cols, order):
    width, span = mixed_all.shape[1], target.shape[1]
    sds = jax.ShapeDtypeStruct
    return pl.pallas_call(
        functools.partial(projector_kernel, piece_rows, cols, order),
        in_specs=[SCALAR, LOCAL, LOCAL, pl.BlockSpec(memory_space=pl.ANY)],
        out_specs=[LOCAL, LOCAL],
        out_shape=[sds((width // 2, span), f32), sds((width // 2, span), bf16)],
        compiler_params=params(),
        cost_estimate=cost(2),
        name="projector",
    )(here, mixed_all, target, after)


def content_kernel(grad_ref, block_ref, merged_front, merged_back, after_ref, out_ref, merged_ref):
    span = out_ref.shape[1]
    for g in range(span // GROUP):
        at = pl.ds(pl.multiple_of(pl.program_id(0) * span + g * GROUP, GROUP), GROUP)
        out_ref[:, pl.ds(g * GROUP, GROUP)] = dot_nn(grad_ref[:, at], block_ref[at, :]).astype(bf16)

    @pl.when(pl.program_id(0) == 0)
    def _():
        merged_ref[...] = merged_front[...]

    @pl.when(pl.program_id(0) != 0)
    def _():
        merged_ref[...] = merged_back[...]


def content_call(grad, block, merged_front, merged_back, after):
    tokens, width = grad.shape
    half = pl.BlockSpec((tokens, width // 2), lambda i: (0, i))
    out = jax.ShapeDtypeStruct((tokens, width), bf16)
    return pl.pallas_call(
        content_kernel,
        grid=(2,),
        in_specs=[LOCAL] * 4 + [pl.BlockSpec(memory_space=pl.ANY)],
        out_specs=[half, half],
        out_shape=[out, out],
        compiler_params=params(),
        cost_estimate=cost(2),
        name="content",
    )(grad, block, merged_front, merged_back, after)


def final_kernel(
    head_size,
    col_ref,
    sharp_ref,
    own_ref,
    far_ref,
    energy_own_ref,
    energy_far_ref,
    attn_ref,
    gram_ref,
    scale_ref,
    q_ref,
    k_ref,
    dq_ref,
    dk_ref,
    heat_ref,
    taps_ref,
    mixer_ref,
):
    half = pl.program_id(0)
    groups = dq_ref.shape[1] // GROUP
    packed = LANES // head_size
    per = GROUP // LANES
    half_blocks = groups * per
    mine = half == col_ref[0]
    owner = lane_head(head_size)
    row = lax.broadcasted_iota(jnp.int32, (head_size, LANES), 0)
    lane = lax.broadcasted_iota(jnp.int32, (head_size, LANES), 1)
    mixer_ref[...] = jnp.zeros(mixer_ref.shape, bf16)
    q_terms, k_terms = [], []

    def take(own, far, at, size):
        return jnp.where(mine, own[pl.ds(at, size), :], far[pl.ds(at, size), :])

    for inner in range(half_blocks):
        block = half * half_blocks + inner
        p = inner % per
        grad = take(own_ref, far_ref, inner * head_size, head_size)
        taps_ref[:, pl.ds(inner * LANES, LANES)] = take(
            own_ref, far_ref, half_blocks * head_size + inner * 16, 16
        )[:9]
        q_line = take(energy_own_ref, energy_far_ref, half_blocks * head_size + inner, 1)
        k_line = take(energy_own_ref, energy_far_ref, half_blocks * head_size + 8 + inner, 1)
        at = pl.ds(pl.multiple_of(block * head_size, head_size), head_size)
        attention, gram, scale = attn_ref[at, :], gram_ref[at, :], scale_ref[at, :]
        scores = attention * (grad - sum_in_head(attention * grad, owner, packed))
        heated = scores * gram
        heat = by_head(
            [jnp.full(scores.shape, sharp_ref[block * packed + k], f32) for k in range(packed)], owner
        )
        for k in range(packed):
            heat_ref[block * packed + k] = jnp.sum(jnp.where(owner == k, heated, 0.0))
        gram_grad = heat * scores
        corr = gram_grad * gram
        k_corr = jnp.sum(corr, axis=0, keepdims=True)
        columns = sum_in_head(corr, owner, packed)
        q_corr = jnp.sum(jnp.where(lane == row + owner * head_size, columns, 0.0), axis=0, keepdims=True)
        q_scale = lax.rsqrt(q_line + epsilon)
        k_scale = lax.rsqrt(k_line + epsilon)
        q_terms.append(q_scale * q_scale * q_corr)
        k_terms.append(k_scale * k_scale * k_corr)
        low = (scale * gram_grad).astype(bf16)
        for k in range(packed):
            mixer_ref[pl.ds(inner * LANES + k * head_size, head_size), pl.ds(p * LANES, LANES)] = jnp.where(
                owner == k, low, jnp.zeros_like(low)
            )
    for g in range(groups):
        here = pl.ds(pl.multiple_of((half * groups + g) * GROUP, GROUP), GROUP)
        at = pl.ds(g * GROUP, GROUP)
        q, k = q_ref[:, here], k_ref[:, here]
        mixer = mixer_ref[at, :]
        q_term = jnp.concatenate(q_terms[g * per : (g + 1) * per], axis=1)
        k_term = jnp.concatenate(k_terms[g * per : (g + 1) * per], axis=1)
        dq_ref[:, at] = (dot_nt(k, mixer) - q.astype(f32) * q_term).astype(bf16)
        dk_ref[:, at] = (dot_nn(q, mixer) - k.astype(f32) * k_term).astype(bf16)


def final_call(col, sharp, own, far, energy_own, energy_far, attn, gram, scale, q, k, head_size):
    tokens, width = q.shape
    sds = jax.ShapeDtypeStruct
    token_block = pl.BlockSpec((tokens, width // 2), lambda i: (0, i))
    args = (col, sharp, own, far, energy_own, energy_far, attn, gram, scale, q, k)
    return pl.pallas_call(
        functools.partial(final_kernel, head_size),
        grid=(2,),
        in_specs=[SCALAR, SCALAR] + [LOCAL] * 9,
        out_specs=[
            token_block,
            token_block,
            SCALAR,
            pl.BlockSpec((9, width // 2), lambda i: (0, i)),
        ],
        out_shape=[
            sds((tokens, width), bf16),
            sds((tokens, width), bf16),
            sds(sharp.shape, f32),
            sds((9, width), f32),
        ],
        scratch_shapes=[pltpu.VMEM((width // 2, GROUP), bf16)],
        compiler_params=params(),
        cost_estimate=cost(5),
        name="final",
    )(*args)


def swap(x, axis, bit):
    return lax.ppermute(x, axis, [(i, i ^ bit) for i in range(lax.axis_size(axis))])


def row_bits():
    bits, bit = [], 1
    while bit < lax.axis_size("row"):
        bits.append(bit)
        bit *= 2
    return bits


def halve(total):
    half = total.shape[0] // 2
    return total[:half], total[half:].astype(bf16)


def add_low(total, got):
    return total + got.astype(f32)


def add_step(total, axis, bit):
    low = total.astype(bf16)
    return low.astype(f32) + swap(low, axis, bit).astype(f32)


def scatter_step(total, group):
    count = 2 ** len(group)
    rows = total.shape[0] // count
    out = total[:rows]
    for k in range(1, count):
        mask = sum(bit for i, bit in enumerate(group) if (k >> (len(group) - 1 - i)) & 1)
        out = add_low(out, swap(total[k * rows : (k + 1) * rows].astype(bf16), "row", mask))
    return out


def scatter_both(first, second, group):
    early, late = group
    quarter, half = first.shape[0] // 4, second.shape[0] // 2
    pieces = [first[k * quarter : (k + 1) * quarter] for k in range(4)]
    joint = swap(jnp.concatenate([pieces[1], second[half:]]).astype(bf16), "row", late)
    first = add_low(pieces[0], swap(pieces[2].astype(bf16), "row", early))
    first = add_low(first, swap(pieces[3].astype(bf16), "row", early | late))
    return add_low(first, joint[:quarter]), add_low(second[:half], joint[quarter:])


def tie(*values):
    return lax.optimization_barrier(values)


def shards(q, k, v, u, sharp, proj, taps):
    tile = v.shape[:2]
    width = v.shape[2]
    tokens = tile[0] * tile[1]
    head_size = width // sharp.shape[0]
    rows, cols = lax.axis_size("row"), lax.axis_size("col")
    flat = lambda x: x.reshape(tokens, width)
    here = jnp.stack([lax.axis_index("col"), lax.axis_index("row")]).astype(jnp.int32)
    q2, k2, v2, u2 = flat(q), flat(k), flat(v), flat(u)
    bits = row_bits()
    early = [("row", bits[0]), ("col", 1)] + [("row", bit) for bit in bits[1:]]
    late = [("col", 1)] + [("row", bit) for bit in bits]
    piece_rows = width // (rows * cols)

    mine, other = gram_call(q2, k2, head_size)
    to_twin, to_next = edges_call(here, v, u)
    total = add_low(mine, swap(other, "col", 1))
    start = jnp.where(lax.axis_index("col") == 0, v.shape[1] - RIM, 0)
    edge = lambda x: lax.dynamic_slice_in_dim(x, start, RIM, axis=1)
    pairs_next = [(j, j + 1) for j in range(1, rows - 1, 2)]
    pairs_next = pairs_next + [(b, a) for a, b in pairs_next]
    side = swap(jnp.concatenate([edge(v), edge(u)]), "col", 1)
    for i, bit in enumerate(bits):
        total = total + swap(total, "row", bit)
        if i == 2:
            from_twin = swap(to_twin, "row", 1)
            total, from_twin = tie(total, from_twin)
        if i == 2:
            from_next = lax.ppermute(to_next, "row", pairs_next)
            total, from_next = tie(total, from_next)
    corner = swap(
        edge(jnp.concatenate([from_twin[:2], from_next[:2], from_twin[2:], from_next[2:]])), "col", 1
    )
    around = tuple(x.reshape(-1, width) for x in (side, from_twin, from_next, corner))
    energy_own, energy_far = total, swap(total, "col", 1)

    (merged_front, attn, gram, scale, block, mixed_all, front_target, front_taps, mine, other, carry) = front_call(
        here, sharp, energy_own, energy_far, v2, u2, around, proj, taps, tile, head_size, piece_rows, cols, early
    )
    halves = [swap(x, "row", bits[0]) for x in jnp.split(other, 2)]
    first = halves[:1]
    front_mine = mine
    merged_back, target, grad, mine, other = back_call(
        here, u2, v2, around, mixed_all, proj, taps, front_target, front_taps, carry, tile, head_size
    )

    mine, other, *first = tie(mine, other, *first)
    after = swap(other, "col", 1)
    total = add_low(mine, after)
    turns = bits[1:2] + bits[:1] + bits[2:]
    back_mine, back_other = projector_call(here, mixed_all, target, after, piece_rows, cols, late)
    front_sum = add_low(front_mine, jnp.concatenate([*first, *halves[1:]]))
    back_sum = add_low(back_mine, swap(back_other, "col", 1))
    total = add_step(total, "row", turns[0])
    total, back_sum = tie(total, back_sum)
    total = add_step(total, "row", turns[1])
    total, front_sum = tie(total, front_sum)
    for bit in turns[2:]:
        total = add_step(total, "row", bit)
    front_sum, leaves = halve(front_sum)
    front_sum = add_low(front_sum, swap(leaves, "col", 1))
    back_sum = scatter_step(back_sum, bits[:2])
    front_sum = scatter_step(front_sum, bits[1:2])
    total, back_sum = tie(total, back_sum)
    for bit in bits[2:-1]:
        front_sum, back_sum = scatter_step(front_sum, [bit]), scatter_step(back_sum, [bit])
    far = swap(total, "col", 1)
    kept, leaves = zip(halve(front_sum), halve(back_sum))
    got = swap(jnp.concatenate(leaves), "row", bits[-1])
    dq, dk, heat, tap_sums = final_call(
        here, sharp, total, far, energy_own, energy_far, attn, gram, scale, q2, k2, head_size
    )
    content, merged = content_call(grad, block, merged_front, merged_back, tap_sums)
    content, *kept = tie(content, *kept)
    front_sum, back_sum = (add_low(x, y) for x, y in zip(kept, jnp.split(got, 2)))
    projector = jnp.concatenate([front_sum, back_sum], axis=1)
    full = lambda x: x.reshape(tile + (width,))
    return full(merged), full(dq), full(dk), full(content), heat, tap_sums, projector


def solution(mesh):
    field = P(("scene", "row"), "col", None)
    return jax.shard_map(
        shards,
        mesh=mesh,
        in_specs=(field, field, field, field, P(), P(), P()),
        out_specs=(
            field,
            field,
            field,
            field,
            P("scene"),
            P("scene", None),
            P(("scene", "row", "col"), None),
        ),
        check_vma=False,
    )
```

```python
import functools

import jax
import jax.numpy as jnp
from jax import lax
from jax.experimental import pallas as pl
from jax.experimental.pallas import tpu as pltpu
from jax.sharding import PartitionSpec as P

epsilon = 1e-06
inverse_root = 0.7071067811865476
density_root = 0.3989422804014327
LANES = 128
GROUP = 256
RIM = 8
f32 = jnp.float32
bf16 = jnp.bfloat16
VMEM_LIMIT = 24 * 1024 * 1024


def whole(shape):
    return pl.BlockSpec(shape, lambda *_: (0,) * len(shape))


SCALAR = pl.BlockSpec(memory_space=pltpu.SMEM)
LOCAL = pl.BlockSpec(memory_space=pltpu.VMEM)


def params(limit=VMEM_LIMIT):
    return pltpu.CompilerParams(vmem_limit_bytes=limit)


def cost(microseconds):
    return pl.CostEstimate(flops=0, bytes_accessed=int(microseconds * 3.6e6), transcendentals=0)


def pad_lines(lines, count):
    blank = jnp.zeros((count - len(lines), LANES), f32)
    return jnp.concatenate(lines + [blank], axis=0) if count > len(lines) else jnp.concatenate(lines, axis=0)


def dot_tn(a, b):
    return lax.dot_general(a, b, (((0,), (0,)), ((), ())), preferred_element_type=f32)


def dot_nt(a, b):
    return lax.dot_general(a, b, (((1,), (1,)), ((), ())), preferred_element_type=f32)


def dot_nn(a, b):
    return jnp.dot(a, b, preferred_element_type=f32)


def lane_head(head_size):
    return lax.broadcasted_iota(jnp.int32, (head_size, LANES), 1) // head_size


def by_head(parts, owner):
    out = parts[0]
    for k in range(1, len(parts)):
        out = jnp.where(owner == k, parts[k], out)
    return out


def pack_diagonal(square, head_size):
    owner = lane_head(head_size)
    return by_head(
        [square[k * head_size : (k + 1) * head_size] for k in range(LANES // head_size)], owner
    )


def sum_in_head(values, owner, packed):
    sums = [jnp.sum(jnp.where(owner == k, values, 0.0), axis=1, keepdims=True) for k in range(packed)]
    return by_head([jnp.broadcast_to(s, values.shape) for s in sums], owner)


def edges_kernel(here_ref, v_head, v_tail, u_head, u_tail, twin_ref, next_ref):
    even = lax.rem(here_ref[1], 2) == 0

    def put(tail_ref, head_ref):
        tail_ref[:2] = v_tail[...]
        tail_ref[2:] = u_tail[...]
        head_ref[:2] = v_head[...]
        head_ref[2:] = u_head[...]

    @pl.when(even)
    def _():
        put(twin_ref, next_ref)

    @pl.when(jnp.logical_not(even))
    def _():
        put(next_ref, twin_ref)


def edges_call(here, v, u):
    rows, cols, width = v.shape
    out = jax.ShapeDtypeStruct((3, cols, width), bf16)
    return pl.pallas_call(
        edges_kernel,
        grid=(1,),
        in_specs=[
            SCALAR,
            pl.BlockSpec((2, cols, width), lambda i: (0, 0, 0)),
            pl.BlockSpec((2, cols, width), lambda i: (rows // 2 - 1, 0, 0)),
            pl.BlockSpec((1, cols, width), lambda i: (0, 0, 0)),
            pl.BlockSpec((1, cols, width), lambda i: (rows - 1, 0, 0)),
        ],
        out_specs=[LOCAL, LOCAL],
        out_shape=[out, out],
        compiler_params=params(),
        cost_estimate=cost(1),
        name="edges",
    )(here, v, v, u, u)


def gram_kernel(head_size, q_ref, k_ref, mine_ref, other_ref):
    half = pl.program_id(0)
    per = GROUP // LANES
    energy = mine_ref.shape[0] - 16
    values = []
    for g in range(q_ref.shape[1] // GROUP):
        at = pl.ds(g * GROUP, GROUP)
        square = dot_tn(q_ref[:, at], k_ref[:, at])
        for p in range(per):
            cut = slice(p * LANES, (p + 1) * LANES)
            block = g * per + p
            values.append((block * head_size, pack_diagonal(square[cut, cut], head_size)))
            for line, ref in ((energy, q_ref), (energy + 8, k_ref)):
                x = ref[:, pl.ds(block * LANES, LANES)].astype(f32)
                values.append((line + block, jnp.sum(x * x, axis=0, keepdims=True)))

    def put(ref):
        for at, value in values:
            ref[pl.ds(at, value.shape[0]), :] = value

    @pl.when(half == 0)
    def _():
        mine_ref[pl.ds(energy, 16), :] = jnp.zeros((16, LANES), f32)
        other_ref[pl.ds(energy, 16), :] = jnp.zeros((16, LANES), f32)

    col = lax.axis_index("col")

    @pl.when(half == col)
    def _():
        put(mine_ref)

    @pl.when(half != col)
    def _():
        put(other_ref)


def gram_call(q, k, head_size):
    tokens, width = q.shape
    lines = width // 2 // LANES * head_size + 16
    out = jax.ShapeDtypeStruct((lines, LANES), f32)
    return pl.pallas_call(
        functools.partial(gram_kernel, head_size),
        grid=(2,),
        in_specs=[
            pl.BlockSpec((tokens, width // 2), lambda i: (0, i)),
            pl.BlockSpec((tokens, width // 2), lambda i: (0, i)),
        ],
        out_specs=[LOCAL, LOCAL],
        out_shape=[out, out],
        compiler_params=params(48 * 1024 * 1024),
        cost_estimate=cost(2.5),
        name="gram",
    )(q, k)


def gelu_terms(u):
    cumul = 0.5 * (1.0 + lax.erf(u * inverse_root))
    return u * cumul, cumul + u * jnp.exp(-0.5 * u * u) * density_root


def attention_block(head_size, raw, q_line, k_line, sharp):
    packed = LANES // head_size
    owner = lane_head(head_size)
    row = lax.broadcasted_iota(jnp.int32, (head_size, LANES), 0)
    lane = lax.broadcasted_iota(jnp.int32, (head_size, LANES), 1)
    q_energy = by_head(
        [
            jnp.broadcast_to(
                jnp.sum(jnp.where(lane == row + k * head_size, q_line, 0.0), axis=1, keepdims=True),
                raw.shape,
            )
            for k in range(packed)
        ],
        owner,
    )
    q_scale = lax.rsqrt(q_energy + epsilon)
    k_scale = lax.rsqrt(k_line + epsilon)
    gram = q_scale * raw * k_scale
    heat = by_head([jnp.full(raw.shape, s, f32) for s in sharp], owner)
    numer = jnp.exp(heat * gram)
    attention = numer / sum_in_head(numer, owner, packed)
    return attention, gram, q_scale * k_scale


def attention_phase(
    head_size, col_ref, sharp_ref, own_ref, far_ref, attn_ref, gram_ref, scale_ref, block_ref
):
    packed = LANES // head_size
    blocks = attn_ref.shape[0] // head_size
    half_blocks = blocks // 2
    is_first = col_ref[0] == 0
    block_ref[...] = jnp.zeros(block_ref.shape, bf16)
    owner = lane_head(head_size)
    for p in range(blocks):
        h, inner = divmod(p, half_blocks)

        def take(at, size):
            a = own_ref[pl.ds(at, size), :]
            b = far_ref[pl.ds(at, size), :]
            return jnp.where(is_first, a, b) if h == 0 else jnp.where(is_first, b, a)

        raw = take(inner * head_size, head_size)
        q_line = take(half_blocks * head_size + inner, 1)
        k_line = take(half_blocks * head_size + 8 + inner, 1)
        attention, gram, scale = attention_block(
            head_size, raw, q_line, k_line, [sharp_ref[p * packed + k] for k in range(packed)]
        )
        at = pl.ds(p * head_size, head_size)
        attn_ref[at, :] = attention
        gram_ref[at, :] = gram
        scale_ref[at, :] = scale
        low = attention.astype(bf16)
        inside = (p * LANES) % GROUP
        for k in range(packed):
            block_ref[pl.ds(p * LANES + k * head_size, head_size), pl.ds(inside, LANES)] = jnp.where(
                owner == k, low, jnp.zeros_like(low)
            )


def keep_side(col_ref, shape):
    place = lax.rem(lax.broadcasted_iota(jnp.int32, shape, 0), RIM)
    second = col_ref[0].astype(f32)
    right = jnp.where(place < 2, 1.0, 0.0)
    left = jnp.where(place >= RIM - 2, 1.0, 0.0)
    return right + second * (left - right)


def stencil_chunk(
    step, tile, col_ref, u_ref, side_ref, twin_ref, next_ref, corner_ref, taps_ref,
    merged_ref, target_ref, tapsum_ref, field_ref, slope_ref, projected_ref, upside_ref,
    first_channel, beside,
):
    tile_rows, tile_cols = tile
    tokens = tile_rows * tile_cols
    ring = tile_cols + RIM
    side = tile_rows * RIM
    chunk = pl.ds(first_channel + step * GROUP, GROUP)
    for at, size, ref, start in (
        (0, side, side_ref, side),
        (side, tile_cols, twin_ref, 2 * tile_cols),
        (side + tile_cols, tile_cols, next_ref, 2 * tile_cols),
        (side + 2 * tile_cols, 2 * RIM, corner_ref, 4 * RIM),
    ):
        piece = ref[pl.ds(start, size), chunk].astype(f32)
        if ref is side_ref or ref is corner_ref:
            piece = piece * keep_side(col_ref, piece.shape)
        upside_ref[pl.ds(at, size), :] = piece

    def lanes_body(part, carry):
        lanes = pl.ds(pl.multiple_of(part * LANES, LANES), LANES)
        glob = pl.ds(pl.multiple_of(first_channel + step * GROUP + part * LANES, LANES), LANES)
        away = pl.ds(pl.multiple_of(step * GROUP + part * LANES, LANES), LANES)
        taps = [taps_ref[pl.ds(t, 1), glob] for t in range(9)]
        rim = tokens + side
        from_next = 1 - lax.rem(col_ref[1], 2)
        beside(part)

        def ring_row(r):
            if 0 <= r < tile_rows:
                pieces = (r * tile_cols, tokens + r * RIM)
            else:
                k = r + 2 if r < 0 else r - tile_rows
                k = k + 2 * (from_next if r < 0 else 1 - from_next)
                pieces = (
                    pl.multiple_of(rim + k * tile_cols, RIM),
                    pl.multiple_of(rim + 4 * tile_cols + k * RIM, RIM),
                )
            return jnp.concatenate(
                [
                    projected_ref[pl.ds(pieces[0], tile_cols), lanes],
                    projected_ref[pl.ds(pieces[1], RIM), lanes],
                ],
                axis=0,
            )

        def up_row(r):
            if 0 <= r < tile_rows:
                return jnp.concatenate(
                    [
                        u_ref[pl.ds(r * tile_cols, tile_cols), glob].astype(f32),
                        upside_ref[pl.ds(r * RIM, RIM), lanes],
                    ],
                    axis=0,
                )
            k = from_next if r < 0 else 1 - from_next
            pieces = (
                pl.multiple_of(side + k * tile_cols, RIM),
                pl.multiple_of(side + 2 * tile_cols + k * RIM, RIM),
            )
            return jnp.concatenate(
                [
                    upside_ref[pl.ds(pieces[0], tile_cols), lanes],
                    upside_ref[pl.ds(pieces[1], RIM), lanes],
                ],
                axis=0,
            )

        for r in range(-2, tile_rows + 2):
            field_ref[r + 2] = ring_row(r).astype(bf16).astype(f32)
        for r in range(-1, tile_rows + 1):
            near = [field_ref[r + 1 + a] for a in range(3)]
            sums = [sum(taps[3 * a + b] * near[a] for a in range(3)) for b in range(3)]
            total = pltpu.roll(sums[0], 1, 0) + sums[1] + pltpu.roll(sums[2], ring - 1, 0)
            active, slope = gelu_terms(total)
            slope_ref[r + 1] = (up_row(r) * slope).astype(bf16).astype(f32)
            if 0 <= r < tile_rows:
                at = pl.ds(r * tile_cols, tile_cols)
                merged_ref[at, away] = (projected_ref[at, lanes] + active[:tile_cols]).astype(bf16)
        weights = [jnp.zeros((8, LANES), f32) for _ in range(9)]
        blank = jnp.zeros((RIM, LANES), f32)
        for r in range(tile_rows):
            near = [slope_ref[r + 2 - a] for a in range(3)]
            sums = [sum(taps[3 * a + b] * near[a] for a in range(3)) for b in range(3)]
            back = pltpu.roll(sums[0], ring - 1, 0) + sums[1] + pltpu.roll(sums[2], 1, 0)
            at = pl.ds(r * tile_cols, tile_cols)
            target_ref[at, away] = (u_ref[at, glob].astype(f32) + back[:tile_cols]).astype(bf16)
            centre = jnp.concatenate([near[1][:tile_cols], blank], axis=0)
            shifted = [pltpu.roll(centre, ring - 1, 0), centre, pltpu.roll(centre, 1, 0)]
            for a in range(3):
                line = field_ref[r + 1 + a]
                for b in range(3):
                    product = shifted[b] * line
                    weights[3 * a + b] = weights[3 * a + b] + jnp.sum(
                        product.reshape(ring // 8, 8, LANES), axis=0
                    )
        for t in range(9):
            tapsum_ref[pl.ds(t, 1), away] = jnp.sum(weights[t], axis=0, keepdims=True)
        return carry

    lax.fori_loop(0, GROUP // LANES, lanes_body, 0)


def spread_product(piece_rows, cols, order, here_ref, mixed_all, target_ref, mine_ref, other_ref):
    tokens = target_ref.shape[0]
    axis, bit = order[0]
    apart = bit if axis == "col" else bit * cols
    index = {"col": here_ref[0], "row": here_ref[1]}
    flipped = (index[axis] // bit) % 2 == 1
    per = GROUP // piece_rows
    for g in range(mixed_all.shape[1] // GROUP):
        product = dot_tn(mixed_all[pl.ds(0, tokens), pl.ds(g * GROUP, GROUP)], target_ref[...])
        for k in range(per):
            if k & apart:
                continue
            owner = g * per + k
            a, b = (product[x * piece_rows : (x + 1) * piece_rows] for x in (k, k | apart))
            away = {"col": (owner % cols) ^ index["col"], "row": (owner // cols) ^ index["row"]}
            place = 0
            for name, digit in order[1:]:
                place = 2 * place + (away[name] // digit) % 2
            at = pl.ds(pl.multiple_of(place * piece_rows, piece_rows), piece_rows)
            mine_ref[at, :] = jnp.where(flipped, b, a)
            other_ref[at, :] = jnp.where(flipped, a, b).astype(bf16)


def front_kernel(
    head_size, tile, piece_rows, cols, order,
    col_ref, sharp_ref, own_ref, far_ref, v_ref, u_ref, side_ref, twin_ref, next_ref,
    corner_ref, proj_ref, taps_ref,
    merged_ref, attn_ref, gram_ref, scale_ref, block_ref, mixed_all, target_ref, tapsum_ref,
    mine_ref, other_ref, carry_ref,
    field_ref, slope_ref, upside_ref, *projected,
):
    tile_rows, tile_cols = tile
    tokens, width = v_ref.shape
    side = tile_rows * RIM
    two = 2 * tile_cols

    tapsum_ref[...] = jnp.zeros(tapsum_ref.shape, f32)
    attention_phase(
        head_size, col_ref, sharp_ref, own_ref, far_ref, attn_ref, gram_ref, scale_ref, block_ref
    )
    for g in range(width // GROUP):
        at = pl.ds(g * GROUP, GROUP)
        weights = block_ref[at, :]
        mixed_all[pl.ds(0, tokens), at] = dot_nt(v_ref[:, at], weights).astype(bf16)
        around = [(side_ref, side), (twin_ref, two), (next_ref, two), (corner_ref, 4 * RIM)]
        value = dot_nt(
            jnp.concatenate([ref[pl.ds(0, size), at] for ref, size in around], axis=0), weights
        )
        start = 0
        for ref, size in around:
            piece = value[start : start + size]
            if ref is side_ref or ref is corner_ref:
                piece = piece * keep_side(col_ref, piece.shape)
            mixed_all[pl.ds(tokens + start, size), at] = piece.astype(bf16)
            start += size

    steps = target_ref.shape[1] // GROUP
    projected[0][...] = dot_nn(mixed_all[...], proj_ref[:, pl.ds(0, GROUP)])
    for step in range(steps):
        into = carry_ref if step == steps - 1 else projected[(step + 1) % 2]
        stencil_chunk(
            step, tile, col_ref, u_ref, side_ref, twin_ref, next_ref, corner_ref, taps_ref,
            merged_ref, target_ref, tapsum_ref, field_ref, slope_ref, projected[step % 2], upside_ref, 0,
            functools.partial(project_part, mixed_all, proj_ref, into, (step + 1) * GROUP),
        )
    spread_product(piece_rows, cols, order, col_ref, mixed_all, target_ref, mine_ref, other_ref)


def project_part(mixed_all, proj_ref, into_ref, channel, part):
    rows = mixed_all.shape[0] // (GROUP // LANES)
    at = pl.ds(pl.multiple_of(part * rows, 16), rows)
    into_ref[at, :] = dot_nn(mixed_all[at, :], proj_ref[:, pl.ds(channel, GROUP)])


def back_kernel(
    head_size, tile, first_channel,
    col_ref, u_ref, v_ref, side_ref, twin_ref, next_ref, corner_ref, mixed_all, proj_ref, taps_ref,
    front_target, front_taps, carry_ref,
    merged_ref, target_ref, grad_ref, mine_ref, other_ref,
    field_ref, slope_ref, upside_ref, projected_a, projected_b, tapsum_ref, partial_ref,
):
    tokens, width = v_ref.shape
    blocks = width // LANES
    half_blocks = blocks // 2
    span = width - first_channel
    tapsum_ref[...] = jnp.zeros(tapsum_ref.shape, f32)

    def grad_part(part):
        rows = width // (GROUP // LANES)
        at = pl.ds(pl.multiple_of(part * rows, LANES), rows)
        partial_ref[:, at] = dot_nt(front_target[...], proj_ref[at, pl.ds(0, first_channel)])

    steps = span // GROUP
    source = carry_ref
    for step in range(steps):
        into = (projected_a, projected_b)[step % 2]
        if step == steps - 1:
            beside = grad_part
        else:
            beside = functools.partial(
                project_part, mixed_all, proj_ref, into, first_channel + (step + 1) * GROUP
            )
        stencil_chunk(
            step, tile, col_ref, u_ref, side_ref, twin_ref, next_ref, corner_ref, taps_ref,
            merged_ref, target_ref, tapsum_ref, field_ref, slope_ref, source, upside_ref, first_channel, beside,
        )
        source = into
    grad_ref[...] = (
        partial_ref[...] + dot_nt(target_ref[...], proj_ref[:, pl.ds(first_channel, span)])
    ).astype(bf16)
    for g in range(width // GROUP):
        at = pl.ds(g * GROUP, GROUP)
        square = dot_tn(grad_ref[:, at], v_ref[:, at])
        for p in range(GROUP // LANES):
            cut = slice(p * LANES, (p + 1) * LANES)
            block = g * (GROUP // LANES) + p
            h, inner = divmod(block, half_blocks)
            packed_rows = pack_diagonal(square[cut, cut], head_size)
            if block * LANES < first_channel:
                tap_rows = front_taps[:, pl.ds(block * LANES, LANES)]
            else:
                tap_rows = tapsum_ref[:, pl.ds(block * LANES - first_channel, LANES)]

            def put(ref, inner=inner, packed_rows=packed_rows, tap_rows=tap_rows):
                ref[pl.ds(inner * head_size, head_size), :] = packed_rows.astype(ref.dtype)
                ref[pl.ds(half_blocks * head_size + inner * 16, 16), :] = tap_rows.astype(ref.dtype)

            @pl.when(col_ref[0] == h)
            def _():
                put(mine_ref)

            @pl.when(col_ref[0] != h)
            def _():
                put(other_ref)


def stencil_scratch(tile):
    ring = tile[1] + RIM
    return [
        pltpu.VMEM((tile[0] + 4, ring, LANES), f32),
        pltpu.VMEM((tile[0] + 2, ring, LANES), f32),
        pltpu.VMEM(((tile[0] + 2) * ring, GROUP), f32),
        pltpu.VMEM(((tile[0] + 4) * ring, GROUP), f32),
        pltpu.VMEM(((tile[0] + 4) * ring, GROUP), f32),
    ]


def front_call(col, sharp, own, far, v, u, halo, proj, taps, tile, head_size, piece_rows, cols, order):
    tokens, width = v.shape
    ring = tile[1] + RIM
    span = width // 2
    grams = width // LANES * head_size
    sds = jax.ShapeDtypeStruct
    outs = [
        sds((tokens, span), bf16),
        sds((grams, LANES), f32),
        sds((grams, LANES), f32),
        sds((grams, LANES), f32),
        sds((width, GROUP), bf16),
        sds(((tile[0] + 4) * ring, width), bf16),
        sds((tokens, span), bf16),
        sds((16, span), f32),
        sds((width // 2, span), f32),
        sds((width // 2, span), bf16),
        sds(((tile[0] + 4) * ring, GROUP), f32),
    ]
    args = (col, sharp, own, far, v, u, *halo, proj, taps)
    return pl.pallas_call(
        functools.partial(front_kernel, head_size, tile, piece_rows, cols, order),
        in_specs=[SCALAR] * 2 + [LOCAL] * (len(args) - 2),
        out_specs=[LOCAL] * len(outs),
        out_shape=outs,
        scratch_shapes=stencil_scratch(tile),
        compiler_params=params(),
        cost_estimate=cost(10),
        name="front",
    )(*args)


def back_call(col, u, v, halo, mixed_all, proj, taps, target, tapsum, carry, tile, head_size):
    tokens, width = v.shape
    span = width // 2
    lines = width // LANES // 2 * (head_size + 16)
    sds = jax.ShapeDtypeStruct
    outs = [
        sds((tokens, span), bf16),
        sds((tokens, span), bf16),
        sds((tokens, width), bf16),
        sds((lines, LANES), f32),
        sds((lines, LANES), bf16),
    ]
    args = (col, u, v, *halo, mixed_all, proj, taps, target, tapsum, carry)
    return pl.pallas_call(
        functools.partial(back_kernel, head_size, tile, span),
        in_specs=[SCALAR] + [LOCAL] * (len(args) - 1),
        out_specs=[LOCAL] * len(outs),
        out_shape=outs,
        scratch_shapes=stencil_scratch(tile)
        + [pltpu.VMEM((16, span), f32), pltpu.VMEM((tokens, width), f32)],
        compiler_params=params(),
        cost_estimate=cost(10),
        name="back",
    )(*args)


def projector_kernel(
    piece_rows, cols, order, here_ref, mixed_all, target_ref, after_ref, mine_ref, other_ref
):
    spread_product(piece_rows, cols, order, here_ref, mixed_all, target_ref, mine_ref, other_ref)


def projector_call(here, mixed_all, target, after, piece_rows, cols, order):
    width, span = mixed_all.shape[1], target.shape[1]
    sds = jax.ShapeDtypeStruct
    return pl.pallas_call(
        functools.partial(projector_kernel, piece_rows, cols, order),
        in_specs=[SCALAR, LOCAL, LOCAL, pl.BlockSpec(memory_space=pl.ANY)],
        out_specs=[LOCAL, LOCAL],
        out_shape=[sds((width // 2, span), f32), sds((width // 2, span), bf16)],
        compiler_params=params(),
        cost_estimate=cost(2),
        name="projector",
    )(here, mixed_all, target, after)


def content_kernel(grad_ref, block_ref, merged_front, merged_back, after_ref, out_ref, merged_ref):
    span = out_ref.shape[1]
    for g in range(span // GROUP):
        at = pl.ds(pl.multiple_of(pl.program_id(0) * span + g * GROUP, GROUP), GROUP)
        out_ref[:, pl.ds(g * GROUP, GROUP)] = dot_nn(grad_ref[:, at], block_ref[at, :]).astype(bf16)

    @pl.when(pl.program_id(0) == 0)
    def _():
        merged_ref[...] = merged_front[...]

    @pl.when(pl.program_id(0) != 0)
    def _():
        merged_ref[...] = merged_back[...]


def content_call(grad, block, merged_front, merged_back, after):
    tokens, width = grad.shape
    half = pl.BlockSpec((tokens, width // 2), lambda i: (0, i))
    out = jax.ShapeDtypeStruct((tokens, width), bf16)
    return pl.pallas_call(
        content_kernel,
        grid=(2,),
        in_specs=[LOCAL] * 4 + [pl.BlockSpec(memory_space=pl.ANY)],
        out_specs=[half, half],
        out_shape=[out, out],
        compiler_params=params(),
        cost_estimate=cost(2),
        name="content",
    )(grad, block, merged_front, merged_back, after)


def final_kernel(
    head_size,
    col_ref,
    sharp_ref,
    own_ref,
    far_ref,
    energy_own_ref,
    energy_far_ref,
    attn_ref,
    gram_ref,
    scale_ref,
    q_ref,
    k_ref,
    dq_ref,
    dk_ref,
    heat_ref,
    taps_ref,
    mixer_ref,
):
    half = pl.program_id(0)
    groups = dq_ref.shape[1] // GROUP
    packed = LANES // head_size
    per = GROUP // LANES
    half_blocks = groups * per
    mine = half == col_ref[0]
    owner = lane_head(head_size)
    row = lax.broadcasted_iota(jnp.int32, (head_size, LANES), 0)
    lane = lax.broadcasted_iota(jnp.int32, (head_size, LANES), 1)
    mixer_ref[...] = jnp.zeros(mixer_ref.shape, bf16)
    q_terms, k_terms = [], []

    def take(own, far, at, size):
        return jnp.where(mine, own[pl.ds(at, size), :], far[pl.ds(at, size), :])

    for inner in range(half_blocks):
        block = half * half_blocks + inner
        p = inner % per
        grad = take(own_ref, far_ref, inner * head_size, head_size)
        taps_ref[:, pl.ds(inner * LANES, LANES)] = take(
            own_ref, far_ref, half_blocks * head_size + inner * 16, 16
        )[:9]
        q_line = take(energy_own_ref, energy_far_ref, half_blocks * head_size + inner, 1)
        k_line = take(energy_own_ref, energy_far_ref, half_blocks * head_size + 8 + inner, 1)
        at = pl.ds(pl.multiple_of(block * head_size, head_size), head_size)
        attention, gram, scale = attn_ref[at, :], gram_ref[at, :], scale_ref[at, :]
        scores = attention * (grad - sum_in_head(attention * grad, owner, packed))
        heated = scores * gram
        heat = by_head(
            [jnp.full(scores.shape, sharp_ref[block * packed + k], f32) for k in range(packed)], owner
        )
        for k in range(packed):
            heat_ref[block * packed + k] = jnp.sum(jnp.where(owner == k, heated, 0.0))
        gram_grad = heat * scores
        corr = gram_grad * gram
        k_corr = jnp.sum(corr, axis=0, keepdims=True)
        columns = sum_in_head(corr, owner, packed)
        q_corr = jnp.sum(jnp.where(lane == row + owner * head_size, columns, 0.0), axis=0, keepdims=True)
        q_scale = lax.rsqrt(q_line + epsilon)
        k_scale = lax.rsqrt(k_line + epsilon)
        q_terms.append(q_scale * q_scale * q_corr)
        k_terms.append(k_scale * k_scale * k_corr)
        low = (scale * gram_grad).astype(bf16)
        for k in range(packed):
            mixer_ref[pl.ds(inner * LANES + k * head_size, head_size), pl.ds(p * LANES, LANES)] = jnp.where(
                owner == k, low, jnp.zeros_like(low)
            )
    for g in range(groups):
        here = pl.ds(pl.multiple_of((half * groups + g) * GROUP, GROUP), GROUP)
        at = pl.ds(g * GROUP, GROUP)
        q, k = q_ref[:, here], k_ref[:, here]
        mixer = mixer_ref[at, :]
        q_term = jnp.concatenate(q_terms[g * per : (g + 1) * per], axis=1)
        k_term = jnp.concatenate(k_terms[g * per : (g + 1) * per], axis=1)
        dq_ref[:, at] = (dot_nt(k, mixer) - q.astype(f32) * q_term).astype(bf16)
        dk_ref[:, at] = (dot_nn(q, mixer) - k.astype(f32) * k_term).astype(bf16)


def final_call(col, sharp, own, far, energy_own, energy_far, attn, gram, scale, q, k, head_size):
    tokens, width = q.shape
    sds = jax.ShapeDtypeStruct
    token_block = pl.BlockSpec((tokens, width // 2), lambda i: (0, i))
    args = (col, sharp, own, far, energy_own, energy_far, attn, gram, scale, q, k)
    return pl.pallas_call(
        functools.partial(final_kernel, head_size),
        grid=(2,),
        in_specs=[SCALAR, SCALAR] + [LOCAL] * 9,
        out_specs=[
            token_block,
            token_block,
            SCALAR,
            pl.BlockSpec((9, width // 2), lambda i: (0, i)),
        ],
        out_shape=[
            sds((tokens, width), bf16),
            sds((tokens, width), bf16),
            sds(sharp.shape, f32),
            sds((9, width), f32),
        ],
        scratch_shapes=[pltpu.VMEM((width // 2, GROUP), bf16)],
        compiler_params=params(),
        cost_estimate=cost(5),
        name="final",
    )(*args)


def swap(x, axis, bit):
    return lax.ppermute(x, axis, [(i, i ^ bit) for i in range(lax.axis_size(axis))])


def row_bits():
    bits, bit = [], 1
    while bit < lax.axis_size("row"):
        bits.append(bit)
        bit *= 2
    return bits


def halve(total):
    half = total.shape[0] // 2
    return total[:half], total[half:].astype(bf16)


def add_low(total, got):
    return total + got.astype(f32)


def add_step(total, axis, bit):
    low = total.astype(bf16)
    return low.astype(f32) + swap(low, axis, bit).astype(f32)


def scatter_step(total, group):
    count = 2 ** len(group)
    rows = total.shape[0] // count
    out = total[:rows]
    for k in range(1, count):
        mask = sum(bit for i, bit in enumerate(group) if (k >> (len(group) - 1 - i)) & 1)
        out = add_low(out, swap(total[k * rows : (k + 1) * rows].astype(bf16), "row", mask))
    return out


def scatter_both(first, second, group):
    early, late = group
    quarter, half = first.shape[0] // 4, second.shape[0] // 2
    pieces = [first[k * quarter : (k + 1) * quarter] for k in range(4)]
    joint = swap(jnp.concatenate([pieces[1], second[half:]]).astype(bf16), "row", late)
    first = add_low(pieces[0], swap(pieces[2].astype(bf16), "row", early))
    first = add_low(first, swap(pieces[3].astype(bf16), "row", early | late))
    return add_low(first, joint[:quarter]), add_low(second[:half], joint[quarter:])


def tie(*values):
    return lax.optimization_barrier(values)


def shards(q, k, v, u, sharp, proj, taps):
    tile = v.shape[:2]
    width = v.shape[2]
    tokens = tile[0] * tile[1]
    head_size = width // sharp.shape[0]
    rows, cols = lax.axis_size("row"), lax.axis_size("col")
    flat = lambda x: x.reshape(tokens, width)
    here = jnp.stack([lax.axis_index("col"), lax.axis_index("row")]).astype(jnp.int32)
    q2, k2, v2, u2 = flat(q), flat(k), flat(v), flat(u)
    bits = row_bits()
    early = [("row", bits[0]), ("col", 1)] + [("row", bit) for bit in bits[1:]]
    late = [("col", 1)] + [("row", bit) for bit in bits]
    piece_rows = width // (rows * cols)

    mine, other = gram_call(q2, k2, head_size)
    to_twin, to_next = edges_call(here, v, u)
    total = add_low(mine, swap(other, "col", 1))
    start = jnp.where(lax.axis_index("col") == 0, v.shape[1] - RIM, 0)
    edge = lambda x: lax.dynamic_slice_in_dim(x, start, RIM, axis=1)
    pairs_next = [(j, j + 1) for j in range(1, rows - 1, 2)]
    pairs_next = pairs_next + [(b, a) for a, b in pairs_next]
    side = swap(jnp.concatenate([edge(v), edge(u)]), "col", 1)
    for i, bit in enumerate(bits[:1] + bits[2:] + bits[1:2]):
        total = total + swap(total, "row", bit)
        if i == 2:
            from_twin = swap(to_twin, "row", 1)
            total, from_twin = tie(total, from_twin)
        if i == 2:
            from_next = lax.ppermute(to_next, "row", pairs_next)
            total, from_next = tie(total, from_next)
    corner = swap(
        edge(jnp.concatenate([from_twin[:2], from_next[:2], from_twin[2:], from_next[2:]])), "col", 1
    )
    around = tuple(x.reshape(-1, width) for x in (side, from_twin, from_next, corner))
    energy_own, energy_far = total, swap(total, "col", 1)

    (merged_front, attn, gram, scale, block, mixed_all, front_target, front_taps, mine, other, carry) = front_call(
        here, sharp, energy_own, energy_far, v2, u2, around, proj, taps, tile, head_size, piece_rows, cols, early
    )
    halves = [swap(x, "row", bits[0]) for x in jnp.split(other, 2)]
    first = halves[:1]
    front_mine = mine
    merged_back, target, grad, mine, other = back_call(
        here, u2, v2, around, mixed_all, proj, taps, front_target, front_taps, carry, tile, head_size
    )

    mine, other, *first = tie(mine, other, *first)
    after = swap(other, "col", 1)
    total = add_low(mine, after)
    turns = bits[1:2] + bits[:1] + bits[2:]
    back_mine, back_other = projector_call(here, mixed_all, target, after, piece_rows, cols, late)
    front_sum = add_low(front_mine, jnp.concatenate([*first, *halves[1:]]))
    back_sum = add_low(back_mine, swap(back_other, "col", 1))
    total = add_step(total, "row", turns[0])
    total, back_sum = tie(total, back_sum)
    total = add_step(total, "row", turns[1])
    total, front_sum = tie(total, front_sum)
    for bit in turns[2:]:
        total = add_step(total, "row", bit)
    front_sum, leaves = halve(front_sum)
    front_sum = add_low(front_sum, swap(leaves, "col", 1))
    back_sum = scatter_step(back_sum, bits[:2])
    front_sum = scatter_step(front_sum, bits[1:2])
    total, back_sum = tie(total, back_sum)
    for bit in bits[2:-1]:
        front_sum, back_sum = scatter_step(front_sum, [bit]), scatter_step(back_sum, [bit])
    far = swap(total, "col", 1)
    kept, leaves = zip(halve(front_sum), halve(back_sum))
    got = swap(jnp.concatenate(leaves), "row", bits[-1])
    dq, dk, heat, tap_sums = final_call(
        here, sharp, total, far, energy_own, energy_far, attn, gram, scale, q2, k2, head_size
    )
    content, merged = content_call(grad, block, merged_front, merged_back, tap_sums)
    content, *kept = tie(content, *kept)
    front_sum, back_sum = (add_low(x, y) for x, y in zip(kept, jnp.split(got, 2)))
    projector = jnp.concatenate([front_sum, back_sum], axis=1)
    full = lambda x: x.reshape(tile + (width,))
    return full(merged), full(dq), full(dk), full(content), heat, tap_sums, projector


def solution(mesh):
    field = P(("scene", "row"), "col", None)
    return jax.shard_map(
        shards,
        mesh=mesh,
        in_specs=(field, field, field, field, P(), P(), P()),
        out_specs=(
            field,
            field,
            field,
            field,
            P("scene"),
            P("scene", None),
            P(("scene", "row", "col"), None),
        ),
        check_vma=False,
    )
```

```python
import functools

import jax
import jax.numpy as jnp
from jax import lax
from jax.experimental import pallas as pl
from jax.experimental.pallas import tpu as pltpu
from jax.sharding import PartitionSpec as P

epsilon = 1e-06
inverse_root = 0.7071067811865476
density_root = 0.3989422804014327
LANES = 128
GROUP = 256
RIM = 8
f32 = jnp.float32
bf16 = jnp.bfloat16
VMEM_LIMIT = 24 * 1024 * 1024


def whole(shape):
    return pl.BlockSpec(shape, lambda *_: (0,) * len(shape))


SCALAR = pl.BlockSpec(memory_space=pltpu.SMEM)
LOCAL = pl.BlockSpec(memory_space=pltpu.VMEM)


def params(limit=VMEM_LIMIT):
    return pltpu.CompilerParams(vmem_limit_bytes=limit)


def cost(microseconds):
    return pl.CostEstimate(flops=0, bytes_accessed=int(microseconds * 3.6e6), transcendentals=0)


def pad_lines(lines, count):
    blank = jnp.zeros((count - len(lines), LANES), f32)
    return jnp.concatenate(lines + [blank], axis=0) if count > len(lines) else jnp.concatenate(lines, axis=0)


def dot_tn(a, b):
    return lax.dot_general(a, b, (((0,), (0,)), ((), ())), preferred_element_type=f32)


def dot_nt(a, b):
    return lax.dot_general(a, b, (((1,), (1,)), ((), ())), preferred_element_type=f32)


def dot_nn(a, b):
    return jnp.dot(a, b, preferred_element_type=f32)


def lane_head(head_size):
    return lax.broadcasted_iota(jnp.int32, (head_size, LANES), 1) // head_size


def by_head(parts, owner):
    out = parts[0]
    for k in range(1, len(parts)):
        out = jnp.where(owner == k, parts[k], out)
    return out


def pack_diagonal(square, head_size):
    owner = lane_head(head_size)
    return by_head(
        [square[k * head_size : (k + 1) * head_size] for k in range(LANES // head_size)], owner
    )


def sum_in_head(values, owner, packed):
    sums = [jnp.sum(jnp.where(owner == k, values, 0.0), axis=1, keepdims=True) for k in range(packed)]
    return by_head([jnp.broadcast_to(s, values.shape) for s in sums], owner)


def edges_kernel(here_ref, v_head, v_tail, u_head, u_tail, twin_ref, next_ref):
    even = lax.rem(here_ref[1], 2) == 0

    def put(tail_ref, head_ref):
        tail_ref[:2] = v_tail[...]
        tail_ref[2:] = u_tail[...]
        head_ref[:2] = v_head[...]
        head_ref[2:] = u_head[...]

    @pl.when(even)
    def _():
        put(twin_ref, next_ref)

    @pl.when(jnp.logical_not(even))
    def _():
        put(next_ref, twin_ref)


def edges_call(here, v, u):
    rows, cols, width = v.shape
    out = jax.ShapeDtypeStruct((3, cols, width), bf16)
    return pl.pallas_call(
        edges_kernel,
        grid=(1,),
        in_specs=[
            SCALAR,
            pl.BlockSpec((2, cols, width), lambda i: (0, 0, 0)),
            pl.BlockSpec((2, cols, width), lambda i: (rows // 2 - 1, 0, 0)),
            pl.BlockSpec((1, cols, width), lambda i: (0, 0, 0)),
            pl.BlockSpec((1, cols, width), lambda i: (rows - 1, 0, 0)),
        ],
        out_specs=[LOCAL, LOCAL],
        out_shape=[out, out],
        compiler_params=params(),
        cost_estimate=cost(1),
        name="edges",
    )(here, v, v, u, u)


def gram_kernel(head_size, q_ref, k_ref, mine_ref, other_ref):
    half = pl.program_id(0)
    per = GROUP // LANES
    energy = mine_ref.shape[0] - 16
    values = []
    for g in range(q_ref.shape[1] // GROUP):
        at = pl.ds(g * GROUP, GROUP)
        square = dot_tn(q_ref[:, at], k_ref[:, at])
        for p in range(per):
            cut = slice(p * LANES, (p + 1) * LANES)
            block = g * per + p
            values.append((block * head_size, pack_diagonal(square[cut, cut], head_size)))
            for line, ref in ((energy, q_ref), (energy + 8, k_ref)):
                x = ref[:, pl.ds(block * LANES, LANES)].astype(f32)
                values.append((line + block, jnp.sum(x * x, axis=0, keepdims=True)))

    def put(ref):
        for at, value in values:
            ref[pl.ds(at, value.shape[0]), :] = value

    @pl.when(half == 0)
    def _():
        mine_ref[pl.ds(energy, 16), :] = jnp.zeros((16, LANES), f32)
        other_ref[pl.ds(energy, 16), :] = jnp.zeros((16, LANES), f32)

    col = lax.axis_index("col")

    @pl.when(half == col)
    def _():
        put(mine_ref)

    @pl.when(half != col)
    def _():
        put(other_ref)


def gram_call(q, k, head_size):
    tokens, width = q.shape
    lines = width // 2 // LANES * head_size + 16
    out = jax.ShapeDtypeStruct((lines, LANES), f32)
    return pl.pallas_call(
        functools.partial(gram_kernel, head_size),
        grid=(2,),
        in_specs=[
            pl.BlockSpec((tokens, width // 2), lambda i: (0, i)),
            pl.BlockSpec((tokens, width // 2), lambda i: (0, i)),
        ],
        out_specs=[LOCAL, LOCAL],
        out_shape=[out, out],
        compiler_params=params(48 * 1024 * 1024),
        cost_estimate=cost(2.5),
        name="gram",
    )(q, k)


def gelu_terms(u):
    cumul = 0.5 * (1.0 + lax.erf(u * inverse_root))
    return u * cumul, cumul + u * jnp.exp(-0.5 * u * u) * density_root


def attention_block(head_size, raw, q_line, k_line, sharp):
    packed = LANES // head_size
    owner = lane_head(head_size)
    row = lax.broadcasted_iota(jnp.int32, (head_size, LANES), 0)
    lane = lax.broadcasted_iota(jnp.int32, (head_size, LANES), 1)
    q_energy = by_head(
        [
            jnp.broadcast_to(
                jnp.sum(jnp.where(lane == row + k * head_size, q_line, 0.0), axis=1, keepdims=True),
                raw.shape,
            )
            for k in range(packed)
        ],
        owner,
    )
    q_scale = lax.rsqrt(q_energy + epsilon)
    k_scale = lax.rsqrt(k_line + epsilon)
    gram = q_scale * raw * k_scale
    heat = by_head([jnp.full(raw.shape, s, f32) for s in sharp], owner)
    numer = jnp.exp(heat * gram)
    attention = numer / sum_in_head(numer, owner, packed)
    return attention, gram, q_scale * k_scale


def attention_phase(
    head_size, col_ref, sharp_ref, own_ref, far_ref, attn_ref, gram_ref, scale_ref, block_ref
):
    packed = LANES // head_size
    blocks = attn_ref.shape[0] // head_size
    half_blocks = blocks // 2
    is_first = col_ref[0] == 0
    block_ref[...] = jnp.zeros(block_ref.shape, bf16)
    owner = lane_head(head_size)
    for p in range(blocks):
        h, inner = divmod(p, half_blocks)

        def take(at, size):
            a = own_ref[pl.ds(at, size), :]
            b = far_ref[pl.ds(at, size), :]
            return jnp.where(is_first, a, b) if h == 0 else jnp.where(is_first, b, a)

        raw = take(inner * head_size, head_size)
        q_line = take(half_blocks * head_size + inner, 1)
        k_line = take(half_blocks * head_size + 8 + inner, 1)
        attention, gram, scale = attention_block(
            head_size, raw, q_line, k_line, [sharp_ref[p * packed + k] for k in range(packed)]
        )
        at = pl.ds(p * head_size, head_size)
        attn_ref[at, :] = attention
        gram_ref[at, :] = gram
        scale_ref[at, :] = scale
        low = attention.astype(bf16)
        inside = (p * LANES) % GROUP
        for k in range(packed):
            block_ref[pl.ds(p * LANES + k * head_size, head_size), pl.ds(inside, LANES)] = jnp.where(
                owner == k, low, jnp.zeros_like(low)
            )


def keep_side(col_ref, shape):
    place = lax.rem(lax.broadcasted_iota(jnp.int32, shape, 0), RIM)
    second = col_ref[0].astype(f32)
    right = jnp.where(place < 2, 1.0, 0.0)
    left = jnp.where(place >= RIM - 2, 1.0, 0.0)
    return right + second * (left - right)


def stencil_chunk(
    step, tile, col_ref, u_ref, side_ref, twin_ref, next_ref, corner_ref, taps_ref,
    merged_ref, target_ref, tapsum_ref, field_ref, slope_ref, projected_ref, upside_ref,
    first_channel, beside,
):
    tile_rows, tile_cols = tile
    tokens = tile_rows * tile_cols
    ring = tile_cols + RIM
    side = tile_rows * RIM
    chunk = pl.ds(first_channel + step * GROUP, GROUP)
    for at, size, ref, start in (
        (0, side, side_ref, side),
        (side, tile_cols, twin_ref, 2 * tile_cols),
        (side + tile_cols, tile_cols, next_ref, 2 * tile_cols),
        (side + 2 * tile_cols, 2 * RIM, corner_ref, 4 * RIM),
    ):
        piece = ref[pl.ds(start, size), chunk].astype(f32)
        if ref is side_ref or ref is corner_ref:
            piece = piece * keep_side(col_ref, piece.shape)
        upside_ref[pl.ds(at, size), :] = piece

    def lanes_body(part, carry):
        lanes = pl.ds(pl.multiple_of(part * LANES, LANES), LANES)
        glob = pl.ds(pl.multiple_of(first_channel + step * GROUP + part * LANES, LANES), LANES)
        away = pl.ds(pl.multiple_of(step * GROUP + part * LANES, LANES), LANES)
        taps = [taps_ref[pl.ds(t, 1), glob] for t in range(9)]
        rim = tokens + side
        from_next = 1 - lax.rem(col_ref[1], 2)
        beside(part)

        def ring_row(r):
            if 0 <= r < tile_rows:
                pieces = (r * tile_cols, tokens + r * RIM)
            else:
                k = r + 2 if r < 0 else r - tile_rows
                k = k + 2 * (from_next if r < 0 else 1 - from_next)
                pieces = (
                    pl.multiple_of(rim + k * tile_cols, RIM),
                    pl.multiple_of(rim + 4 * tile_cols + k * RIM, RIM),
                )
            return jnp.concatenate(
                [
                    projected_ref[pl.ds(pieces[0], tile_cols), lanes],
                    projected_ref[pl.ds(pieces[1], RIM), lanes],
                ],
                axis=0,
            )

        def up_row(r):
            if 0 <= r < tile_rows:
                return jnp.concatenate(
                    [
                        u_ref[pl.ds(r * tile_cols, tile_cols), glob].astype(f32),
                        upside_ref[pl.ds(r * RIM, RIM), lanes],
                    ],
                    axis=0,
                )
            k = from_next if r < 0 else 1 - from_next
            pieces = (
                pl.multiple_of(side + k * tile_cols, RIM),
                pl.multiple_of(side + 2 * tile_cols + k * RIM, RIM),
            )
            return jnp.concatenate(
                [
                    upside_ref[pl.ds(pieces[0], tile_cols), lanes],
                    upside_ref[pl.ds(pieces[1], RIM), lanes],
                ],
                axis=0,
            )

        for r in range(-2, tile_rows + 2):
            field_ref[r + 2] = ring_row(r).astype(bf16).astype(f32)
        for r in range(-1, tile_rows + 1):
            near = [field_ref[r + 1 + a] for a in range(3)]
            sums = [sum(taps[3 * a + b] * near[a] for a in range(3)) for b in range(3)]
            total = pltpu.roll(sums[0], 1, 0) + sums[1] + pltpu.roll(sums[2], ring - 1, 0)
            active, slope = gelu_terms(total)
            slope_ref[r + 1] = (up_row(r) * slope).astype(bf16).astype(f32)
            if 0 <= r < tile_rows:
                at = pl.ds(r * tile_cols, tile_cols)
                merged_ref[at, away] = (projected_ref[at, lanes] + active[:tile_cols]).astype(bf16)
        weights = [jnp.zeros((8, LANES), f32) for _ in range(9)]
        blank = jnp.zeros((RIM, LANES), f32)
        for r in range(tile_rows):
            near = [slope_ref[r + 2 - a] for a in range(3)]
            sums = [sum(taps[3 * a + b] * near[a] for a in range(3)) for b in range(3)]
            back = pltpu.roll(sums[0], ring - 1, 0) + sums[1] + pltpu.roll(sums[2], 1, 0)
            at = pl.ds(r * tile_cols, tile_cols)
            target_ref[at, away] = (u_ref[at, glob].astype(f32) + back[:tile_cols]).astype(bf16)
            centre = jnp.concatenate([near[1][:tile_cols], blank], axis=0)
            shifted = [pltpu.roll(centre, ring - 1, 0), centre, pltpu.roll(centre, 1, 0)]
            for a in range(3):
                line = field_ref[r + 1 + a]
                for b in range(3):
                    product = shifted[b] * line
                    weights[3 * a + b] = weights[3 * a + b] + jnp.sum(
                        product.reshape(ring // 8, 8, LANES), axis=0
                    )
        for t in range(9):
            tapsum_ref[pl.ds(t, 1), away] = jnp.sum(weights[t], axis=0, keepdims=True)
        return carry

    lax.fori_loop(0, GROUP // LANES, lanes_body, 0)


def spread_product(piece_rows, cols, order, here_ref, mixed_all, target_ref, mine_ref, other_ref):
    tokens = target_ref.shape[0]
    axis, bit = order[0]
    apart = bit if axis == "col" else bit * cols
    index = {"col": here_ref[0], "row": here_ref[1]}
    flipped = (index[axis] // bit) % 2 == 1
    per = GROUP // piece_rows
    for g in range(mixed_all.shape[1] // GROUP):
        product = dot_tn(mixed_all[pl.ds(0, tokens), pl.ds(g * GROUP, GROUP)], target_ref[...])
        for k in range(per):
            if k & apart:
                continue
            owner = g * per + k
            a, b = (product[x * piece_rows : (x + 1) * piece_rows] for x in (k, k | apart))
            away = {"col": (owner % cols) ^ index["col"], "row": (owner // cols) ^ index["row"]}
            place = 0
            for name, digit in order[1:]:
                place = 2 * place + (away[name] // digit) % 2
            at = pl.ds(pl.multiple_of(place * piece_rows, piece_rows), piece_rows)
            mine_ref[at, :] = jnp.where(flipped, b, a)
            other_ref[at, :] = jnp.where(flipped, a, b).astype(bf16)


def front_kernel(
    head_size, tile, piece_rows, cols, order,
    col_ref, sharp_ref, own_ref, far_ref, v_ref, u_ref, side_ref, twin_ref, next_ref,
    corner_ref, proj_ref, taps_ref,
    merged_ref, attn_ref, gram_ref, scale_ref, block_ref, mixed_all, target_ref, tapsum_ref,
    mine_ref, other_ref, carry_ref,
    field_ref, slope_ref, upside_ref, *projected,
):
    tile_rows, tile_cols = tile
    tokens, width = v_ref.shape
    side = tile_rows * RIM
    two = 2 * tile_cols

    tapsum_ref[...] = jnp.zeros(tapsum_ref.shape, f32)
    attention_phase(
        head_size, col_ref, sharp_ref, own_ref, far_ref, attn_ref, gram_ref, scale_ref, block_ref
    )
    for g in range(width // GROUP):
        at = pl.ds(g * GROUP, GROUP)
        weights = block_ref[at, :]
        mixed_all[pl.ds(0, tokens), at] = dot_nt(v_ref[:, at], weights).astype(bf16)
        around = [(side_ref, side), (twin_ref, two), (next_ref, two), (corner_ref, 4 * RIM)]
        value = dot_nt(
            jnp.concatenate([ref[pl.ds(0, size), at] for ref, size in around], axis=0), weights
        )
        start = 0
        for ref, size in around:
            piece = value[start : start + size]
            if ref is side_ref or ref is corner_ref:
                piece = piece * keep_side(col_ref, piece.shape)
            mixed_all[pl.ds(tokens + start, size), at] = piece.astype(bf16)
            start += size

    steps = target_ref.shape[1] // GROUP
    projected[0][...] = dot_nn(mixed_all[...], proj_ref[:, pl.ds(0, GROUP)])
    for step in range(steps):
        into = carry_ref if step == steps - 1 else projected[(step + 1) % 2]
        stencil_chunk(
            step, tile, col_ref, u_ref, side_ref, twin_ref, next_ref, corner_ref, taps_ref,
            merged_ref, target_ref, tapsum_ref, field_ref, slope_ref, projected[step % 2], upside_ref, 0,
            functools.partial(project_part, mixed_all, proj_ref, into, (step + 1) * GROUP),
        )
    spread_product(piece_rows, cols, order, col_ref, mixed_all, target_ref, mine_ref, other_ref)


def project_part(mixed_all, proj_ref, into_ref, channel, part):
    rows = mixed_all.shape[0] // (GROUP // LANES)
    at = pl.ds(pl.multiple_of(part * rows, 16), rows)
    into_ref[at, :] = dot_nn(mixed_all[at, :], proj_ref[:, pl.ds(channel, GROUP)])


def back_kernel(
    head_size, tile, first_channel,
    col_ref, u_ref, v_ref, side_ref, twin_ref, next_ref, corner_ref, mixed_all, proj_ref, taps_ref,
    front_target, front_taps, carry_ref,
    merged_ref, target_ref, grad_ref, mine_ref, other_ref,
    field_ref, slope_ref, upside_ref, projected_a, projected_b, tapsum_ref, partial_ref,
):
    tokens, width = v_ref.shape
    blocks = width // LANES
    half_blocks = blocks // 2
    span = width - first_channel
    tapsum_ref[...] = jnp.zeros(tapsum_ref.shape, f32)

    def grad_part(part):
        rows = width // (GROUP // LANES)
        at = pl.ds(pl.multiple_of(part * rows, LANES), rows)
        partial_ref[:, at] = dot_nt(front_target[...], proj_ref[at, pl.ds(0, first_channel)])

    steps = span // GROUP
    source = carry_ref
    for step in range(steps):
        into = (projected_a, projected_b)[step % 2]
        if step == steps - 1:
            beside = grad_part
        else:
            beside = functools.partial(
                project_part, mixed_all, proj_ref, into, first_channel + (step + 1) * GROUP
            )
        stencil_chunk(
            step, tile, col_ref, u_ref, side_ref, twin_ref, next_ref, corner_ref, taps_ref,
            merged_ref, target_ref, tapsum_ref, field_ref, slope_ref, source, upside_ref, first_channel, beside,
        )
        source = into
    grad_ref[...] = (
        partial_ref[...] + dot_nt(target_ref[...], proj_ref[:, pl.ds(first_channel, span)])
    ).astype(bf16)
    for g in range(width // GROUP):
        at = pl.ds(g * GROUP, GROUP)
        square = dot_tn(grad_ref[:, at], v_ref[:, at])
        for p in range(GROUP // LANES):
            cut = slice(p * LANES, (p + 1) * LANES)
            block = g * (GROUP // LANES) + p
            h, inner = divmod(block, half_blocks)
            packed_rows = pack_diagonal(square[cut, cut], head_size)
            if block * LANES < first_channel:
                tap_rows = front_taps[:, pl.ds(block * LANES, LANES)]
            else:
                tap_rows = tapsum_ref[:, pl.ds(block * LANES - first_channel, LANES)]

            def put(ref, inner=inner, packed_rows=packed_rows, tap_rows=tap_rows):
                ref[pl.ds(inner * head_size, head_size), :] = packed_rows.astype(ref.dtype)
                ref[pl.ds(half_blocks * head_size + inner * 16, 16), :] = tap_rows.astype(ref.dtype)

            @pl.when(col_ref[0] == h)
            def _():
                put(mine_ref)

            @pl.when(col_ref[0] != h)
            def _():
                put(other_ref)


def stencil_scratch(tile):
    ring = tile[1] + RIM
    return [
        pltpu.VMEM((tile[0] + 4, ring, LANES), f32),
        pltpu.VMEM((tile[0] + 2, ring, LANES), f32),
        pltpu.VMEM(((tile[0] + 2) * ring, GROUP), f32),
        pltpu.VMEM(((tile[0] + 4) * ring, GROUP), f32),
        pltpu.VMEM(((tile[0] + 4) * ring, GROUP), f32),
    ]


def front_call(col, sharp, own, far, v, u, halo, proj, taps, tile, head_size, piece_rows, cols, order):
    tokens, width = v.shape
    ring = tile[1] + RIM
    span = width // 2
    grams = width // LANES * head_size
    sds = jax.ShapeDtypeStruct
    outs = [
        sds((tokens, span), bf16),
        sds((grams, LANES), f32),
        sds((grams, LANES), f32),
        sds((grams, LANES), f32),
        sds((width, GROUP), bf16),
        sds(((tile[0] + 4) * ring, width), bf16),
        sds((tokens, span), bf16),
        sds((16, span), f32),
        sds((width // 2, span), f32),
        sds((width // 2, span), bf16),
        sds(((tile[0] + 4) * ring, GROUP), f32),
    ]
    args = (col, sharp, own, far, v, u, *halo, proj, taps)
    return pl.pallas_call(
        functools.partial(front_kernel, head_size, tile, piece_rows, cols, order),
        in_specs=[SCALAR] * 2 + [LOCAL] * (len(args) - 2),
        out_specs=[LOCAL] * len(outs),
        out_shape=outs,
        scratch_shapes=stencil_scratch(tile),
        compiler_params=params(),
        cost_estimate=cost(10),
        name="front",
    )(*args)


def back_call(col, u, v, halo, mixed_all, proj, taps, target, tapsum, carry, tile, head_size):
    tokens, width = v.shape
    span = width // 2
    lines = width // LANES // 2 * (head_size + 16)
    sds = jax.ShapeDtypeStruct
    outs = [
        sds((tokens, span), bf16),
        sds((tokens, span), bf16),
        sds((tokens, width), bf16),
        sds((lines, LANES), f32),
        sds((lines, LANES), bf16),
    ]
    args = (col, u, v, *halo, mixed_all, proj, taps, target, tapsum, carry)
    return pl.pallas_call(
        functools.partial(back_kernel, head_size, tile, span),
        in_specs=[SCALAR] + [LOCAL] * (len(args) - 1),
        out_specs=[LOCAL] * len(outs),
        out_shape=outs,
        scratch_shapes=stencil_scratch(tile)
        + [pltpu.VMEM((16, span), f32), pltpu.VMEM((tokens, width), f32)],
        compiler_params=params(),
        cost_estimate=cost(10),
        name="back",
    )(*args)


def projector_kernel(
    piece_rows, cols, order, here_ref, mixed_all, target_ref, after_ref, mine_ref, other_ref
):
    spread_product(piece_rows, cols, order, here_ref, mixed_all, target_ref, mine_ref, other_ref)


def projector_call(here, mixed_all, target, after, piece_rows, cols, order):
    width, span = mixed_all.shape[1], target.shape[1]
    sds = jax.ShapeDtypeStruct
    return pl.pallas_call(
        functools.partial(projector_kernel, piece_rows, cols, order),
        in_specs=[SCALAR, LOCAL, LOCAL, pl.BlockSpec(memory_space=pl.ANY)],
        out_specs=[LOCAL, LOCAL],
        out_shape=[sds((width // 2, span), f32), sds((width // 2, span), bf16)],
        compiler_params=params(),
        cost_estimate=cost(2),
        name="projector",
    )(here, mixed_all, target, after)


def content_kernel(grad_ref, block_ref, merged_front, merged_back, after_ref, out_ref, merged_ref):
    span = out_ref.shape[1]
    for g in range(span // GROUP):
        at = pl.ds(pl.multiple_of(pl.program_id(0) * span + g * GROUP, GROUP), GROUP)
        out_ref[:, pl.ds(g * GROUP, GROUP)] = dot_nn(grad_ref[:, at], block_ref[at, :]).astype(bf16)

    @pl.when(pl.program_id(0) == 0)
    def _():
        merged_ref[...] = merged_front[...]

    @pl.when(pl.program_id(0) != 0)
    def _():
        merged_ref[...] = merged_back[...]


def content_call(grad, block, merged_front, merged_back, after):
    tokens, width = grad.shape
    half = pl.BlockSpec((tokens, width // 2), lambda i: (0, i))
    out = jax.ShapeDtypeStruct((tokens, width), bf16)
    return pl.pallas_call(
        content_kernel,
        grid=(2,),
        in_specs=[LOCAL] * 4 + [pl.BlockSpec(memory_space=pl.ANY)],
        out_specs=[half, half],
        out_shape=[out, out],
        compiler_params=params(),
        cost_estimate=cost(2),
        name="content",
    )(grad, block, merged_front, merged_back, after)


def final_kernel(
    head_size,
    col_ref,
    sharp_ref,
    own_ref,
    far_ref,
    energy_own_ref,
    energy_far_ref,
    attn_ref,
    gram_ref,
    scale_ref,
    q_ref,
    k_ref,
    dq_ref,
    dk_ref,
    heat_ref,
    taps_ref,
    mixer_ref,
):
    half = pl.program_id(0)
    groups = dq_ref.shape[1] // GROUP
    packed = LANES // head_size
    per = GROUP // LANES
    half_blocks = groups * per
    mine = half == col_ref[0]
    owner = lane_head(head_size)
    row = lax.broadcasted_iota(jnp.int32, (head_size, LANES), 0)
    lane = lax.broadcasted_iota(jnp.int32, (head_size, LANES), 1)
    mixer_ref[...] = jnp.zeros(mixer_ref.shape, bf16)
    q_terms, k_terms = [], []

    def take(own, far, at, size):
        return jnp.where(mine, own[pl.ds(at, size), :], far[pl.ds(at, size), :])

    for inner in range(half_blocks):
        block = half * half_blocks + inner
        p = inner % per
        grad = take(own_ref, far_ref, inner * head_size, head_size)
        taps_ref[:, pl.ds(inner * LANES, LANES)] = take(
            own_ref, far_ref, half_blocks * head_size + inner * 16, 16
        )[:9]
        q_line = take(energy_own_ref, energy_far_ref, half_blocks * head_size + inner, 1)
        k_line = take(energy_own_ref, energy_far_ref, half_blocks * head_size + 8 + inner, 1)
        at = pl.ds(pl.multiple_of(block * head_size, head_size), head_size)
        attention, gram, scale = attn_ref[at, :], gram_ref[at, :], scale_ref[at, :]
        scores = attention * (grad - sum_in_head(attention * grad, owner, packed))
        heated = scores * gram
        heat = by_head(
            [jnp.full(scores.shape, sharp_ref[block * packed + k], f32) for k in range(packed)], owner
        )
        for k in range(packed):
            heat_ref[block * packed + k] = jnp.sum(jnp.where(owner == k, heated, 0.0))
        gram_grad = heat * scores
        corr = gram_grad * gram
        k_corr = jnp.sum(corr, axis=0, keepdims=True)
        columns = sum_in_head(corr, owner, packed)
        q_corr = jnp.sum(jnp.where(lane == row + owner * head_size, columns, 0.0), axis=0, keepdims=True)
        q_scale = lax.rsqrt(q_line + epsilon)
        k_scale = lax.rsqrt(k_line + epsilon)
        q_terms.append(q_scale * q_scale * q_corr)
        k_terms.append(k_scale * k_scale * k_corr)
        low = (scale * gram_grad).astype(bf16)
        for k in range(packed):
            mixer_ref[pl.ds(inner * LANES + k * head_size, head_size), pl.ds(p * LANES, LANES)] = jnp.where(
                owner == k, low, jnp.zeros_like(low)
            )
    for g in range(groups):
        here = pl.ds(pl.multiple_of((half * groups + g) * GROUP, GROUP), GROUP)
        at = pl.ds(g * GROUP, GROUP)
        q, k = q_ref[:, here], k_ref[:, here]
        mixer = mixer_ref[at, :]
        q_term = jnp.concatenate(q_terms[g * per : (g + 1) * per], axis=1)
        k_term = jnp.concatenate(k_terms[g * per : (g + 1) * per], axis=1)
        dq_ref[:, at] = (dot_nt(k, mixer) - q.astype(f32) * q_term).astype(bf16)
        dk_ref[:, at] = (dot_nn(q, mixer) - k.astype(f32) * k_term).astype(bf16)


def final_call(col, sharp, own, far, energy_own, energy_far, attn, gram, scale, q, k, head_size):
    tokens, width = q.shape
    sds = jax.ShapeDtypeStruct
    token_block = pl.BlockSpec((tokens, width // 2), lambda i: (0, i))
    args = (col, sharp, own, far, energy_own, energy_far, attn, gram, scale, q, k)
    return pl.pallas_call(
        functools.partial(final_kernel, head_size),
        grid=(2,),
        in_specs=[SCALAR, SCALAR] + [LOCAL] * 9,
        out_specs=[
            token_block,
            token_block,
            SCALAR,
            pl.BlockSpec((9, width // 2), lambda i: (0, i)),
        ],
        out_shape=[
            sds((tokens, width), bf16),
            sds((tokens, width), bf16),
            sds(sharp.shape, f32),
            sds((9, width), f32),
        ],
        scratch_shapes=[pltpu.VMEM((width // 2, GROUP), bf16)],
        compiler_params=params(),
        cost_estimate=cost(5),
        name="final",
    )(*args)


def swap(x, axis, bit):
    return lax.ppermute(x, axis, [(i, i ^ bit) for i in range(lax.axis_size(axis))])


def row_bits():
    bits, bit = [], 1
    while bit < lax.axis_size("row"):
        bits.append(bit)
        bit *= 2
    return bits


def halve(total):
    half = total.shape[0] // 2
    return total[:half], total[half:].astype(bf16)


def add_low(total, got):
    return total + got.astype(f32)


def add_step(total, axis, bit):
    low = total.astype(bf16)
    return low.astype(f32) + swap(low, axis, bit).astype(f32)


def scatter_step(total, group):
    count = 2 ** len(group)
    rows = total.shape[0] // count
    out = total[:rows]
    for k in range(1, count):
        mask = sum(bit for i, bit in enumerate(group) if (k >> (len(group) - 1 - i)) & 1)
        out = add_low(out, swap(total[k * rows : (k + 1) * rows].astype(bf16), "row", mask))
    return out


def scatter_both(first, second, group):
    early, late = group
    quarter, half = first.shape[0] // 4, second.shape[0] // 2
    pieces = [first[k * quarter : (k + 1) * quarter] for k in range(4)]
    joint = swap(jnp.concatenate([pieces[1], second[half:]]).astype(bf16), "row", late)
    first = add_low(pieces[0], swap(pieces[2].astype(bf16), "row", early))
    first = add_low(first, swap(pieces[3].astype(bf16), "row", early | late))
    return add_low(first, joint[:quarter]), add_low(second[:half], joint[quarter:])


def tie(*values):
    return lax.optimization_barrier(values)


def shards(q, k, v, u, sharp, proj, taps):
    tile = v.shape[:2]
    width = v.shape[2]
    tokens = tile[0] * tile[1]
    head_size = width // sharp.shape[0]
    rows, cols = lax.axis_size("row"), lax.axis_size("col")
    flat = lambda x: x.reshape(tokens, width)
    here = jnp.stack([lax.axis_index("col"), lax.axis_index("row")]).astype(jnp.int32)
    q2, k2, v2, u2 = flat(q), flat(k), flat(v), flat(u)
    bits = row_bits()
    early = [("row", bits[0]), ("col", 1)] + [("row", bit) for bit in bits[1:]]
    late = [("col", 1)] + [("row", bit) for bit in bits]
    piece_rows = width // (rows * cols)

    mine, other = gram_call(q2, k2, head_size)
    to_twin, to_next = edges_call(here, v, u)
    total = add_low(mine, swap(other, "col", 1))
    start = jnp.where(lax.axis_index("col") == 0, v.shape[1] - RIM, 0)
    edge = lambda x: lax.dynamic_slice_in_dim(x, start, RIM, axis=1)
    pairs_next = [(j, j + 1) for j in range(1, rows - 1, 2)]
    pairs_next = pairs_next + [(b, a) for a, b in pairs_next]
    side = swap(jnp.concatenate([edge(v), edge(u)]), "col", 1)
    for i, bit in enumerate(bits[:1] + bits[2:] + bits[1:2]):
        total = total + swap(total, "row", bit)
        if i == 2:
            from_twin = swap(to_twin, "row", 1)
            total, from_twin = tie(total, from_twin)
        if i == 2:
            from_next = lax.ppermute(to_next, "row", pairs_next)
            total, from_next = tie(total, from_next)
    corner = swap(
        edge(jnp.concatenate([from_twin[:2], from_next[:2], from_twin[2:], from_next[2:]])), "col", 1
    )
    around = tuple(x.reshape(-1, width) for x in (side, from_twin, from_next, corner))
    energy_own, energy_far = total, swap(total, "col", 1)

    (merged_front, attn, gram, scale, block, mixed_all, front_target, front_taps, mine, other, carry) = front_call(
        here, sharp, energy_own, energy_far, v2, u2, around, proj, taps, tile, head_size, piece_rows, cols, early
    )
    halves = [swap(x, "row", bits[0]) for x in jnp.split(other, [other.shape[0] * 3 // 8])]
    first = halves[:1]
    front_mine = mine
    merged_back, target, grad, mine, other = back_call(
        here, u2, v2, around, mixed_all, proj, taps, front_target, front_taps, carry, tile, head_size
    )

    mine, other, *first = tie(mine, other, *first)
    after = swap(other, "col", 1)
    total = add_low(mine, after)
    turns = bits[1:2] + bits[:1] + bits[2:]
    back_mine, back_other = projector_call(here, mixed_all, target, after, piece_rows, cols, late)
    front_sum = add_low(front_mine, jnp.concatenate([*first, *halves[1:]]))
    back_sum = add_low(back_mine, swap(back_other, "col", 1))
    total = add_step(total, "row", turns[0])
    total, back_sum = tie(total, back_sum)
    total = add_step(total, "row", turns[1])
    total, front_sum = tie(total, front_sum)
    for bit in turns[2:]:
        total = add_step(total, "row", bit)
    front_sum, leaves = halve(front_sum)
    front_sum = add_low(front_sum, swap(leaves, "col", 1))
    back_sum = scatter_step(back_sum, bits[:2])
    front_sum = scatter_step(front_sum, bits[1:2])
    total, back_sum = tie(total, back_sum)
    for bit in bits[2:-1]:
        front_sum, back_sum = scatter_step(front_sum, [bit]), scatter_step(back_sum, [bit])
    far = swap(total, "col", 1)
    kept, leaves = zip(halve(front_sum), halve(back_sum))
    got = swap(jnp.concatenate(leaves), "row", bits[-1])
    dq, dk, heat, tap_sums = final_call(
        here, sharp, total, far, energy_own, energy_far, attn, gram, scale, q2, k2, head_size
    )
    content, merged = content_call(grad, block, merged_front, merged_back, tap_sums)
    content, *kept = tie(content, *kept)
    front_sum, back_sum = (add_low(x, y) for x, y in zip(kept, jnp.split(got, 2)))
    projector = jnp.concatenate([front_sum, back_sum], axis=1)
    full = lambda x: x.reshape(tile + (width,))
    return full(merged), full(dq), full(dk), full(content), heat, tap_sums, projector


def solution(mesh):
    field = P(("scene", "row"), "col", None)
    return jax.shard_map(
        shards,
        mesh=mesh,
        in_specs=(field, field, field, field, P(), P(), P()),
        out_specs=(
            field,
            field,
            field,
            field,
            P("scene"),
            P("scene", None),
            P(("scene", "row", "col"), None),
        ),
        check_vma=False,
    )
```
